256 devices in a mesh: gx: 16 (over z, y_hi), gy: 16 (over y_lo, x, core).
Axes of the slice: x: 4, y: 4 (y_hi: 2, y_lo: 2; y = y_hi * 2 + y_lo), z: 8, core: 2. Of those that a mesh axis runs over, the one named last changes fastest.
Arguments:
- populations: float32 [19, 256, 256, 256], P(None, 'gx', 'gy'), may hold values from 0.022 to 0.4, as said below
- concentrations: float32 [2, 256, 256, 256], P(None, 'gx', 'gy'), may hold values from 0.5 to 1.5
- potential: float32 [256, 256, 256], P('gx', 'gy'), may hold values from -4 to 4
- mobility: float32 [256, 256, 256], P('gx', 'gy'), may hold values from 0.5 to 2
- solid: int32 [256, 256, 256], P('gx', 'gy'), may hold values from 0 to 1, as said below
- wall_class: int32 [256, 256, 256], P('gx', 'gy'), may hold values from 0 to 3
- wall_charge: float32 [4], replicated, may hold values from -2 to -0.25
Outputs:
- populations_out: float32 [19, 256, 256, 256], P(None, 'gx', 'gy')
- concentrations_out: float32 [2, 256, 256, 256], P(None, 'gx', 'gy')
- potential_out: float32 [256, 256, 256], P('gx', 'gy')
The draws below stay inside these ranges and needn't reach their ends.
Inputs may be any that keep to these rules, and one draw needn't show every extreme that they name: populations[i] lies within 0.8 w_i to 1.2 w_i. 1 marks a solid node.
All inputs are finite; a program needn't handle non-finite values.
Results may differ from the reference program's by a relative error of at most 0.00002.
Values sent between devices are 32-bit elements; how exact they have to be, the bound alone decides.
No kernel may reach another device: no remote copies, remote signals or barrier semaphores. Data moves between devices by JAX's collectives and lax.ppermute only.
A program may use at most 128 MiB of HBM per device.

```python
import math
import jax
import jax.numpy as jnp
from jax import lax

CX = 16
CY = 16
NZ = 256
SWEEPS = 3
CLASSES = 4
NX = 256
NY = 256


draw_weights = [1.0 / 3.0] + [1.0 / 18.0] * 6 + [1.0 / 36.0] * 12


def draw_populations(key, part):
    base = jnp.array(draw_weights, jnp.float32).reshape(19, 1, 1, 1)
    noise = jax.random.uniform(key, (19, NX, NY, NZ), jnp.float32, -1.0, 1.0)
    return base * (1.0 + 0.2 * noise)


def draw_solid(key, part):
    key_x, key_y, key_narrow, key_wide = jax.random.split(jax.random.fold_in(key, 17), 4)
    blocks_x = NX // CX
    blocks_y = NY // CY
    reach = max(2, min(CX, CY) // 4 + 1)
    centre_x = jax.random.randint(key_x, (blocks_x, blocks_y), 0, CX)
    centre_y = jax.random.randint(key_y, (blocks_x, blocks_y), 0, CY)
    narrow_radius = jax.random.randint(key_narrow, (blocks_x, blocks_y), 1, reach)
    wide = narrow_radius + jax.random.randint(key_wide, (blocks_x, blocks_y), 1, reach)
    coord_x = lax.broadcasted_iota(jnp.int32, (NX, NY), 0)
    coord_y = lax.broadcasted_iota(jnp.int32, (NX, NY), 1)
    own_x = coord_x // CX
    own_y = coord_y // CY
    lowest = NZ // 4
    highest = NZ - NZ // 4
    thickness = highest - lowest
    height = jnp.arange(NZ, dtype=jnp.int32)
    climb = jnp.clip(height - lowest, 0, thickness - 1)
    inside = jnp.zeros((NX, NY, NZ), dtype=bool)
    for step_x in (-1, 0, 1):
        for step_y in (-1, 0, 1):
            pore_x = (own_x + step_x) % blocks_x
            pore_y = (own_y + step_y) % blocks_y
            offset_x = coord_x - (own_x + step_x) * CX - centre_x[pore_x, pore_y]
            offset_y = coord_y - (own_y + step_y) * CY - centre_y[pore_x, pore_y]
            distance = offset_x * offset_x + offset_y * offset_y
            bottom = narrow_radius[pore_x, pore_y]
            spread = wide[pore_x, pore_y] - bottom
            radius = bottom[:, :, None] + spread[:, :, None] * climb[None, None, :] // thickness
            inside = inside | (distance[:, :, None] <= radius * radius)
    membrane = (height >= lowest) & (height < highest)
    return (membrane[None, None, :] & jnp.logical_not(inside)).astype(jnp.int32)


def plant(values, stream_key, low, high):
    dims = values.shape
    place = [jax.random.randint(jax.random.fold_in(stream_key, axis), (), 0, dims[axis]) for axis in range(len(dims))]
    values = values.at[tuple(place)].set(low)
    longest = dims.index(max(dims))
    place[longest] = (place[longest] + 1) % dims[longest]
    return values.at[tuple(place)].set(high)


def block_levels(key, shape, cuts, low, top_value):
    def one(axis_at, shards_of):
        draws = jax.random.uniform(jax.random.fold_in(jax.random.fold_in(key, 6), axis_at), (shards_of,), jnp.float32, low / len(cuts), top_value / len(cuts))
        return jnp.repeat(jnp.exp(draws), shape[axis_at] // shards_of).reshape((-1,) + (1,) * (len(shape) - axis_at - 1))

    factor_of = one(*cuts[0])
    for cut in cuts[1:]:
        factor_of = factor_of * one(*cut)
    return factor_of


def gaussian(key, dims, scale, most, cuts=(), kind=jnp.bfloat16):
    gain = block_levels(key, dims, cuts, -0.22, 0.18) if cuts else 1.0
    values = jax.random.normal(key, dims, jnp.float32) * scale * gain
    return jnp.minimum(jnp.maximum(values, -most), most).astype(kind)


def setup_inputs(seed: int = 0) -> dict:
    arg_keys = jax.random.split(jax.random.key(seed), 8)
    return {
        "populations": draw_populations(jax.random.fold_in(arg_keys[7], 71), 0),
        "concentrations": jnp.clip(0.5 + 1.0 * jax.random.uniform(arg_keys[1], (2, NX, NY, NZ), jnp.float32) ** block_levels(arg_keys[1], (2, NX, NY, NZ), ((1, 16), (2, 16)), -0.2, 0.2), 0.5, 1.5),
        "potential": gaussian(arg_keys[2], (NX, NY, NZ), 1.0, 4.0, ((0, 16), (1, 16)), jnp.float32),
        "mobility": jnp.clip(jnp.exp(math.log(2.0) - 1.3862944 * jax.random.uniform(arg_keys[3], (NX, NY, NZ), jnp.float32) ** block_levels(arg_keys[3], (NX, NY, NZ), ((0, 16), (1, 16)), -0.2, 0.2)), 0.5, 2.0),
        "solid": draw_solid(jax.random.fold_in(arg_keys[7], 71), 0),
        "wall_class": plant(jax.random.randint(arg_keys[5], (NX, NY, NZ), 0, CLASSES), jax.random.fold_in(arg_keys[5], 1), 0, CLASSES - 1).astype(jnp.int32),
        "wall_charge": jnp.clip(jax.random.uniform(arg_keys[6], (CLASSES,), jnp.float32, -2.0, -0.25), -2.0, -0.25),
    }


lattice_dirs = [(0, 0, 0), (1, 0, 0), (-1, 0, 0), (0, 1, 0), (0, -1, 0), (0, 0, 1), (0, 0, -1), (1, 1, 0), (-1, -1, 0), (1, -1, 0), (-1, 1, 0), (1, 0, 1), (-1, 0, -1), (1, 0, -1), (-1, 0, 1), (0, 1, 1), (0, -1, -1), (0, 1, -1), (0, -1, 1)]
opposite = [0, 2, 1, 4, 3, 6, 5, 8, 7, 10, 9, 12, 11, 14, 13, 16, 15, 18, 17]
lattice_weights = [1.0 / 3.0] + [1.0 / 18.0] * 6 + [1.0 / 36.0] * 12
relax_time = 0.9
coupling = 0.002
diffusion_rates = (0.06, 0.08)
valences = (1.0, -1.0)
overrelax_factor = 1.6

def first_moments(populations):
    result = []
    for axis_number in range(3):
        total = jnp.zeros_like(populations[0])
        for slot, direction in enumerate(lattice_dirs):
            if direction[axis_number] != 0:
                total = total + direction[axis_number] * populations[slot]
        result.append(total)
    return result

def equilibrium(density, shifted):
    square = shifted[0] * shifted[0] + shifted[1] * shifted[1] + shifted[2] * shifted[2]
    layers = []
    for direction, weight in zip(lattice_dirs, lattice_weights):
        along = jnp.zeros_like(density)
        for axis_number in range(3):
            if direction[axis_number] != 0:
                along = along + direction[axis_number] * shifted[axis_number]
        layers.append(weight * density * (1.0 + 3.0 * along + 4.5 * along * along - 1.5 * square))
    return jnp.stack(layers)

def collide(populations, force, solid):
    density = lax.optimization_barrier(jnp.sum(populations, axis=0))
    moment = first_moments(populations)
    shifted = [moment[axis_number] / density + relax_time * force[axis_number] / density for axis_number in range(3)]
    balanced = equilibrium(density, shifted)
    relaxed = populations - (populations - balanced) / relax_time
    reversed_set = jnp.stack([populations[slot] for slot in opposite])
    return jnp.where(solid[None] == 0, relaxed, reversed_set)

def drift_velocity(read, force, fluid):
    density = lax.optimization_barrier(jnp.sum(read, axis=0))
    moment = first_moments(read)
    return [fluid * (moment[axis_number] + 0.5 * force[axis_number]) / density for axis_number in range(3)]

def relax_half(node_values, source_term, color, parity):
    neighbour_total = jnp.roll(node_values, -1, 0) + jnp.roll(node_values, 1, 0)
    neighbour_total = neighbour_total + jnp.roll(node_values, -1, 1) + jnp.roll(node_values, 1, 1)
    neighbour_total = neighbour_total + jnp.roll(node_values, -1, 2) + jnp.roll(node_values, 1, 2)
    updated_potential = (1.0 - overrelax_factor) * node_values + overrelax_factor * (neighbour_total + source_term) / 6.0
    return jnp.where(parity == color, updated_potential, node_values)

def reference(populations, concentrations, potential, mobility, solid, wall_class, wall_charge):
    fluid = (solid == 0).astype(jnp.float32)
    conductance = fluid * jnp.sqrt(mobility)
    ion_charge = valences[0] * concentrations[0] + valences[1] * concentrations[1]
    force = []
    for axis_number in range(3):
        upper = jnp.roll(potential, -1, axis_number)
        lower = jnp.roll(potential, 1, axis_number)
        force.append(coupling * fluid * ion_charge * (-(upper - lower) * 0.5))
    post = collide(populations, force, solid)
    read = jnp.stack([jnp.roll(post[slot], direction, axis=(0, 1, 2)) for slot, direction in enumerate(lattice_dirs)])
    drift = drift_velocity(read, force, fluid)
    fields = jnp.concatenate([concentrations, conductance[None], potential[None]], axis=0)
    totals = [jnp.zeros_like(potential), jnp.zeros_like(potential)]
    for axis_number in range(3):
        for sign in (1, -1):
            other = jnp.roll(fields, -sign, axis_number + 1)
            moving = jnp.roll(drift[axis_number], -sign, axis_number)
            link = conductance * other[2]
            carried_over = 0.5 * sign * (drift[axis_number] + moving)
            drop = potential - other[3]
            for species in range(2):
                mean = 0.5 * (concentrations[species] + other[species])
                flux = link * (diffusion_rates[species] * (concentrations[species] - other[species] + valences[species] * mean * drop) + mean * carried_over)
                totals[species] = totals[species] + flux
    concentrations_out = jnp.stack([concentrations[species] - totals[species] for species in range(2)])
    wall = wall_charge[wall_class]
    source_term = fluid * (valences[0] * concentrations_out[0] + valences[1] * concentrations_out[1]) + (1.0 - fluid) * wall
    shape = potential.shape
    parity = (lax.broadcasted_iota(jnp.int32, shape, 0) + lax.broadcasted_iota(jnp.int32, shape, 1) + lax.broadcasted_iota(jnp.int32, shape, 2)) % 2
    current = potential
    for sweep in range(SWEEPS):
        for color in (0, 1):
            current = relax_half(current, source_term, color, parity)
    return (read, concentrations_out, current)
```

```python
import jax
import jax.numpy as jnp
from jax import lax
from jax.experimental import pallas as pl
from jax.experimental.pallas import tpu as pltpu
from jax.sharding import PartitionSpec as P

C = [(0, 0, 0), (1, 0, 0), (-1, 0, 0), (0, 1, 0), (0, -1, 0), (0, 0, 1), (0, 0, -1),
     (1, 1, 0), (-1, -1, 0), (1, -1, 0), (-1, 1, 0), (1, 0, 1), (-1, 0, -1), (1, 0, -1), (-1, 0, 1),
     (0, 1, 1), (0, -1, -1), (0, 1, -1), (0, -1, 1)]
W = [1.0 / 3.0] + [1.0 / 18.0] * 6 + [1.0 / 36.0] * 12
XPOS = [i for i in range(19) if C[i][0] == 1]
XNEG = [i for i in range(19) if C[i][0] == -1]
YPOS = [i for i in range(19) if C[i][1] == 1]
YNEG = [i for i in range(19) if C[i][1] == -1]
RATES = (0.06, 0.08)
VAL = (1.0, -1.0)
N = 16
Z = 256
XB = 4
RING = 6
OFF = 8
F32 = jnp.float32
VM = pltpu.VMEM


def sds(*shape):
    return jax.ShapeDtypeStruct(shape, F32)


def params(mib):
    return pltpu.CompilerParams(vmem_limit_bytes=mib * 1024 * 1024)


def rows():
    return lax.broadcasted_iota(jnp.int32, (N, Z), 0)


def roll_y(v, s):
    return pltpu.roll(v, s % v.shape[0], 0)


def roll_z(v, s):
    return pltpu.roll(v, s % v.shape[1], 1)


def row_of(v, y):
    return v[y:y + 1, :]


def spread(row):
    return jnp.broadcast_to(row, (N, Z))


def add_groups(groups, x_dir, parts):
    got = groups[x_dir]
    for k in range(3):
        if parts[k] is not None:
            got[k] = parts[k] if got[k] is None else got[k] + parts[k]


def collide_kernel(pops, conc, mob, solid, pot, pxlo, pxhi, pylo, pyhi,
                   out, mom, cond, yf_hi, yf_lo, xf_hi, xf_lo, ay_hi, ay_lo, ax_hi, ax_lo,
                   buf, sems):
    j = pl.program_id(0)
    last = N // XB - 1
    row = rows()
    zero = jnp.zeros((N, Z), F32)

    @pl.when(j == 0)
    def _():
        for m in range(4):
            mom[m, 0] = zero
            mom[m, 1] = zero
        for k in range(RING):
            ax_hi[k] = pot[N - 1 - k]
            ax_lo[k] = pot[k]

    for k in range(XB):
        xg = j * XB + k
        centre = pot[xg]
        c0, c1 = conc[0, k], conc[1, k]
        is_fluid = solid[k] == 0
        fluid = jnp.where(is_fluid, 1.0, 0.0).astype(F32)
        cnd = fluid * jnp.sqrt(mob[k])
        cond[k] = cnd
        if k == 0:
            below = jnp.where(j == 0, pxlo[...], pot[jnp.maximum(xg - 1, 0)])
        else:
            below = pot[xg - 1]
        if k == XB - 1:
            above = jnp.where(j == last, pxhi[...], pot[jnp.minimum(xg + 1, N - 1)])
        else:
            above = pot[xg + 1]
        here = pl.ds(xg, 1)
        y_up = jnp.where(row == N - 1, spread(pyhi[here, :]), roll_y(centre, -1))
        y_dn = jnp.where(row == 0, spread(pylo[here, :]), roll_y(centre, 1))
        pull = fluid * (c0 - c1) * (-0.001)
        fx = pull * (above - below)
        fy = pull * (y_up - y_dn)
        fz = pull * (roll_z(centre, -1) - roll_z(centre, 1))
        p = [pops[i, k] for i in range(19)]
        density = p[0]
        for i in range(1, 19):
            density = density + p[i]
        moment = []
        for a in range(3):
            total = None
            for i in range(19):
                if C[i][a] == 1:
                    term = p[i] - p[i + 1 if i % 2 else i - 1]
                    total = term if total is None else total + term
            moment.append(total)
        inv = 1.0 / density
        ux = (moment[0] + 0.9 * fx) * inv
        uy = (moment[1] + 0.9 * fy) * inv
        uz = (moment[2] + 0.9 * fz) * inv
        base = 1.0 - 1.5 * (ux * ux + uy * uy + uz * uz)
        scaled = density * (10.0 / 9.0)
        groups = {-1: [None, None, None], 0: [None, None, None], 1: [None, None, None]}
        u = (ux, uy, uz)

        def place(i, v):
            cx, cy, cz = C[i]
            if cz:
                v = roll_z(v, cz)
            if cy == 1:
                v = roll_y(v, 1)
                yf_hi[YPOS.index(i), here, :] = row_of(v, 0)
                v = jnp.where(row == 0, 0.0, v)
            elif cy == -1:
                v = roll_y(v, -1)
                yf_lo[YNEG.index(i), here, :] = row_of(v, N - 1)
                v = jnp.where(row == N - 1, 0.0, v)
            buf[i, xg + 1 + cx] = v
            add_groups(groups, cx, (v, v * float(cy) if cy else None, v * float(cz) if cz else None))

        rest = jnp.where(is_fluid, (W[0] * scaled) * base - p[0] * (1.0 / 9.0), p[0])
        place(0, rest)
        for i in range(1, 19, 2):
            along = None
            for a in range(3):
                if C[i][a]:
                    term = u[a] if C[i][a] == 1 else -u[a]
                    along = term if along is None else along + term
            even = base + 4.5 * along * along
            odd = 3.0 * along
            ws = W[i] * scaled
            fwd = ws * (even + odd) - p[i] * (1.0 / 9.0)
            bwd = ws * (even - odd) - p[i + 1] * (1.0 / 9.0)
            place(i, jnp.where(is_fluid, fwd, p[i + 1]))
            place(i + 1, jnp.where(is_fluid, bwd, p[i]))
        g = groups[0]
        mom[0, xg + 1] += g[0]
        mom[1, xg + 1] += 0.5 * fx
        mom[2, xg + 1] += g[1] + 0.5 * fy
        mom[3, xg + 1] += g[2] + 0.5 * fz
        g = groups[1]
        mom[0, xg + 2] = g[0]
        mom[1, xg + 2] = g[0]
        mom[2, xg + 2] = g[1]
        mom[3, xg + 2] = g[2]
        g = groups[-1]
        mom[0, xg] += g[0]
        mom[1, xg] -= g[0]
        mom[2, xg] += g[1]
        mom[3, xg] += g[2]
        for r in range(RING):
            ay_hi[r, here, :] = row_of(centre, N - 1 - r)
            ay_lo[r, here, :] = row_of(centre, r)
        for q, v in enumerate((c0, c1, cnd)):
            ay_hi[RING + q, here, :] = row_of(v, N - 1)
            ay_lo[RING + q, here, :] = row_of(v, 0)
        if k == 0:
            @pl.when(j == 0)
            def _(vals=(c0, c1, cnd)):
                for q in range(3):
                    ax_lo[RING + q] = vals[q]
        if k == XB - 1:
            @pl.when(j == last)
            def _(vals=(c0, c1, cnd)):
                for q in range(3):
                    ax_hi[RING + q] = vals[q]

    copies = []
    for s in range(last + 1):
        lo = max(s * XB - 1, 0)
        hi = N if s == last else s * XB + XB - 1
        copies.append(pltpu.make_async_copy(buf.at[:, lo + 1:hi + 1], out.at[:, lo:hi], sems.at[s]))
    for s in range(last + 1):
        @pl.when(j == s)
        def _(s=s):
            copies[s].start()

    @pl.when(j == last)
    def _():
        for q, i in enumerate(XPOS):
            xf_hi[q] = buf[i, N + 1]
        for q, i in enumerate(XNEG):
            xf_lo[q] = buf[i, 0]
        for s in range(last + 1):
            copies[s].wait()


def collide(pops, conc, mob, solid, pot, pxlo, pxhi, pylo, pyhi):
    def whole(*shape):
        return pl.BlockSpec(shape, lambda j: (0,) * len(shape))

    plane = pl.BlockSpec((XB, N, Z), lambda j: (j, 0, 0))
    face = whole(N, Z)
    return pl.pallas_call(
        collide_kernel,
        grid=(N // XB,),
        in_specs=[
            pl.BlockSpec((19, XB, N, Z), lambda j: (0, j, 0, 0)),
            pl.BlockSpec((2, XB, N, Z), lambda j: (0, j, 0, 0)),
            plane, plane, whole(N, N, Z), face, face, face, face,
        ],
        out_specs=[pl.BlockSpec(memory_space=pl.ANY), whole(4, N + 2, N, Z), plane]
        + [whole(5, N, Z)] * 4 + [whole(9, N, Z)] * 4,
        out_shape=[sds(19, N, N, Z), sds(4, N + 2, N, Z), sds(N, N, Z)]
        + [sds(5, N, Z)] * 4 + [sds(9, N, Z)] * 4,
        scratch_shapes=[VM((19, N + 2, N, Z), F32), pltpu.SemaphoreType.DMA((N // XB,))],
        compiler_params=params(32),
        name="collide",
    )(pops, conc, mob, solid, pot, pxlo, pxhi, pylo, pyhi)


def corner_kernel(xf_hi, xf_lo, yh_lo, yh_hi, o_hi, o_lo):
    row = rows()
    o_hi[...] = xf_hi[...]
    o_lo[...] = xf_lo[...]

    def fix(dst, slots, slot, halo, halo_slots, x, y):
        q = slots.index(slot)
        line = halo[halo_slots.index(slot), x:x + 1, :]
        dst[q] = jnp.where(row == y, spread(line), dst[q])

    fix(o_hi, XPOS, 7, yh_lo, YPOS, N - 1, 0)
    fix(o_hi, XPOS, 9, yh_hi, YNEG, N - 1, N - 1)
    fix(o_lo, XNEG, 8, yh_hi, YNEG, 0, N - 1)
    fix(o_lo, XNEG, 10, yh_lo, YPOS, 0, 0)


def simple(kernel, outs, name, scratch=(), mib=16, smem=None, count=0):
    in_specs = [pl.BlockSpec(memory_space=pltpu.SMEM if i == smem else VM) for i in range(count)]
    return pl.pallas_call(
        kernel,
        in_specs=in_specs,
        out_specs=[pl.BlockSpec(memory_space=VM) for _ in outs],
        out_shape=outs,
        scratch_shapes=list(scratch),
        compiler_params=params(mib),
        name=name,
    )


def ring_rows(depth, total):
    listed = []
    at = depth
    for a in range(1, total):
        for side in (0, 1):
            for b in range(1, total - a + 1):
                listed.append((at, a, side, b))
                at += 1
    return listed


POT_ROWS = ring_rows((RING + 3) * N, RING)
SRC_ROWS = ring_rows((RING - 1) * N, RING - 1)
POT_LEN = 176
SRC_LEN = 104


def pack_pot_kernel(ax_hi, ax_lo, ya_lo, ya_hi, o_hi, o_lo):
    for k in range(RING + 3):
        o_hi[k * N:(k + 1) * N, :] = ax_hi[k]
        o_lo[k * N:(k + 1) * N, :] = ax_lo[k]
    for at, a, side, b in POT_ROWS:
        halo = ya_hi if side else ya_lo
        o_hi[at:at + 1, :] = halo[b - 1, N - a:N - a + 1, :]
        o_lo[at:at + 1, :] = halo[b - 1, a - 1:a, :]
    end = POT_ROWS[-1][0] + 1
    o_hi[end:, :] = jnp.zeros((POT_LEN - end, Z), F32)
    o_lo[end:, :] = jnp.zeros((POT_LEN - end, Z), F32)


def pack_src_kernel(src, ys_lo, ys_hi, o_hi, o_lo):
    for k in range(RING - 1):
        o_hi[k * N:(k + 1) * N, :] = src[N - 1 - k]
        o_lo[k * N:(k + 1) * N, :] = src[k]
    for at, a, side, b in SRC_ROWS:
        halo = ys_hi if side else ys_lo
        o_hi[at:at + 1, :] = halo[b - 1, N - a:N - a + 1, :]
        o_lo[at:at + 1, :] = halo[b - 1, a - 1:a, :]
    end = SRC_ROWS[-1][0] + 1
    o_hi[end:, :] = jnp.zeros((SRC_LEN - end, Z), F32)
    o_lo[end:, :] = jnp.zeros((SRC_LEN - end, Z), F32)


def drift_kernel(mom, cond, yh_lo, yh_hi, xh_lo, xh_hi, drift, dx_lo, dx_hi, dy_lo, dy_hi, lines):
    row = rows()

    def up(v):
        return jnp.where(row == 0, 0.0, roll_y(v, 1))

    def down(v):
        return jnp.where(row == N - 1, 0.0, roll_y(v, -1))

    s3, s7, s10, s15, s17 = (yh_lo[q] for q in range(5))
    s7, s10 = up(s7), down(s10)
    total = s3 + s7 + s10 + s15 + s17
    lines[0] = total
    lines[1] = s7 - s10
    lines[2] = total
    lines[3] = s15 - s17
    s4, s8, s9, s16, s18 = (yh_hi[q] for q in range(5))
    s8, s9 = down(s8), up(s9)
    total = s4 + s8 + s9 + s16 + s18
    lines[4] = total
    lines[5] = s9 - s8
    lines[6] = -total
    lines[7] = s18 - s16

    def step(x, extra):
        here = pl.ds(x, 1)

        def full(m):
            v = mom[m, x + 1]
            if extra is not None:
                v = v + extra[m]
            v = v + jnp.where(row == 0, spread(lines[m, here, :]), 0.0)
            return v + jnp.where(row == N - 1, spread(lines[4 + m, here, :]), 0.0)

        scale = jnp.where(cond[x] > 0.0, 1.0 / full(0), 0.0)
        drift[0, x] = full(1) * scale
        v = full(2) * scale
        drift[1, x] = v
        drift[2, x] = full(3) * scale
        dy_lo[here, :] = row_of(v, 0)
        dy_hi[here, :] = row_of(v, N - 1)

    a, b = xh_lo, xh_hi
    total = a[0] + a[1] + a[2] + a[3] + a[4]
    step(0, (total, total, a[1] - a[2], a[3] - a[4]))
    total = b[0] + b[1] + b[2] + b[3] + b[4]
    step(N - 1, (total, -total, b[2] - b[1], b[4] - b[3]))

    def loop(x, carry):
        step(x, None)
        return carry

    lax.fori_loop(1, N - 1, loop, 0, unroll=2)
    dx_lo[...] = drift[0, 0]
    dx_hi[...] = drift[0, N - 1]


def flux(a, b):
    link = a[2] * b[2]
    carried = 0.5 * (a[4] + b[4])
    drop = a[3] - b[3]
    got = []
    for s in range(2):
        mean = 0.5 * (a[s] + b[s])
        got.append(link * (RATES[s] * ((a[s] - b[s]) + (VAL[s] * mean) * drop) + mean * carried))
    return got


def transport_kernel(charge, conc, cond, pot, drift, classes, ya_lo, ya_hi, xa_lo, xa_hi,
                     own_lo, dxh_lo, dxh_hi, dyh_lo, dyh_hi, own_dy_lo,
                     conc_out, src, sy_lo, sy_hi, low):
    row = rows()
    base = RING

    def x_face(ref, d):
        at = [ref[(base + q) * N:(base + q + 1) * N, :] for q in range(3)]
        return (at[0], at[1], at[2], ref[0:N, :], d[...])

    left = (ya_lo[base], ya_lo[base + 1], ya_lo[base + 2], ya_lo[0], dyh_lo[...])
    right = (own_lo[base], own_lo[base + 1], own_lo[base + 2], own_lo[0], own_dy_lo[...])
    first = flux(left, right)
    low[0] = first[0]
    low[1] = first[1]

    def fields(x, d):
        return (conc[0, x], conc[1, x], cond[x], pot[x], drift[d, x])

    def one(x, behind, ahead):
        here = pl.ds(x, 1)
        me = fields(x, 0)
        fx = flux(me, ahead)
        tot = [fx[s] - behind[s] for s in range(2)]
        mine = me[:4] + (drift[1, x],)
        halo = (ya_hi[base, here, :], ya_hi[base + 1, here, :], ya_hi[base + 2, here, :],
                ya_hi[0, here, :], dyh_hi[here, :])
        nxt = tuple(jnp.where(row == N - 1, spread(halo[q]), roll_y(mine[q], -1)) for q in range(5))
        fy = flux(mine, nxt)
        for s in range(2):
            before = jnp.where(row == 0, spread(low[s, here, :]), roll_y(fy[s], 1))
            tot[s] = tot[s] + (fy[s] - before)
        mine = me[:4] + (drift[2, x],)
        fz = flux(mine, tuple(roll_z(v, -1) for v in mine))
        for s in range(2):
            tot[s] = tot[s] + (fz[s] - roll_z(fz[s], 1))
        c0 = me[0] - tot[0]
        c1 = me[1] - tot[1]
        conc_out[0, x] = c0
        conc_out[1, x] = c1
        cls = classes[x]
        wall = jnp.zeros((N, Z), F32)
        for q in range(4):
            wall = wall + jnp.where(cls == q, charge[q], 0.0)
        s_val = jnp.where(me[2] > 0.0, c0 - c1, wall)
        src[x] = s_val
        for r in range(RING - 1):
            sy_lo[r, here, :] = row_of(s_val, r)
            sy_hi[r, here, :] = row_of(s_val, N - 1 - r)
        return tuple(fx)

    carry = tuple(flux(x_face(xa_lo, dxh_lo), fields(0, 0)))
    carry = lax.fori_loop(0, N - 1, lambda x, c: one(x, c, fields(x + 1, 0)), carry)
    one(N - 1, carry, x_face(xa_hi, dxh_hi))


def sweep_kernel(pot, src, ya_lo, ya_hi, xa_lo, xa_hi, ys_lo, ys_hi, xs_lo, xs_hi, out, phi, s):
    mid = slice(OFF, OFF + N)
    top = RING + N

    def fill(dst, centre, y_lo, y_hi, x_lo, x_hi, depth, listed):
        for x in range(N):
            dst[RING + x, mid] = centre[x]
            for r in range(depth):
                dst[RING + x, OFF - 1 - r:OFF - r, :] = y_lo[r, x:x + 1, :]
                dst[RING + x, OFF + N + r:OFF + N + r + 1, :] = y_hi[r, x:x + 1, :]
        for r in range(depth):
            dst[RING - 1 - r, mid] = x_lo[r * N:(r + 1) * N, :]
            dst[top + r, mid] = x_hi[r * N:(r + 1) * N, :]
        for at, a, side, b in listed:
            y = OFF + N + b - 1 if side else OFF - b
            dst[RING - a, y:y + 1, :] = x_lo[at:at + 1, :]
            dst[top + a - 1, y:y + 1, :] = x_hi[at:at + 1, :]

    fill(phi, pot, ya_lo, ya_hi, xa_lo, xa_hi, RING, POT_ROWS)
    fill(s, src, ys_lo, ys_hi, xs_lo, xs_hi, RING - 1, SRC_ROWS)
    shape = (N + 2 * OFF, Z)
    checker = (lax.broadcasted_iota(jnp.int32, shape, 0) + lax.broadcasted_iota(jnp.int32, shape, 1)) % 2
    even_mask = checker == 0

    for h in range(6):
        lo = h + 1

        def update(x, mask):
            c = phi[x]
            nb = phi[x - 1] + phi[x + 1] + roll_y(c, 1) + roll_y(c, -1) + roll_z(c, 1) + roll_z(c, -1)
            new = -0.6 * c + (1.6 / 6.0) * (nb + s[x])
            phi[x] = jnp.where(mask, new, c)

        first = even_mask if (lo + h) % 2 == 0 else jnp.logical_not(even_mask)
        second = jnp.logical_not(first)

        def pair(k, carry):
            x = lo + 2 * k
            update(x, first)
            update(x + 1, second)
            return carry

        lax.fori_loop(0, (N + 2 * RING - 2 * lo) // 2, pair, 0)
    out[...] = phi[RING:RING + N, mid, :]


def patch_kernel(given, yh_lo, yh_hi, xh_lo, xh_hi, out, lo_buf, hi_buf, sems):
    del given
    spans = {0: (0, N), 1: (1, N), -1: (0, N - 1)}
    ins, outs, planes = [], [], []
    for q in range(5):
        for which, (slots, buf) in enumerate(((YPOS, lo_buf), (YNEG, hi_buf))):
            i = slots[q]
            x0, x1 = spans[C[i][0]]
            rows8 = pl.ds(8 * which, 8)
            remote = out.at[i, x0:x1, rows8, :]
            local = buf.at[q, x0:x1]
            ins.append(pltpu.make_async_copy(remote, local, sems.at[0, 2 * q + which]))
            outs.append(pltpu.make_async_copy(local, remote, sems.at[1, 2 * q + which]))
        planes.append(pltpu.make_async_copy(xh_lo.at[q], out.at[XPOS[q], 0], sems.at[2, 2 * q]))
        planes.append(pltpu.make_async_copy(xh_hi.at[q], out.at[XNEG[q], N - 1], sems.at[2, 2 * q + 1]))
    for c in ins:
        c.start()
    for c in ins:
        c.wait()
    for c in planes:
        c.start()
    for q in range(5):
        for which, (slots, buf, halo, y) in enumerate(((YPOS, lo_buf, yh_lo, 0), (YNEG, hi_buf, yh_hi, 7))):
            cx = C[slots[q]][0]
            x0, x1 = spans[cx]
            for x in range(x0, x1):
                buf[q, x, y:y + 1, :] = halo[q, x - cx:x - cx + 1, :]
            outs[2 * q + which].start()
    for c in outs:
        c.wait()
    for c in planes:
        c.wait()


def patch(pop, yh_lo, yh_hi, xh_lo, xh_hi):
    any_spec = pl.BlockSpec(memory_space=pl.ANY)
    return pl.pallas_call(
        patch_kernel,
        in_specs=[any_spec] + [pl.BlockSpec(memory_space=VM)] * 4,
        out_specs=any_spec,
        out_shape=sds(19, N, N, Z),
        input_output_aliases={0: 0},
        scratch_shapes=[VM((5, N, 8, Z), F32), VM((5, N, 8, Z), F32), pltpu.SemaphoreType.DMA((3, 10))],
        compiler_params=params(16),
        cost_estimate=pl.CostEstimate(flops=100000, bytes_accessed=4000000, transcendentals=0),
        name="patch",
    )(pop, yh_lo, yh_hi, xh_lo, xh_hi)


def swap(axis, hi, lo):
    n = lax.axis_size(axis)
    up = [(i, (i + 1) % n) for i in range(n)]
    down = [(b, a) for a, b in up]
    return lax.ppermute(hi, axis, up), lax.ppermute(lo, axis, down)


def body(pops, conc, pot, mob, solid, classes, charge):
    pxlo, pxhi = swap("gx", pot[N - 1], pot[0])
    pylo, pyhi = swap("gy", pot[:, N - 1], pot[:, 0])
    (pop, mom, cond, yf_hi, yf_lo, xf_hi, xf_lo, ay_hi, ay_lo, ax_hi, ax_lo) = collide(
        pops, conc, mob, solid, pot, pxlo, pxhi, pylo, pyhi)
    yh_lo, yh_hi = swap("gy", yf_hi, yf_lo)
    ya_lo, ya_hi = swap("gy", ay_hi, ay_lo)
    xf_hi, xf_lo = simple(corner_kernel, [sds(5, N, Z)] * 2, "corner", count=4)(xf_hi, xf_lo, yh_lo, yh_hi)
    xh_lo, xh_hi = swap("gx", xf_hi, xf_lo)
    bx_hi, bx_lo = simple(pack_pot_kernel, [sds(POT_LEN, Z)] * 2, "pack_pot", count=4)(ax_hi, ax_lo, ya_lo, ya_hi)
    xa_lo, xa_hi = swap("gx", bx_hi, bx_lo)
    drift, dx_lo, dx_hi, dy_lo, dy_hi = simple(
        drift_kernel, [sds(3, N, N, Z)] + [sds(N, Z)] * 4, "drift", scratch=[VM((8, N, Z), F32)], count=6)(
        mom, cond, yh_lo, yh_hi, xh_lo, xh_hi)
    dxh_lo, dxh_hi = swap("gx", dx_hi, dx_lo)
    dyh_lo, dyh_hi = swap("gy", dy_hi, dy_lo)
    conc_out, src, sy_lo, sy_hi = simple(
        transport_kernel, [sds(2, N, N, Z), sds(N, N, Z), sds(RING - 1, N, Z), sds(RING - 1, N, Z)], "transport",
        scratch=[VM((2, N, Z), F32)], smem=0, count=16)(
        charge, conc, cond, pot, drift, classes, ya_lo, ya_hi, xa_lo, xa_hi,
        ay_lo, dxh_lo, dxh_hi, dyh_lo, dyh_hi, dy_lo)
    ys_lo, ys_hi = swap("gy", sy_hi, sy_lo)
    bs_hi, bs_lo = simple(pack_src_kernel, [sds(SRC_LEN, Z)] * 2, "pack_src", count=3)(src, ys_lo, ys_hi)
    xs_lo, xs_hi = swap("gx", bs_hi, bs_lo)
    ext = VM((N + 2 * RING, N + 2 * OFF, Z), F32)
    potential_out = simple(sweep_kernel, [sds(N, N, Z)], "sweep", scratch=[ext, ext], count=10)(
        pot, src, ya_lo, ya_hi, xa_lo, xa_hi, ys_lo, ys_hi, xs_lo, xs_hi)[0]
    pop = patch(pop, yh_lo, yh_hi, xh_lo, xh_hi)
    return (pop, conc_out, potential_out)


def solution(mesh):
    lattice = P(None, "gx", "gy", None)
    flat = P("gx", "gy", None)
    return jax.shard_map(
        body, mesh=mesh, in_specs=(lattice, lattice, flat, flat, flat, flat, P()),
        out_specs=(lattice, lattice, flat), check_vma=False)
```

```python
import jax
import jax.numpy as jnp
from jax import lax
from jax.experimental import pallas as pl
from jax.experimental.pallas import tpu as pltpu
from jax.sharding import PartitionSpec as P

C = [(0, 0, 0), (1, 0, 0), (-1, 0, 0), (0, 1, 0), (0, -1, 0), (0, 0, 1), (0, 0, -1),
     (1, 1, 0), (-1, -1, 0), (1, -1, 0), (-1, 1, 0), (1, 0, 1), (-1, 0, -1), (1, 0, -1), (-1, 0, 1),
     (0, 1, 1), (0, -1, -1), (0, 1, -1), (0, -1, 1)]
W = [1.0 / 3.0] + [1.0 / 18.0] * 6 + [1.0 / 36.0] * 12
XPOS = [i for i in range(19) if C[i][0] == 1]
XNEG = [i for i in range(19) if C[i][0] == -1]
YPOS = [i for i in range(19) if C[i][1] == 1]
YNEG = [i for i in range(19) if C[i][1] == -1]
RATES = (0.06, 0.08)
VAL = (1.0, -1.0)
N = 16
Z = 256
CHUNK = 4
RING = 6
OFF = 8
ROWS = 7 * N + 8
LINE = 7 * N
F32 = jnp.float32
VM = pltpu.VMEM


def sds(*shape):
    return jax.ShapeDtypeStruct(shape, F32)


def params(mib):
    return pltpu.CompilerParams(vmem_limit_bytes=mib * 1024 * 1024)


def rows():
    return lax.broadcasted_iota(jnp.int32, (N, Z), 0)


def roll_y(v, s):
    return pltpu.roll(v, s % v.shape[0], 0)


def roll_z(v, s):
    return pltpu.roll(v, s % v.shape[1], 1)


def row_of(v, y):
    return v[y:y + 1, :]


def spread(row):
    return jnp.broadcast_to(row, (N, Z))


def shift_up(v):
    return jnp.where(rows() == 0, 0.0, roll_y(v, 1))


def shift_down(v):
    return jnp.where(rows() == N - 1, 0.0, roll_y(v, -1))


def shift_by(v, c):
    return shift_up(v) if c == 1 else shift_down(v) if c == -1 else v


def call(kernel, outs, name, specs, scratch=(), mib=16, flops=0, out_specs=None, moved=0):
    return pl.pallas_call(
        kernel,
        in_specs=[pl.BlockSpec(memory_space={"v": VM, "h": pltpu.HBM, "s": pltpu.SMEM}[c]) for c in specs],
        out_specs=[pl.BlockSpec(memory_space={"v": VM, "h": pltpu.HBM}[c]) for c in out_specs or "v" * len(outs)],
        out_shape=outs,
        scratch_shapes=list(scratch),
        compiler_params=params(mib),
        cost_estimate=pl.CostEstimate(flops=flops, bytes_accessed=moved, transcendentals=0),
        name=name,
    )


def faces_kernel(pot_h, conc_h, mob_h, solid_h, gx_hi, gx_lo, gy_hi, gy_lo, pot, conc, cond, mob, solid, sems):
    pairs = ((pot_h, pot), (conc_h, conc), (mob_h, mob), (solid_h, solid))
    copies = [pltpu.make_async_copy(a, b, sems.at[q]) for q, (a, b) in enumerate(pairs)]
    for c in copies:
        c.start()
    for c in copies:
        c.wait()

    def step(x, carry):
        here = pl.ds(x, 1)
        cond[x] = jnp.where(solid[x] == 0, jnp.sqrt(mob[x]), 0.0)
        for r in range(RING):
            gy_hi[r, here, :] = pot[x, N - 1 - r:N - r, :]
            gy_lo[r, here, :] = pot[x, r:r + 1, :]
        for q, v in ((0, conc.at[0]), (1, conc.at[1]), (2, cond)):
            gy_hi[RING + q, here, :] = v[x, N - 1:N, :]
            gy_lo[RING + q, here, :] = v[x, 0:1, :]
        return carry

    lax.fori_loop(0, N, step, 0, unroll=2)
    for x, face in ((N - 1, gx_hi), (0, gx_lo)):
        face[0] = pot[x]
        face[1] = conc[0, x]
        face[2] = conc[1, x]
        face[3] = cond[x]


def post_of(p, fluid, q, slopes):
    pull = jnp.where(fluid, q * (-0.001), 0.0)
    force = [pull * d for d in slopes]
    density = p[0]
    for i in range(1, 19):
        density = density + p[i]
    inv = 1.0 / density
    u = []
    for a in range(3):
        total = 0.9 * force[a]
        for i in range(1, 19, 2):
            if C[i][a]:
                term = p[i] - p[i + 1]
                total = total + term if C[i][a] == 1 else total - term
        u.append(total * inv)
    base = 1.0 - 1.5 * (u[0] * u[0] + u[1] * u[1] + u[2] * u[2])
    scaled = density * (10.0 / 9.0)
    out = [jnp.where(fluid, (W[0] * scaled) * base - p[0] * (1.0 / 9.0), p[0])]
    for i in range(1, 19, 2):
        along = None
        for a in range(3):
            if C[i][a]:
                term = u[a] if C[i][a] == 1 else -u[a]
                along = term if along is None else along + term
        even = base + 4.5 * along * along
        odd = 3.0 * along
        ws = W[i] * scaled
        fwd = ws * (even + odd) - p[i] * (1.0 / 9.0)
        bwd = ws * (even - odd) - p[i + 1] * (1.0 / 9.0)
        out.append(jnp.where(fluid, fwd, p[i + 1]))
        out.append(jnp.where(fluid, bwd, p[i]))
    return out, force


def sums(values, keep):
    total = [None] * 4
    for cy in (0, 1, -1):
        part = [None] * 4
        for i, v in values:
            if C[i][1] != cy:
                continue
            for m, c in enumerate((1,) + C[i]):
                if c and m != 2:
                    w = v if c == 1 else -v
                    part[m] = w if part[m] is None else part[m] + w
        for m in (0, 1, 3):
            if part[m] is None:
                continue
            w = part[m] if keep[cy] is None else jnp.where(keep[cy], part[m], 0.0)
            total[m] = w if total[m] is None else total[m] + w
            if m == 0 and cy:
                w = w if cy == 1 else -w
                total[2] = w if total[2] is None else total[2] + w
    return total


def collide_kernel(pops, pot, conc, cond, buf, mom, px_lo, px_hi, pr_lo, pr_hi, held, sems, psems):
    chunks = [pltpu.make_async_copy(pops.at[:, pl.ds(CHUNK * s, CHUNK)], held.at[:, pl.ds(CHUNK * s, CHUNK)], sems.at[s])
              for s in range(N // CHUNK)]
    ends = [pltpu.make_async_copy(pops.at[:, 0], px_lo, psems.at[0]),
            pltpu.make_async_copy(pops.at[:, N - 1], px_hi, psems.at[1])]
    for c in chunks + ends:
        c.start()
    row = rows()
    zero = jnp.zeros((N, Z), F32)
    keep = {0: (row >= 1) & (row <= N - 2), 1: row >= 2, -1: row <= N - 3}
    for m in range(4):
        mom[m, 0] = zero
        mom[m, 1] = zero

    def step(x, carry):
        here = pl.ds(x, 1)
        p = [held[i, x] for i in range(19)]
        for i in range(19):
            pr_lo[i, here, :] = row_of(p[i], 0)
            pr_hi[i, here, :] = row_of(p[i], N - 1)
        centre = pot[x]
        slopes = (pot[x + 1] - pot[x - 1], roll_y(centre, -1) - roll_y(centre, 1), roll_z(centre, -1) - roll_z(centre, 1))
        post, force = post_of(p, cond[x] > 0.0, conc[0, x] - conc[1, x], slopes)
        moved = []
        for i in range(19):
            v = post[i]
            if C[i][2]:
                v = roll_z(v, C[i][2])
            if C[i][1]:
                v = roll_y(v, C[i][1])
            buf[i, x + C[i][0]] = v
            moved.append(v)
        g = sums([(i, moved[i]) for i in range(19) if C[i][0] == 0], keep)
        mom[0, x] += g[0]
        for m in (1, 2, 3):
            w = jnp.where(keep[0], 0.5 * force[m - 1], 0.0)
            mom[m, x] += w if g[m] is None else g[m] + w
        g = sums([(i, moved[i]) for i in XPOS], keep)
        for m in range(4):
            mom[m, x + 1] = g[m]
        g = sums([(i, moved[i]) for i in XNEG], keep)
        for m in range(4):
            mom[m, x - 1] += g[m]
        return carry

    for s in range(N // CHUNK):
        chunks[s].wait()
        lax.fori_loop(max(CHUNK * s, 1), min(CHUNK * s + CHUNK, N - 1), step, 0)
    for c in ends:
        c.wait()


def edge_kernel(px_lo, px_hi, pr_lo, pr_hi, gx_lo, gx_hi, gy_lo, gy_hi, fx_lo, fx_hi, fy_lo, fy_hi, pot, mom0,
                mom, ex_lo, ex_hi, ey_lo, ey_hi, yb_lo, yb_hi):
    row = rows()
    inner = (row >= 1) & (row <= N - 2)
    keep = {0: None, 1: row >= 1, -1: row <= N - 2}
    lines = {}
    for pr, gy, fy, ey, low in ((pr_lo, gy_lo, fy_lo, ey_lo, True), (pr_hi, gy_hi, fy_hi, ey_hi, False)):
        centre = gy[0]
        y_slope = gy[1] - fy[0] if low else fy[0] - gy[1]
        slopes = (roll_y(centre, -1) - roll_y(centre, 1), y_slope, roll_z(centre, -1) - roll_z(centre, 1))
        post, force = post_of([pr[i] for i in range(19)], gy[RING + 2] > 0.0, gy[RING] - gy[RING + 1], slopes)
        for i in range(19):
            v = roll_z(post[i], C[i][2]) if C[i][2] else post[i]
            v = jnp.where(inner, v, 0.0)
            ey[i] = v
            if low and C[i][1] == -1:
                q = YNEG.index(i)
                yb_lo[q * N:(q + 1) * N, :] = v
            if not low and C[i][1] == 1:
                q = YPOS.index(i)
                yb_hi[q * N:(q + 1) * N, :] = v
            post[i] = shift_by(v, C[i][0])
        for cy in (0, 1 if low else -1):
            y = (0 if low else N - 1) + cy
            total = [None] * 4
            for i in range(19):
                if C[i][1] == cy:
                    for m, c in enumerate((1,) + C[i]):
                        if c:
                            w = post[i] if c == 1 else -post[i]
                            total[m] = w if total[m] is None else total[m] + w
            if cy == 0:
                for a in range(3):
                    w = jnp.where(inner, 0.5 * force[a], 0.0)
                    total[a + 1] = w if total[a + 1] is None else total[a + 1] + w
            lines[y] = total
    for x in range(N):
        for m in range(4):
            v = mom0[m, x]
            for y in (0, 1, N - 2, N - 1):
                v = v + jnp.where(row == y, spread(row_of(lines[y][m], x)), 0.0)
            mom[m, x] = v
    for px, gx, fx, ex, low in ((px_lo, gx_lo, fx_lo, ex_lo, True), (px_hi, gx_hi, fx_hi, ex_hi, False)):
        at = 0 if low else N - 1
        centre = gx[0]
        x_slope = pot[1] - fx[0] if low else fx[0] - pot[N - 2]
        y_up = jnp.where(row == N - 1, spread(fy_hi[0, at:at + 1, :]), roll_y(centre, -1))
        y_dn = jnp.where(row == 0, spread(fy_lo[0, at:at + 1, :]), roll_y(centre, 1))
        slopes = (x_slope, y_up - y_dn, roll_z(centre, -1) - roll_z(centre, 1))
        post, force = post_of([px[i] for i in range(19)], gx[3] > 0.0, gx[1] - gx[2], slopes)
        for i in range(19):
            v = roll_z(post[i], C[i][2]) if C[i][2] else post[i]
            if C[i][1] == 1:
                v = roll_y(v, 1)
                at_row = YPOS.index(i) * N + at
                yb_hi[at_row:at_row + 1, :] = row_of(v, 0)
                v = jnp.where(row == 0, 0.0, v)
            elif C[i][1] == -1:
                v = roll_y(v, -1)
                at_row = YNEG.index(i) * N + at
                yb_lo[at_row:at_row + 1, :] = row_of(v, N - 1)
                v = jnp.where(row == N - 1, 0.0, v)
            ex[i] = v
            post[i] = v
        none = {0: None, 1: None, -1: None}
        g = sums([(i, post[i]) for i in range(19) if C[i][0] == 0], none)
        mom[0, at] += g[0]
        for m in (1, 2, 3):
            w = 0.5 * force[m - 1]
            mom[m, at] += w if g[m] is None else g[m] + w
        g = sums([(i, post[i]) for i in (XPOS if low else XNEG)], none)
        for m in range(4):
            mom[m, 1 if low else N - 2] += g[m]
        g = sums([(i, post[i]) for i in (XNEG if low else XPOS)], none)
        k = LINE + (2 if low else 0)
        yb_hi[k:k + 1, :] = row_of(g[0], N - 1)
        yb_hi[k + 1:k + 2, :] = row_of(g[2], N - 1)
        yb_lo[k:k + 1, :] = row_of(g[0], 0)
        yb_lo[k + 1:k + 2, :] = row_of(g[2], 0)
    for x in range(N):
        for q, m in ((5, 0), (6, 2)):
            yb_lo[q * N + x:q * N + x + 1, :] = mom[m, x, 0:1, :]
            yb_hi[q * N + x:q * N + x + 1, :] = mom[m, x, N - 1:N, :]
    yb_lo[LINE + 4:, :] = jnp.zeros((4, Z), F32)
    yb_hi[LINE + 4:, :] = jnp.zeros((4, Z), F32)


def plane(ref, q):
    return ref[q * N:(q + 1) * N, :]


def line(ref, q, x):
    return ref[q * N + x:q * N + x + 1, :]


def y_terms(lo, hi):
    s3, s7, s10, s15, s17 = (plane(lo, q) for q in range(5))
    s7, s10 = shift_up(s7), shift_down(s10)
    total = s3 + s7 + s10 + s15 + s17
    below = (total, s7 - s10, total, s15 - s17)
    s4, s8, s9, s16, s18 = (plane(hi, q) for q in range(5))
    s8, s9 = shift_down(s8), shift_up(s9)
    total = s4 + s8 + s9 + s16 + s18
    return below, (total, s9 - s8, -total, s18 - s16)


def corner_kernel(ex_lo, ex_hi, yh_lo, yh_hi, yb_lo, yb_hi, mom, xb_lo, xb_hi):
    row = rows()
    below, above = y_terms(yh_lo, yh_hi)
    for ex, xb, slots, at in ((ex_hi, xb_hi, XPOS, N - 1), (ex_lo, xb_lo, XNEG, 0)):
        for q, i in enumerate(slots):
            v = ex[i]
            if C[i][1] == 1:
                v = jnp.where(row == 0, spread(line(yh_lo, YPOS.index(i), at)), v)
            elif C[i][1] == -1:
                v = jnp.where(row == N - 1, spread(line(yh_hi, YNEG.index(i), at)), v)
            xb[q * N:(q + 1) * N, :] = v
        for q, m in ((5, 0), (6, 1)):
            v = mom[m, at] + jnp.where(row == 0, spread(row_of(below[m], at)), 0.0)
            xb[q * N:(q + 1) * N, :] = v + jnp.where(row == N - 1, spread(row_of(above[m], at)), 0.0)
        c = 1 if at else -1
        k = LINE if at else LINE + 2
        down = line(yb_lo, YNEG.index(9 if c == 1 else 8), at)
        up = line(yb_hi, YPOS.index(7 if c == 1 else 10), at)
        xb[LINE:LINE + 1, :] = yh_lo[k:k + 1, :] + down
        xb[LINE + 1:LINE + 2, :] = yh_lo[k + 1:k + 2, :] - down
        xb[LINE + 2:LINE + 3, :] = yh_hi[k:k + 1, :] + up
        xb[LINE + 3:LINE + 4, :] = yh_hi[k + 1:k + 2, :] + up
        xb[LINE + 4:, :] = jnp.zeros((4, Z), F32)


def pack_pot_kernel(pot, fy_lo, fy_hi, o_hi, o_lo):
    for k in range(RING):
        o_hi[k * N:(k + 1) * N, :] = pot[N - 1 - k]
        o_lo[k * N:(k + 1) * N, :] = pot[k]
    for at, a, side, b in POT_ROWS:
        halo = fy_hi if side else fy_lo
        o_hi[at:at + 1, :] = halo[b - 1, N - a:N - a + 1, :]
        o_lo[at:at + 1, :] = halo[b - 1, a - 1:a, :]
    end = POT_ROWS[-1][0] + 1
    o_hi[end:, :] = jnp.zeros((POT_LEN - end, Z), F32)
    o_lo[end:, :] = jnp.zeros((POT_LEN - end, Z), F32)


def transport_kernel(charge, classes_h, mom, cond, conc, pot, yh_lo, yh_hi, xh_lo, xh_hi, yb_lo, yb_hi, xb_lo, xb_hi,
                     fx_lo, fx_hi, fy_lo, fy_hi, gy_lo, conc_out, src, sy_lo, sy_hi,
                     drift, lines, low, dy_hi, own_dy, classes, sem):
    fetch = pltpu.make_async_copy(classes_h, classes, sem)
    fetch.start()
    row = rows()
    below, above = y_terms(yh_lo, yh_hi)
    for m in range(4):
        lines[m] = below[m]
        lines[4 + m] = above[m]

    def step(x, extra):
        here = pl.ds(x, 1)

        def full(m):
            v = mom[m, x]
            if extra is not None:
                v = v + extra[m]
            v = v + jnp.where(row == 0, spread(lines[m, here, :]), 0.0)
            return v + jnp.where(row == N - 1, spread(lines[4 + m, here, :]), 0.0)

        scale = jnp.where(cond[x] > 0.0, 1.0 / full(0), 0.0)
        drift[0, x] = full(1) * scale
        v = full(2) * scale
        drift[1, x] = v
        drift[2, x] = full(3) * scale
        own_dy[here, :] = row_of(v, 0)

    a = [plane(xh_lo, q) for q in range(5)]
    total = a[0] + a[1] + a[2] + a[3] + a[4]
    step(0, (total, total, a[1] - a[2], a[3] - a[4]))
    b = [plane(xh_hi, q) for q in range(5)]
    total = b[0] + b[1] + b[2] + b[3] + b[4]
    step(N - 1, (total, -total, b[2] - b[1], b[4] - b[3]))

    def loop(x, carry):
        step(x, None)
        return carry

    lax.fori_loop(1, N - 1, loop, 0, unroll=2)

    def velocity(conductance, density, momentum):
        return jnp.where(conductance > 0.0, momentum / density, 0.0)

    def x_face(fx, xh, xb, sign):
        out = plane(xb, 0) + plane(xb, 1) + plane(xb, 2) + plane(xb, 3) + plane(xb, 4)
        d = velocity(fx[3], plane(xh, 5) + out, plane(xh, 6) + sign * out)
        return (fx[1], fx[2], fx[3], fx[0], d)

    from_hi, from_lo = y_terms(yb_hi, yb_lo)

    def y_face(fy, yh, terms, k):
        density = plane(yh, 5) + terms[0]
        momentum = plane(yh, 6) + terms[2]
        for xh, x in ((xh_lo, 0), (xh_hi, N - 1)):
            density = density + jnp.where(row == x, spread(xh[k:k + 1, :]), 0.0)
            momentum = momentum + jnp.where(row == x, spread(xh[k + 1:k + 2, :]), 0.0)
        d = velocity(fy[RING + 2], density, momentum)
        return (fy[RING], fy[RING + 1], fy[RING + 2], fy[0], d)

    left = y_face(fy_lo, yh_lo, from_lo, LINE)
    first = flux(left, (gy_lo[RING], gy_lo[RING + 1], gy_lo[RING + 2], gy_lo[0], own_dy[...]))
    low[0] = first[0]
    low[1] = first[1]
    dy_hi[...] = y_face(fy_hi, yh_hi, from_hi, LINE + 2)[4]
    fetch.wait()

    def fields(x, d):
        return (conc[0, x], conc[1, x], cond[x], pot[x], drift[d, x])

    def one(x, behind, ahead):
        here = pl.ds(x, 1)
        me = fields(x, 0)
        fx = flux(me, ahead)
        tot = [fx[s] - behind[s] for s in range(2)]
        mine = me[:4] + (drift[1, x],)
        halo = (fy_hi[RING, here, :], fy_hi[RING + 1, here, :], fy_hi[RING + 2, here, :], fy_hi[0, here, :], dy_hi[here, :])
        nxt = tuple(jnp.where(row == N - 1, spread(halo[q]), roll_y(mine[q], -1)) for q in range(5))
        fy = flux(mine, nxt)
        for s in range(2):
            before = jnp.where(row == 0, spread(low[s, here, :]), roll_y(fy[s], 1))
            tot[s] = tot[s] + (fy[s] - before)
        mine = me[:4] + (drift[2, x],)
        fz = flux(mine, tuple(roll_z(v, -1) for v in mine))
        for s in range(2):
            tot[s] = tot[s] + (fz[s] - roll_z(fz[s], 1))
        c0 = me[0] - tot[0]
        c1 = me[1] - tot[1]
        conc_out[0, x] = c0
        conc_out[1, x] = c1
        cls = classes[x]
        wall = jnp.zeros((N, Z), F32)
        for q in range(4):
            wall = wall + jnp.where(cls == q, charge[q], 0.0)
        s_val = jnp.where(me[2] > 0.0, c0 - c1, wall)
        src[x] = s_val
        for r in range(RING - 1):
            sy_lo[r, here, :] = row_of(s_val, r)
            sy_hi[r, here, :] = row_of(s_val, N - 1 - r)
        return tuple(fx)

    carry = tuple(flux(x_face(fx_lo, xh_lo, xb_lo, -1.0), fields(0, 0)))
    carry = lax.fori_loop(0, N - 1, lambda x, c: one(x, c, fields(x + 1, 0)), carry)
    one(N - 1, carry, x_face(fx_hi, xh_hi, xb_hi, 1.0))


def sweep_kernel(pot, src, fy_lo, fy_hi, xa_lo, xa_hi, ys_lo, ys_hi, xs_lo, xs_hi, out, ext, even, odd, s_even, s_odd):
    mid = slice(OFF, OFF + N)
    top = RING + N
    half = (N + 2 * RING) // 2
    shape = (N + 2 * OFF, Z)
    mask = (lax.broadcasted_iota(jnp.int32, shape, 0) + lax.broadcasted_iota(jnp.int32, shape, 1)) % 2 == 0

    def fill(centre, y_lo, y_hi, x_lo, x_hi, depth, listed):
        def own(x, carry):
            here = pl.ds(x, 1)
            ext[RING + x, mid] = centre[x]
            for r in range(depth):
                ext[RING + x, OFF - 1 - r:OFF - r, :] = y_lo[r, here, :]
                ext[RING + x, OFF + N + r:OFF + N + r + 1, :] = y_hi[r, here, :]
            return carry

        lax.fori_loop(0, N, own, 0, unroll=2)
        for r in range(depth):
            ext[RING - 1 - r, mid] = x_lo[r * N:(r + 1) * N, :]
            ext[top + r, mid] = x_hi[r * N:(r + 1) * N, :]
        for at, a, side, b in listed:
            y = OFF + N + b - 1 if side else OFF - b
            ext[RING - a, y:y + 1, :] = x_lo[at:at + 1, :]
            ext[top + a - 1, y:y + 1, :] = x_hi[at:at + 1, :]

    def split(a, b):
        def pack(k, carry):
            p, q = ext[2 * k], ext[2 * k + 1]
            a[k + 1] = jnp.where(mask, p, q)
            b[k + 1] = jnp.where(mask, q, p)
            return carry

        lax.fori_loop(0, half, pack, 0, unroll=2)

    zero = jnp.zeros(shape, F32)
    for ref in (even, odd):
        ref[0] = zero
        ref[half + 1] = zero
    fill(pot, fy_lo, fy_hi, xa_lo, xa_hi, RING, POT_ROWS)
    split(even, odd)
    fill(src, ys_lo, ys_hi, xs_lo, xs_hi, RING - 1, SRC_ROWS)
    split(s_even, s_odd)
    for h in range(6):
        this, other, s = (even, odd, s_even) if h % 2 == 0 else (odd, even, s_odd)

        def update(k, carry, h=h, this=this, other=other, s=s):
            c = other[k]
            before, after = other[k - 1], other[k + 1]
            far = jnp.where(mask, before, after) if h % 2 == 0 else jnp.where(mask, after, before)
            nb = (c + far) + (roll_y(c, 1) + roll_y(c, -1)) + (roll_z(c, 1) + roll_z(c, -1))
            this[k] = -0.6 * this[k] + (1.6 / 6.0) * (nb + s[k])
            return carry

        lo = (h + 1) // 2
        lax.fori_loop(lo + 1, half - lo + 1, update, 0, unroll=2)

    def last(k, carry):
        p, q = even[k], odd[k]
        out[2 * (k - 1) - RING] = jnp.where(mask, p, q)[OFF:OFF + N]
        out[2 * (k - 1) - RING + 1] = jnp.where(mask, q, p)[OFF:OFF + N]
        return carry

    lax.fori_loop(RING // 2 + 1, RING // 2 + N // 2 + 1, last, 0)


def patch_kernel(buf, ex_lo, ex_hi, ey_lo, ey_hi, yh_lo, yh_hi, xh_lo, xh_hi, out, done, sems):
    row = rows()
    copies = []
    for i in range(19):
        cx, cy, _ = C[i]

        def halo(v, src, i=i, cy=cy):
            if cy == 1:
                return jnp.where(row == 0, spread(yh_lo[pl.ds(YPOS.index(i) * N + src, 1), :]), v)
            if cy == -1:
                return jnp.where(row == N - 1, spread(yh_hi[pl.ds(YNEG.index(i) * N + src, 1), :]), v)
            return v

        def inner(src, carry, i=i, cx=cx, cy=cy, halo=halo):
            here = pl.ds(src, 1)
            v = buf[i, src + cx]
            if cy != -1:
                v = jnp.where(row == cy, spread(ey_lo[i, here, :]), v)
            if cy != 1:
                v = jnp.where(row == N - 1 + cy, spread(ey_hi[i, here, :]), v)
            done[i, src + cx] = halo(v, src)
            return carry

        lax.fori_loop(1, N - 1, inner, 0, unroll=2)
        if cx != -1:
            done[i, cx] = halo(ex_lo[i], 0)
        if cx != 1:
            done[i, N - 1 + cx] = halo(ex_hi[i], N - 1)
        if cx == 1:
            done[i, 0] = plane(xh_lo, XPOS.index(i))
        if cx == -1:
            done[i, N - 1] = plane(xh_hi, XNEG.index(i))
        copy = pltpu.make_async_copy(done.at[i], out.at[i], sems.at[i])
        copy.start()
        copies.append(copy)
    for copy in copies:
        copy.wait()


def flux(a, b):
    link = a[2] * b[2]
    carried = 0.5 * (a[4] + b[4])
    drop = a[3] - b[3]
    got = []
    for s in range(2):
        mean = 0.5 * (a[s] + b[s])
        got.append(link * (RATES[s] * ((a[s] - b[s]) + (VAL[s] * mean) * drop) + mean * carried))
    return got


def ring_rows(depth, total):
    listed = []
    at = depth
    for a in range(1, total):
        for side in (0, 1):
            for b in range(1, total - a + 1):
                listed.append((at, a, side, b))
                at += 1
    return listed


POT_ROWS = ring_rows(RING * N, RING)
SRC_ROWS = ring_rows((RING - 1) * N, RING - 1)
POT_LEN = 128
SRC_LEN = 104


def pack_src_kernel(src, ys_lo, ys_hi, o_hi, o_lo):
    for k in range(RING - 1):
        o_hi[k * N:(k + 1) * N, :] = src[N - 1 - k]
        o_lo[k * N:(k + 1) * N, :] = src[k]
    for at, a, side, b in SRC_ROWS:
        halo = ys_hi if side else ys_lo
        o_hi[at:at + 1, :] = halo[b - 1, N - a:N - a + 1, :]
        o_lo[at:at + 1, :] = halo[b - 1, a - 1:a, :]
    end = SRC_ROWS[-1][0] + 1
    o_hi[end:, :] = jnp.zeros((SRC_LEN - end, Z), F32)
    o_lo[end:, :] = jnp.zeros((SRC_LEN - end, Z), F32)


def swap(axis, hi, lo):
    n = lax.axis_size(axis)
    up = [(i, (i + 1) % n) for i in range(n)]
    down = [(b, a) for a, b in up]
    return lax.ppermute(hi, axis, up), lax.ppermute(lo, axis, down)


def body(pops, conc, pot, mob, solid, classes, charge):
    cube = sds(N, N, Z)
    msg = sds(ROWS, Z)
    gx_hi, gx_lo, gy_hi, gy_lo, pot, conc, cond = call(
        faces_kernel, [sds(4, N, Z)] * 2 + [sds(RING + 3, N, Z)] * 2 + [cube, sds(2, N, N, Z), cube], "faces", "hhhh",
        scratch=[VM((N, N, Z), F32), VM((N, N, Z), jnp.int32), pltpu.SemaphoreType.DMA((4,))], moved=2600000)(
        pot, conc, mob, solid)
    fx_lo, fx_hi = swap("gx", gx_hi, gx_lo)
    fy_lo, fy_hi = swap("gy", gy_hi, gy_lo)
    chunks = N // CHUNK
    buf, mom, px_lo, px_hi, pr_lo, pr_hi = call(
        collide_kernel, [sds(19, N, N, Z), sds(4, N, N, Z)] + [sds(19, N, Z)] * 4, "collide", "hvvv",
        scratch=[VM((19, N, N, Z), F32), pltpu.SemaphoreType.DMA((chunks,)), pltpu.SemaphoreType.DMA((2,))],
        mib=24, flops=20000000, moved=14000000)(pops, pot, conc, cond)
    mom, ex_lo, ex_hi, ey_lo, ey_hi, yb_lo, yb_hi = call(
        edge_kernel, [sds(4, N, N, Z)] + [sds(19, N, Z)] * 4 + [msg, msg], "edge", "v" * 14, moved=3000000)(
        px_lo, px_hi, pr_lo, pr_hi, gx_lo, gx_hi, gy_lo, gy_hi, fx_lo, fx_hi, fy_lo, fy_hi, pot, mom)
    yh_lo, yh_hi = swap("gy", yb_hi, yb_lo)
    xb_lo, xb_hi = call(corner_kernel, [msg, msg], "corner", "v" * 7)(ex_lo, ex_hi, yh_lo, yh_hi, yb_lo, yb_hi, mom)
    xh_lo, xh_hi = swap("gx", xb_hi, xb_lo)
    fy_lo2, fy_hi2, _, _ = lax.optimization_barrier((fy_lo, fy_hi, yh_lo, yh_hi))
    bx_hi, bx_lo = call(pack_pot_kernel, [sds(POT_LEN, Z)] * 2, "pack_pot", "vvv")(pot, fy_lo2, fy_hi2)
    xa_lo, xa_hi = swap("gx", bx_hi, bx_lo)
    face = VM((N, Z), F32)
    conc_out, src, sy_lo, sy_hi = call(
        transport_kernel, [sds(2, N, N, Z), cube, sds(RING - 1, N, Z), sds(RING - 1, N, Z)], "transport", "sh" + "v" * 17,
        scratch=[VM((3, N, N, Z), F32), VM((8, N, Z), F32), VM((2, N, Z), F32), face, face, VM((N, N, Z), jnp.int32),
                 pltpu.SemaphoreType.DMA], flops=10000000, moved=8000000)(
        charge, classes, mom, cond, conc, pot, yh_lo, yh_hi, xh_lo, xh_hi, yb_lo, yb_hi, xb_lo, xb_hi,
        fx_lo, fx_hi, fy_lo, fy_hi, gy_lo)
    ys_lo, ys_hi = swap("gy", sy_hi, sy_lo)
    bs_hi, bs_lo = call(pack_src_kernel, [sds(SRC_LEN, Z)] * 2, "pack_src", "vvv")(src, ys_lo, ys_hi)
    xs_lo, xs_hi = swap("gx", bs_hi, bs_lo)
    packed = VM(((N + 2 * RING) // 2 + 2, N + 2 * OFF, Z), F32)
    potential_out = call(
        sweep_kernel, [cube], "sweep", "v" * 10,
        scratch=[VM((N + 2 * RING, N + 2 * OFF, Z), F32)] + [packed] * 4, flops=20000000, moved=4000000)(
        pot, src, fy_lo, fy_hi, xa_lo, xa_hi, ys_lo, ys_hi, xs_lo, xs_hi)[0]
    pop = call(
        patch_kernel, [sds(19, N, N, Z)], "patch", "v" * 9, out_specs="h",
        scratch=[VM((19, N, N, Z), F32), pltpu.SemaphoreType.DMA((19,))], mib=16, moved=10000000)(
        buf, ex_lo, ex_hi, ey_lo, ey_hi, yh_lo, yh_hi, xh_lo, xh_hi)[0]
    return (pop, conc_out, potential_out)


def solution(mesh):
    lattice = P(None, "gx", "gy", None)
    flat = P("gx", "gy", None)
    return jax.shard_map(
        body, mesh=mesh, in_specs=(lattice, lattice, flat, flat, flat, flat, P()),
        out_specs=(lattice, lattice, flat), check_vma=False)
```

```python
import jax
import jax.numpy as jnp
from jax import lax
from jax.experimental import pallas as pl
from jax.experimental.pallas import tpu as pltpu
from jax.sharding import PartitionSpec as P

C = [(0, 0, 0), (1, 0, 0), (-1, 0, 0), (0, 1, 0), (0, -1, 0), (0, 0, 1), (0, 0, -1),
     (1, 1, 0), (-1, -1, 0), (1, -1, 0), (-1, 1, 0), (1, 0, 1), (-1, 0, -1), (1, 0, -1), (-1, 0, 1),
     (0, 1, 1), (0, -1, -1), (0, 1, -1), (0, -1, 1)]
W = [1.0 / 3.0] + [1.0 / 18.0] * 6 + [1.0 / 36.0] * 12
XPOS = [i for i in range(19) if C[i][0] == 1]
XNEG = [i for i in range(19) if C[i][0] == -1]
YPOS = [i for i in range(19) if C[i][1] == 1]
YNEG = [i for i in range(19) if C[i][1] == -1]
RATES = (0.06, 0.08)
VAL = (1.0, -1.0)
N = 16
Z = 256
CHUNK = 4
RING = 6
OFF = 8
ROWS = 7 * N + 8
LINE = 7 * N
F32 = jnp.float32
VM = pltpu.VMEM


def sds(*shape):
    return jax.ShapeDtypeStruct(shape, F32)


def params(mib):
    return pltpu.CompilerParams(vmem_limit_bytes=mib * 1024 * 1024)


def rows():
    return lax.broadcasted_iota(jnp.int32, (N, Z), 0)


def roll_y(v, s):
    return pltpu.roll(v, s % v.shape[0], 0)


def roll_z(v, s):
    return pltpu.roll(v, s % v.shape[1], 1)


def row_of(v, y):
    return v[y:y + 1, :]


def spread(row):
    return jnp.broadcast_to(row, (N, Z))


def shift_up(v):
    return jnp.where(rows() == 0, 0.0, roll_y(v, 1))


def shift_down(v):
    return jnp.where(rows() == N - 1, 0.0, roll_y(v, -1))


def shift_by(v, c):
    return shift_up(v) if c == 1 else shift_down(v) if c == -1 else v


def call(kernel, outs, name, specs, scratch=(), mib=16, flops=0, out_specs=None, moved=0):
    return pl.pallas_call(
        kernel,
        in_specs=[pl.BlockSpec(memory_space={"v": VM, "h": pltpu.HBM, "s": pltpu.SMEM}[c]) for c in specs],
        out_specs=[pl.BlockSpec(memory_space={"v": VM, "h": pltpu.HBM}[c]) for c in out_specs or "v" * len(outs)],
        out_shape=outs,
        scratch_shapes=list(scratch),
        compiler_params=params(mib),
        cost_estimate=pl.CostEstimate(flops=flops, bytes_accessed=moved, transcendentals=0),
        name=name,
    )


def faces_kernel(pot_h, conc_h, mob_h, solid_h, gx_hi, gx_lo, gy_hi, gy_lo, cond, pot, conc, mob, solid, sems):
    pairs = ((pot_h, pot), (conc_h, conc), (mob_h, mob), (solid_h, solid))
    copies = [pltpu.make_async_copy(a, b, sems.at[q]) for q, (a, b) in enumerate(pairs)]
    for c in copies:
        c.start()
    for c in copies:
        c.wait()

    def step(x, carry):
        here = pl.ds(x, 1)
        cond[x] = jnp.where(solid[x] == 0, jnp.sqrt(mob[x]), 0.0)
        for r in range(RING):
            gy_hi[r, here, :] = pot[x, N - 1 - r:N - r, :]
            gy_lo[r, here, :] = pot[x, r:r + 1, :]
        for q, v in ((0, conc.at[0]), (1, conc.at[1]), (2, cond)):
            gy_hi[RING + q, here, :] = v[x, N - 1:N, :]
            gy_lo[RING + q, here, :] = v[x, 0:1, :]
        return carry

    lax.fori_loop(0, N, step, 0, unroll=2)
    for x, face in ((N - 1, gx_hi), (0, gx_lo)):
        for r in range(RING):
            face[r] = pot[abs(x - r)]
        face[RING] = conc[0, x]
        face[RING + 1] = conc[1, x]
        face[RING + 2] = cond[x]


def post_of(p, fluid, q, slopes):
    pull = jnp.where(fluid, q * (-0.001), 0.0)
    force = [pull * d for d in slopes]
    density = p[0]
    for i in range(1, 19):
        density = density + p[i]
    inv = 1.0 / density
    u = []
    for a in range(3):
        total = 0.9 * force[a]
        for i in range(1, 19, 2):
            if C[i][a]:
                term = p[i] - p[i + 1]
                total = total + term if C[i][a] == 1 else total - term
        u.append(total * inv)
    base = 1.0 - 1.5 * (u[0] * u[0] + u[1] * u[1] + u[2] * u[2])
    scaled = density * (10.0 / 9.0)
    out = [jnp.where(fluid, (W[0] * scaled) * base - p[0] * (1.0 / 9.0), p[0])]
    for i in range(1, 19, 2):
        along = None
        for a in range(3):
            if C[i][a]:
                term = u[a] if C[i][a] == 1 else -u[a]
                along = term if along is None else along + term
        even = base + 4.5 * along * along
        odd = 3.0 * along
        ws = W[i] * scaled
        fwd = ws * (even + odd) - p[i] * (1.0 / 9.0)
        bwd = ws * (even - odd) - p[i + 1] * (1.0 / 9.0)
        out.append(jnp.where(fluid, fwd, p[i + 1]))
        out.append(jnp.where(fluid, bwd, p[i]))
    return out, force


def sums(values, keep):
    total = [None] * 4
    for cy in (0, 1, -1):
        part = [None] * 4
        for i, v in values:
            if C[i][1] != cy:
                continue
            for m, c in enumerate((1,) + C[i]):
                if c and m != 2:
                    w = v if c == 1 else -v
                    part[m] = w if part[m] is None else part[m] + w
        for m in (0, 1, 3):
            if part[m] is None:
                continue
            w = part[m] if keep[cy] is None else jnp.where(keep[cy], part[m], 0.0)
            total[m] = w if total[m] is None else total[m] + w
            if m == 0 and cy:
                w = w if cy == 1 else -w
                total[2] = w if total[2] is None else total[2] + w
    return total


def collide_kernel(pops, pot_h, conc_h, cond, buf, mom, px_lo, px_hi, pr_lo, pr_hi, held, pot, conc, sems, psems):
    chunks = [pltpu.make_async_copy(pops.at[:, pl.ds(CHUNK * s, CHUNK)], held.at[:, pl.ds(CHUNK * s, CHUNK)], sems.at[s])
              for s in range(N // CHUNK)]
    ends = [pltpu.make_async_copy(pops.at[:, 0], px_lo, psems.at[0]),
            pltpu.make_async_copy(pops.at[:, N - 1], px_hi, psems.at[1])]
    fields = [pltpu.make_async_copy(pot_h, pot, psems.at[2]), pltpu.make_async_copy(conc_h, conc, psems.at[3])]
    for c in fields + chunks + ends:
        c.start()
    row = rows()
    zero = jnp.zeros((N, Z), F32)
    keep = {0: (row >= 1) & (row <= N - 2), 1: row >= 2, -1: row <= N - 3}
    for m in range(4):
        mom[m, 0] = zero
        mom[m, 1] = zero

    def step(x, carry):
        here = pl.ds(x, 1)
        p = [held[i, x] for i in range(19)]
        for i in range(19):
            pr_lo[i, here, :] = row_of(p[i], 0)
            pr_hi[i, here, :] = row_of(p[i], N - 1)
        centre = pot[x]
        slopes = (pot[x + 1] - pot[x - 1], roll_y(centre, -1) - roll_y(centre, 1), roll_z(centre, -1) - roll_z(centre, 1))
        post, force = post_of(p, cond[x] > 0.0, conc[0, x] - conc[1, x], slopes)
        moved = []
        for i in range(19):
            v = post[i]
            if C[i][2]:
                v = roll_z(v, C[i][2])
            if C[i][1]:
                v = roll_y(v, C[i][1])
            buf[i, x + C[i][0]] = v
            moved.append(v)
        g = sums([(i, moved[i]) for i in range(19) if C[i][0] == 0], keep)
        mom[0, x] += g[0]
        for m in (1, 2, 3):
            w = jnp.where(keep[0], 0.5 * force[m - 1], 0.0)
            mom[m, x] += w if g[m] is None else g[m] + w
        g = sums([(i, moved[i]) for i in XPOS], keep)
        for m in range(4):
            mom[m, x + 1] = g[m]
        g = sums([(i, moved[i]) for i in XNEG], keep)
        for m in range(4):
            mom[m, x - 1] += g[m]
        return carry

    for c in fields:
        c.wait()
    for s in range(N // CHUNK):
        chunks[s].wait()
        lax.fori_loop(max(CHUNK * s, 1), min(CHUNK * s + CHUNK, N - 1), step, 0)
    for c in ends:
        c.wait()


def edge_kernel(px_lo, px_hi, pr_lo, pr_hi, gx_lo, gx_hi, gy_lo, gy_hi, fx_lo, fx_hi, fy_lo, fy_hi, mom0,
                mom, ex_lo, ex_hi, ey_lo, ey_hi, yb_lo, yb_hi):
    row = rows()
    inner = (row >= 1) & (row <= N - 2)
    keep = {0: None, 1: row >= 1, -1: row <= N - 2}
    lines = {}
    for pr, gy, fy, ey, low in ((pr_lo, gy_lo, fy_lo, ey_lo, True), (pr_hi, gy_hi, fy_hi, ey_hi, False)):
        centre = gy[0]
        y_slope = gy[1] - fy[0] if low else fy[0] - gy[1]
        slopes = (roll_y(centre, -1) - roll_y(centre, 1), y_slope, roll_z(centre, -1) - roll_z(centre, 1))
        post, force = post_of([pr[i] for i in range(19)], gy[RING + 2] > 0.0, gy[RING] - gy[RING + 1], slopes)
        for i in range(19):
            v = roll_z(post[i], C[i][2]) if C[i][2] else post[i]
            v = jnp.where(inner, v, 0.0)
            ey[i] = v
            if low and C[i][1] == -1:
                q = YNEG.index(i)
                yb_lo[q * N:(q + 1) * N, :] = v
            if not low and C[i][1] == 1:
                q = YPOS.index(i)
                yb_hi[q * N:(q + 1) * N, :] = v
            post[i] = shift_by(v, C[i][0])
        for cy in (0, 1 if low else -1):
            y = (0 if low else N - 1) + cy
            total = [None] * 4
            for i in range(19):
                if C[i][1] == cy:
                    for m, c in enumerate((1,) + C[i]):
                        if c:
                            w = post[i] if c == 1 else -post[i]
                            total[m] = w if total[m] is None else total[m] + w
            if cy == 0:
                for a in range(3):
                    w = jnp.where(inner, 0.5 * force[a], 0.0)
                    total[a + 1] = w if total[a + 1] is None else total[a + 1] + w
            lines[y] = total
    for x in range(N):
        for m in range(4):
            v = mom0[m, x]
            for y in (0, 1, N - 2, N - 1):
                v = v + jnp.where(row == y, spread(row_of(lines[y][m], x)), 0.0)
            mom[m, x] = v
    for px, gx, fx, ex, low in ((px_lo, gx_lo, fx_lo, ex_lo, True), (px_hi, gx_hi, fx_hi, ex_hi, False)):
        at = 0 if low else N - 1
        centre = gx[0]
        x_slope = gx[1] - fx[0] if low else fx[0] - gx[1]
        y_up = jnp.where(row == N - 1, spread(fy_hi[0, at:at + 1, :]), roll_y(centre, -1))
        y_dn = jnp.where(row == 0, spread(fy_lo[0, at:at + 1, :]), roll_y(centre, 1))
        slopes = (x_slope, y_up - y_dn, roll_z(centre, -1) - roll_z(centre, 1))
        post, force = post_of([px[i] for i in range(19)], gx[RING + 2] > 0.0, gx[RING] - gx[RING + 1], slopes)
        for i in range(19):
            v = roll_z(post[i], C[i][2]) if C[i][2] else post[i]
            if C[i][1] == 1:
                v = roll_y(v, 1)
                at_row = YPOS.index(i) * N + at
                yb_hi[at_row:at_row + 1, :] = row_of(v, 0)
                v = jnp.where(row == 0, 0.0, v)
            elif C[i][1] == -1:
                v = roll_y(v, -1)
                at_row = YNEG.index(i) * N + at
                yb_lo[at_row:at_row + 1, :] = row_of(v, N - 1)
                v = jnp.where(row == N - 1, 0.0, v)
            ex[i] = v
            post[i] = v
        none = {0: None, 1: None, -1: None}
        g = sums([(i, post[i]) for i in range(19) if C[i][0] == 0], none)
        mom[0, at] += g[0]
        for m in (1, 2, 3):
            w = 0.5 * force[m - 1]
            mom[m, at] += w if g[m] is None else g[m] + w
        g = sums([(i, post[i]) for i in (XPOS if low else XNEG)], none)
        for m in range(4):
            mom[m, 1 if low else N - 2] += g[m]
        g = sums([(i, post[i]) for i in (XNEG if low else XPOS)], none)
        k = LINE + (2 if low else 0)
        yb_hi[k:k + 1, :] = row_of(g[0], N - 1)
        yb_hi[k + 1:k + 2, :] = row_of(g[2], N - 1)
        yb_lo[k:k + 1, :] = row_of(g[0], 0)
        yb_lo[k + 1:k + 2, :] = row_of(g[2], 0)
    for x in range(N):
        for q, m in ((5, 0), (6, 2)):
            yb_lo[q * N + x:q * N + x + 1, :] = mom[m, x, 0:1, :]
            yb_hi[q * N + x:q * N + x + 1, :] = mom[m, x, N - 1:N, :]
    yb_lo[LINE + 4:, :] = jnp.zeros((4, Z), F32)
    yb_hi[LINE + 4:, :] = jnp.zeros((4, Z), F32)


def plane(ref, q):
    return ref[q * N:(q + 1) * N, :]


def line(ref, q, x):
    return ref[q * N + x:q * N + x + 1, :]


def y_terms(lo, hi):
    s3, s7, s10, s15, s17 = (plane(lo, q) for q in range(5))
    s7, s10 = shift_up(s7), shift_down(s10)
    total = s3 + s7 + s10 + s15 + s17
    below = (total, s7 - s10, total, s15 - s17)
    s4, s8, s9, s16, s18 = (plane(hi, q) for q in range(5))
    s8, s9 = shift_down(s8), shift_up(s9)
    total = s4 + s8 + s9 + s16 + s18
    return below, (total, s9 - s8, -total, s18 - s16)


def corner_kernel(ex_lo, ex_hi, yh_lo, yh_hi, yb_lo, yb_hi, mom, xb_lo, xb_hi):
    row = rows()
    below, above = y_terms(yh_lo, yh_hi)
    for ex, xb, slots, at in ((ex_hi, xb_hi, XPOS, N - 1), (ex_lo, xb_lo, XNEG, 0)):
        for q, i in enumerate(slots):
            v = ex[i]
            if C[i][1] == 1:
                v = jnp.where(row == 0, spread(line(yh_lo, YPOS.index(i), at)), v)
            elif C[i][1] == -1:
                v = jnp.where(row == N - 1, spread(line(yh_hi, YNEG.index(i), at)), v)
            xb[q * N:(q + 1) * N, :] = v
        for q, m in ((5, 0), (6, 1)):
            v = mom[m, at] + jnp.where(row == 0, spread(row_of(below[m], at)), 0.0)
            xb[q * N:(q + 1) * N, :] = v + jnp.where(row == N - 1, spread(row_of(above[m], at)), 0.0)
        c = 1 if at else -1
        k = LINE if at else LINE + 2
        down = line(yb_lo, YNEG.index(9 if c == 1 else 8), at)
        up = line(yb_hi, YPOS.index(7 if c == 1 else 10), at)
        xb[LINE:LINE + 1, :] = yh_lo[k:k + 1, :] + down
        xb[LINE + 1:LINE + 2, :] = yh_lo[k + 1:k + 2, :] - down
        xb[LINE + 2:LINE + 3, :] = yh_hi[k:k + 1, :] + up
        xb[LINE + 3:LINE + 4, :] = yh_hi[k + 1:k + 2, :] + up
        xb[LINE + 4:, :] = jnp.zeros((4, Z), F32)


def transport_kernel(charge, classes_h, mom, cond, conc, pot, yh_lo, yh_hi, xh_lo, xh_hi, yb_lo, yb_hi, xb_lo, xb_hi,
                     fx_lo, fx_hi, fy_lo, fy_hi, gy_lo, conc_out, src, sy_lo, sy_hi,
                     drift, lines, low, dy_hi, own_dy, classes, sem):
    fetch = pltpu.make_async_copy(classes_h, classes, sem)
    fetch.start()
    row = rows()
    below, above = y_terms(yh_lo, yh_hi)
    for m in range(4):
        lines[m] = below[m]
        lines[4 + m] = above[m]

    def step(x, extra):
        here = pl.ds(x, 1)

        def full(m):
            v = mom[m, x]
            if extra is not None:
                v = v + extra[m]
            v = v + jnp.where(row == 0, spread(lines[m, here, :]), 0.0)
            return v + jnp.where(row == N - 1, spread(lines[4 + m, here, :]), 0.0)

        scale = jnp.where(cond[x] > 0.0, 1.0 / full(0), 0.0)
        drift[0, x] = full(1) * scale
        v = full(2) * scale
        drift[1, x] = v
        drift[2, x] = full(3) * scale
        own_dy[here, :] = row_of(v, 0)

    a = [plane(xh_lo, q) for q in range(5)]
    total = a[0] + a[1] + a[2] + a[3] + a[4]
    step(0, (total, total, a[1] - a[2], a[3] - a[4]))
    b = [plane(xh_hi, q) for q in range(5)]
    total = b[0] + b[1] + b[2] + b[3] + b[4]
    step(N - 1, (total, -total, b[2] - b[1], b[4] - b[3]))

    def loop(x, carry):
        step(x, None)
        return carry

    lax.fori_loop(1, N - 1, loop, 0, unroll=2)

    def velocity(conductance, density, momentum):
        return jnp.where(conductance > 0.0, momentum / density, 0.0)

    def x_face(fx, xh, xb, sign):
        out = plane(xb, 0) + plane(xb, 1) + plane(xb, 2) + plane(xb, 3) + plane(xb, 4)
        d = velocity(fx[RING + 2], plane(xh, 5) + out, plane(xh, 6) + sign * out)
        return (fx[RING], fx[RING + 1], fx[RING + 2], fx[0], d)

    from_hi, from_lo = y_terms(yb_hi, yb_lo)

    def y_face(fy, yh, terms, k):
        density = plane(yh, 5) + terms[0]
        momentum = plane(yh, 6) + terms[2]
        for xh, x in ((xh_lo, 0), (xh_hi, N - 1)):
            density = density + jnp.where(row == x, spread(xh[k:k + 1, :]), 0.0)
            momentum = momentum + jnp.where(row == x, spread(xh[k + 1:k + 2, :]), 0.0)
        d = velocity(fy[RING + 2], density, momentum)
        return (fy[RING], fy[RING + 1], fy[RING + 2], fy[0], d)

    left = y_face(fy_lo, yh_lo, from_lo, LINE)
    first = flux(left, (gy_lo[RING], gy_lo[RING + 1], gy_lo[RING + 2], gy_lo[0], own_dy[...]))
    low[0] = first[0]
    low[1] = first[1]
    dy_hi[...] = y_face(fy_hi, yh_hi, from_hi, LINE + 2)[4]
    fetch.wait()

    def fields(x, d):
        return (conc[0, x], conc[1, x], cond[x], pot[x], drift[d, x])

    def one(x, behind, ahead):
        here = pl.ds(x, 1)
        me = fields(x, 0)
        fx = flux(me, ahead)
        tot = [fx[s] - behind[s] for s in range(2)]
        mine = me[:4] + (drift[1, x],)
        halo = (fy_hi[RING, here, :], fy_hi[RING + 1, here, :], fy_hi[RING + 2, here, :], fy_hi[0, here, :], dy_hi[here, :])
        nxt = tuple(jnp.where(row == N - 1, spread(halo[q]), roll_y(mine[q], -1)) for q in range(5))
        fy = flux(mine, nxt)
        for s in range(2):
            before = jnp.where(row == 0, spread(low[s, here, :]), roll_y(fy[s], 1))
            tot[s] = tot[s] + (fy[s] - before)
        mine = me[:4] + (drift[2, x],)
        fz = flux(mine, tuple(roll_z(v, -1) for v in mine))
        for s in range(2):
            tot[s] = tot[s] + (fz[s] - roll_z(fz[s], 1))
        c0 = me[0] - tot[0]
        c1 = me[1] - tot[1]
        conc_out[0, x] = c0
        conc_out[1, x] = c1
        cls = classes[x]
        wall = jnp.zeros((N, Z), F32)
        for q in range(4):
            wall = wall + jnp.where(cls == q, charge[q], 0.0)
        s_val = jnp.where(me[2] > 0.0, c0 - c1, wall)
        src[x] = s_val
        for r in range(RING - 1):
            sy_lo[r, here, :] = row_of(s_val, r)
            sy_hi[r, here, :] = row_of(s_val, N - 1 - r)
        return tuple(fx)

    carry = tuple(flux(x_face(fx_lo, xh_lo, xb_lo, -1.0), fields(0, 0)))
    for x in range(N - 1):
        carry = one(x, carry, fields(x + 1, 0))
    one(N - 1, carry, x_face(fx_hi, xh_hi, xb_hi, 1.0))


def sweep_kernel(pot, src, fy_lo, fy_hi, fx_lo, fx_hi, ys_lo, ys_hi, xs_lo, xs_hi, out, ext, even, odd, s_even, s_odd):
    mid = slice(OFF, OFF + N)
    top = RING + N
    half = (N + 2 * RING) // 2
    shape = (N + 2 * OFF, Z)
    mask = (lax.broadcasted_iota(jnp.int32, shape, 0) + lax.broadcasted_iota(jnp.int32, shape, 1)) % 2 == 0

    def fill(centre, y_lo, y_hi, x_lo, x_hi, depth, listed):
        def own(x, carry):
            here = pl.ds(x, 1)
            ext[RING + x, mid] = centre[x]
            for r in range(depth):
                ext[RING + x, OFF - 1 - r:OFF - r, :] = y_lo[r, here, :]
                ext[RING + x, OFF + N + r:OFF + N + r + 1, :] = y_hi[r, here, :]
            return carry

        lax.fori_loop(0, N, own, 0, unroll=2)
        for r in range(depth):
            ext[RING - 1 - r, mid] = x_lo(r)
            ext[top + r, mid] = x_hi(r)
        for at, a, side, b in listed:
            y = OFF + N + b - 1 if side else OFF - b
            ext[RING - a, y:y + 1, :] = xs_lo[at:at + 1, :]
            ext[top + a - 1, y:y + 1, :] = xs_hi[at:at + 1, :]

    def split(a, b):
        def pack(k, carry):
            p, q = ext[2 * k], ext[2 * k + 1]
            a[k + 1] = jnp.where(mask, p, q)
            b[k + 1] = jnp.where(mask, q, p)
            return carry

        lax.fori_loop(0, half, pack, 0, unroll=2)

    zero = jnp.zeros(shape, F32)
    for ref in (even, odd):
        ref[0] = zero
        ref[half + 1] = zero
    fill(pot, fy_lo, fy_hi, lambda r: fx_lo[r], lambda r: fx_hi[r], RING, POT_ROWS)
    split(even, odd)
    fill(src, ys_lo, ys_hi, lambda r: plane(xs_lo, r), lambda r: plane(xs_hi, r), RING - 1, SRC_ROWS)
    split(s_even, s_odd)
    for h in range(6):
        this, other, s = (even, odd, s_even) if h % 2 == 0 else (odd, even, s_odd)

        def update(k, carry, h=h, this=this, other=other, s=s):
            c = other[k]
            before, after = other[k - 1], other[k + 1]
            far = jnp.where(mask, before, after) if h % 2 == 0 else jnp.where(mask, after, before)
            nb = (c + far) + (roll_y(c, 1) + roll_y(c, -1)) + (roll_z(c, 1) + roll_z(c, -1))
            this[k] = -0.6 * this[k] + (1.6 / 6.0) * (nb + s[k])
            return carry

        lo = (h + 1) // 2
        lax.fori_loop(lo + 1, half - lo + 1, update, 0, unroll=2)

    def last(k, carry):
        p, q = even[k], odd[k]
        out[2 * (k - 1) - RING] = jnp.where(mask, p, q)[OFF:OFF + N]
        out[2 * (k - 1) - RING + 1] = jnp.where(mask, q, p)[OFF:OFF + N]
        return carry

    lax.fori_loop(RING // 2 + 1, RING // 2 + N // 2 + 1, last, 0)


def patch_kernel(buf, ex_lo, ex_hi, ey_lo, ey_hi, yh_lo, yh_hi, xh_lo, xh_hi, out, done, sems):
    row = rows()
    copies = []
    for i in range(19):
        cx, cy, _ = C[i]

        def halo(v, src, i=i, cy=cy):
            if cy == 1:
                return jnp.where(row == 0, spread(yh_lo[pl.ds(YPOS.index(i) * N + src, 1), :]), v)
            if cy == -1:
                return jnp.where(row == N - 1, spread(yh_hi[pl.ds(YNEG.index(i) * N + src, 1), :]), v)
            return v

        def inner(src, carry, i=i, cx=cx, cy=cy, halo=halo):
            here = pl.ds(src, 1)
            v = buf[i, src + cx]
            if cy != -1:
                v = jnp.where(row == cy, spread(ey_lo[i, here, :]), v)
            if cy != 1:
                v = jnp.where(row == N - 1 + cy, spread(ey_hi[i, here, :]), v)
            done[i, src + cx] = halo(v, src)
            return carry

        lax.fori_loop(1, N - 1, inner, 0, unroll=2)
        if cx != -1:
            done[i, cx] = halo(ex_lo[i], 0)
        if cx != 1:
            done[i, N - 1 + cx] = halo(ex_hi[i], N - 1)
        if cx == 1:
            done[i, 0] = plane(xh_lo, XPOS.index(i))
        if cx == -1:
            done[i, N - 1] = plane(xh_hi, XNEG.index(i))
        copy = pltpu.make_async_copy(done.at[i], out.at[i], sems.at[i])
        copy.start()
        copies.append(copy)
    for copy in copies:
        copy.wait()


def flux(a, b):
    link = a[2] * b[2]
    carried = 0.5 * (a[4] + b[4])
    drop = a[3] - b[3]
    got = []
    for s in range(2):
        mean = 0.5 * (a[s] + b[s])
        got.append(link * (RATES[s] * ((a[s] - b[s]) + (VAL[s] * mean) * drop) + mean * carried))
    return got


def ring_rows(depth, total):
    listed = []
    at = depth
    for a in range(1, total):
        for side in (0, 1):
            for b in range(1, total - a + 1):
                listed.append((at, a, side, b))
                at += 1
    return listed


SRC_ROWS = ring_rows((RING - 1) * N, RING - 1)
POT_ROWS = ring_rows(SRC_ROWS[-1][0] + 1, RING)
SRC_LEN = 136


def pack_src_kernel(src, ys_lo, ys_hi, fy_lo, fy_hi, o_hi, o_lo):
    for k in range(RING - 1):
        o_hi[k * N:(k + 1) * N, :] = src[N - 1 - k]
        o_lo[k * N:(k + 1) * N, :] = src[k]
    for listed, lo, hi in ((SRC_ROWS, ys_lo, ys_hi), (POT_ROWS, fy_lo, fy_hi)):
        for at, a, side, b in listed:
            halo = hi if side else lo
            o_hi[at:at + 1, :] = halo[b - 1, N - a:N - a + 1, :]
            o_lo[at:at + 1, :] = halo[b - 1, a - 1:a, :]
    end = POT_ROWS[-1][0] + 1
    o_hi[end:, :] = jnp.zeros((SRC_LEN - end, Z), F32)
    o_lo[end:, :] = jnp.zeros((SRC_LEN - end, Z), F32)


def swap(axis, hi, lo):
    n = lax.axis_size(axis)
    even = lax.axis_index(axis) % 2 == 0
    first = lax.ppermute(jnp.where(even, hi, lo), axis, [(i, i + 1 - 2 * (i % 2)) for i in range(n)])
    second = lax.ppermute(jnp.where(even, lo, hi), axis, [(i, (i - 1 + 2 * (i % 2)) % n) for i in range(n)])
    return jnp.where(even, second, first), jnp.where(even, first, second)


def body(pops, conc, pot, mob, solid, classes, charge):
    cube = sds(N, N, Z)
    msg = sds(ROWS, Z)
    gx_hi, gx_lo, gy_hi, gy_lo, cond = call(
        faces_kernel, [sds(RING + 3, N, Z)] * 4 + [cube], "faces", "hhhh",
        scratch=[VM((N, N, Z), F32), VM((2, N, N, Z), F32), VM((N, N, Z), F32), VM((N, N, Z), jnp.int32),
                 pltpu.SemaphoreType.DMA((4,))], mib=53, moved=2600000)(
        pot, conc, mob, solid)
    fx_lo, fx_hi = swap("gx", gx_hi, gx_lo)
    fy_lo, fy_hi = swap("gy", gy_hi, gy_lo)
    chunks = N // CHUNK
    buf, mom, px_lo, px_hi, pr_lo, pr_hi = call(
        collide_kernel, [sds(19, N, N, Z), sds(4, N, N, Z)] + [sds(19, N, Z)] * 4, "collide", "hhhv",
        scratch=[VM((19, N, N, Z), F32), VM((N, N, Z), F32), VM((2, N, N, Z), F32),
                 pltpu.SemaphoreType.DMA((chunks,)), pltpu.SemaphoreType.DMA((4,))],
        mib=43, flops=20000000, moved=14000000)(pops, pot, conc, cond)
    mom, ex_lo, ex_hi, ey_lo, ey_hi, yb_lo, yb_hi = call(
        edge_kernel, [sds(4, N, N, Z)] + [sds(19, N, Z)] * 4 + [msg, msg], "edge", "v" * 13, moved=3000000)(
        px_lo, px_hi, pr_lo, pr_hi, gx_lo, gx_hi, gy_lo, gy_hi, fx_lo, fx_hi, fy_lo, fy_hi, mom)
    yh_lo, yh_hi = swap("gy", yb_hi, yb_lo)
    xb_lo, xb_hi = call(corner_kernel, [msg, msg], "corner", "v" * 7)(ex_lo, ex_hi, yh_lo, yh_hi, yb_lo, yb_hi, mom)
    xh_lo, xh_hi = swap("gx", xb_hi, xb_lo)
    face = VM((N, Z), F32)
    conc_out, src, sy_lo, sy_hi = call(
        transport_kernel, [sds(2, N, N, Z), cube, sds(RING - 1, N, Z), sds(RING - 1, N, Z)], "transport", "sh" + "v" * 17,
        scratch=[VM((3, N, N, Z), F32), VM((8, N, Z), F32), VM((2, N, Z), F32), face, face, VM((N, N, Z), jnp.int32),
                 pltpu.SemaphoreType.DMA], flops=10000000, moved=8000000)(
        charge, classes, mom, cond, conc, pot, yh_lo, yh_hi, xh_lo, xh_hi, yb_lo, yb_hi, xb_lo, xb_hi,
        fx_lo, fx_hi, fy_lo, fy_hi, gy_lo)
    ys_lo, ys_hi = swap("gy", sy_hi, sy_lo)
    bs_hi, bs_lo = call(pack_src_kernel, [sds(SRC_LEN, Z)] * 2, "pack_src", "v" * 5)(src, ys_lo, ys_hi, fy_lo, fy_hi)
    xs_lo, xs_hi = swap("gx", bs_hi, bs_lo)
    packed = VM(((N + 2 * RING) // 2 + 2, N + 2 * OFF, Z), F32)
    potential_out = call(
        sweep_kernel, [cube], "sweep", "v" * 10,
        scratch=[VM((N + 2 * RING, N + 2 * OFF, Z), F32)] + [packed] * 4, flops=20000000, moved=4000000)(
        pot, src, fy_lo, fy_hi, fx_lo, fx_hi, ys_lo, ys_hi, xs_lo, xs_hi)[0]
    pop = call(
        patch_kernel, [sds(19, N, N, Z)], "patch", "v" * 9, out_specs="h",
        scratch=[VM((19, N, N, Z), F32), pltpu.SemaphoreType.DMA((19,))], mib=16, moved=10000000)(
        buf, ex_lo, ex_hi, ey_lo, ey_hi, yh_lo, yh_hi, xh_lo, xh_hi)[0]
    return (pop, conc_out, potential_out)


def solution(mesh):
    lattice = P(None, "gx", "gy", None)
    flat = P("gx", "gy", None)
    return jax.shard_map(
        body, mesh=mesh, in_specs=(lattice, lattice, flat, flat, flat, flat, P()),
        out_specs=(lattice, lattice, flat), check_vma=False)
```

```python
import jax
import jax.numpy as jnp
from jax import lax
from jax.experimental import pallas as pl
from jax.experimental.pallas import tpu as pltpu
from jax.sharding import PartitionSpec as P

C = [(0, 0, 0), (1, 0, 0), (-1, 0, 0), (0, 1, 0), (0, -1, 0), (0, 0, 1), (0, 0, -1),
     (1, 1, 0), (-1, -1, 0), (1, -1, 0), (-1, 1, 0), (1, 0, 1), (-1, 0, -1), (1, 0, -1), (-1, 0, 1),
     (0, 1, 1), (0, -1, -1), (0, 1, -1), (0, -1, 1)]
W = [1.0 / 3.0] + [1.0 / 18.0] * 6 + [1.0 / 36.0] * 12
XPOS = [i for i in range(19) if C[i][0] == 1]
XNEG = [i for i in range(19) if C[i][0] == -1]
YPOS = [i for i in range(19) if C[i][1] == 1]
YNEG = [i for i in range(19) if C[i][1] == -1]
RATES = (0.06, 0.08)
VAL = (1.0, -1.0)
N = 16
Z = 256
CHUNK = 4
RING = 6
OFF = 8
ROWS = 7 * N + 8
LINE = 7 * N
F32 = jnp.float32
VM = pltpu.VMEM


def sds(*shape):
    return jax.ShapeDtypeStruct(shape, F32)


def params(mib):
    return pltpu.CompilerParams(vmem_limit_bytes=mib * 1024 * 1024)


def rows():
    return lax.broadcasted_iota(jnp.int32, (N, Z), 0)


def roll_y(v, s):
    return pltpu.roll(v, s % v.shape[0], 0)


def roll_z(v, s):
    return pltpu.roll(v, s % v.shape[1], 1)


def row_of(v, y):
    return v[y:y + 1, :]


def spread(row):
    return jnp.broadcast_to(row, (N, Z))


def shift_up(v):
    return jnp.where(rows() == 0, 0.0, roll_y(v, 1))


def shift_down(v):
    return jnp.where(rows() == N - 1, 0.0, roll_y(v, -1))


def shift_by(v, c):
    return shift_up(v) if c == 1 else shift_down(v) if c == -1 else v


def call(kernel, outs, name, specs, scratch=(), mib=16, flops=0, out_specs=None, moved=0):
    return pl.pallas_call(
        kernel,
        in_specs=[pl.BlockSpec(memory_space={"v": VM, "h": pltpu.HBM, "s": pltpu.SMEM}[c]) for c in specs],
        out_specs=[pl.BlockSpec(memory_space={"v": VM, "h": pltpu.HBM}[c]) for c in out_specs or "v" * len(outs)],
        out_shape=outs,
        scratch_shapes=list(scratch),
        compiler_params=params(mib),
        cost_estimate=pl.CostEstimate(flops=flops, bytes_accessed=moved, transcendentals=0),
        name=name,
    )


def faces_kernel(pot_h, conc_h, mob_h, solid_h, gx_hi, gx_lo, gy_hi, gy_lo, cond, pot, conc, mob, solid, sems):
    pairs = ((pot_h, pot), (conc_h, conc), (mob_h, mob), (solid_h, solid))
    copies = [pltpu.make_async_copy(a, b, sems.at[q]) for q, (a, b) in enumerate(pairs)]
    for c in copies:
        c.start()
    for c in copies:
        c.wait()

    def step(x, carry):
        here = pl.ds(x, 1)
        cond[x] = jnp.where(solid[x] == 0, jnp.sqrt(mob[x]), 0.0)
        for r in range(RING):
            gy_hi[r, here, :] = pot[x, N - 1 - r:N - r, :]
            gy_lo[r, here, :] = pot[x, r:r + 1, :]
        for q, v in ((0, conc.at[0]), (1, conc.at[1]), (2, cond)):
            gy_hi[RING + q, here, :] = v[x, N - 1:N, :]
            gy_lo[RING + q, here, :] = v[x, 0:1, :]
        return carry

    lax.fori_loop(0, N, step, 0, unroll=2)
    for x, face in ((N - 1, gx_hi), (0, gx_lo)):
        for r in range(RING):
            face[r] = pot[abs(x - r)]
        face[RING] = conc[0, x]
        face[RING + 1] = conc[1, x]
        face[RING + 2] = cond[x]


def post_of(p, fluid, q, slopes):
    pull = jnp.where(fluid, q * (-0.001), 0.0)
    force = [pull * d for d in slopes]
    density = p[0]
    for i in range(1, 19):
        density = density + p[i]
    inv = 1.0 / density
    u = []
    for a in range(3):
        total = 0.9 * force[a]
        for i in range(1, 19, 2):
            if C[i][a]:
                term = p[i] - p[i + 1]
                total = total + term if C[i][a] == 1 else total - term
        u.append(total * inv)
    base = 1.0 - 1.5 * (u[0] * u[0] + u[1] * u[1] + u[2] * u[2])
    scaled = density * (10.0 / 9.0)
    out = [jnp.where(fluid, (W[0] * scaled) * base - p[0] * (1.0 / 9.0), p[0])]
    for i in range(1, 19, 2):
        along = None
        for a in range(3):
            if C[i][a]:
                term = u[a] if C[i][a] == 1 else -u[a]
                along = term if along is None else along + term
        even = base + 4.5 * along * along
        odd = 3.0 * along
        ws = W[i] * scaled
        fwd = ws * (even + odd) - p[i] * (1.0 / 9.0)
        bwd = ws * (even - odd) - p[i + 1] * (1.0 / 9.0)
        out.append(jnp.where(fluid, fwd, p[i + 1]))
        out.append(jnp.where(fluid, bwd, p[i]))
    return out, force


def sums(values, keep):
    total = [None] * 4
    for cy in (0, 1, -1):
        part = [None] * 4
        for i, v in values:
            if C[i][1] != cy:
                continue
            for m, c in enumerate((1,) + C[i]):
                if c and m != 2:
                    w = v if c == 1 else -v
                    part[m] = w if part[m] is None else part[m] + w
        for m in (0, 1, 3):
            if part[m] is None:
                continue
            w = part[m] if keep[cy] is None else jnp.where(keep[cy], part[m], 0.0)
            total[m] = w if total[m] is None else total[m] + w
            if m == 0 and cy:
                w = w if cy == 1 else -w
                total[2] = w if total[2] is None else total[2] + w
    return total


def collide_kernel(pops, pot_h, conc_h, cond, buf, mom, px_lo, px_hi, pr_lo, pr_hi, held, pot, conc, sems, psems):
    chunks = [pltpu.make_async_copy(pops.at[:, pl.ds(CHUNK * s, CHUNK)], held.at[:, pl.ds(CHUNK * s, CHUNK)], sems.at[s])
              for s in range(N // CHUNK)]
    ends = [pltpu.make_async_copy(pops.at[:, 0], px_lo, psems.at[0]),
            pltpu.make_async_copy(pops.at[:, N - 1], px_hi, psems.at[1])]
    fields = [pltpu.make_async_copy(pot_h, pot, psems.at[2]), pltpu.make_async_copy(conc_h, conc, psems.at[3])]
    for c in fields + chunks + ends:
        c.start()
    row = rows()
    zero = jnp.zeros((N, Z), F32)
    keep = {0: (row >= 1) & (row <= N - 2), 1: row >= 2, -1: row <= N - 3}
    for m in range(4):
        mom[m, 0] = zero
        mom[m, 1] = zero

    def step(x, carry):
        here = pl.ds(x, 1)
        p = [held[i, x] for i in range(19)]
        for i in range(19):
            pr_lo[i, here, :] = row_of(p[i], 0)
            pr_hi[i, here, :] = row_of(p[i], N - 1)
        centre = pot[x]
        slopes = (pot[x + 1] - pot[x - 1], roll_y(centre, -1) - roll_y(centre, 1), roll_z(centre, -1) - roll_z(centre, 1))
        post, force = post_of(p, cond[x] > 0.0, conc[0, x] - conc[1, x], slopes)
        moved = []
        for i in range(19):
            v = post[i]
            if C[i][2]:
                v = roll_z(v, C[i][2])
            if C[i][1]:
                v = roll_y(v, C[i][1])
            buf[i, x + C[i][0]] = v
            moved.append(v)
        g = sums([(i, moved[i]) for i in range(19) if C[i][0] == 0], keep)
        mom[0, x] += g[0]
        for m in (1, 2, 3):
            w = jnp.where(keep[0], 0.5 * force[m - 1], 0.0)
            mom[m, x] += w if g[m] is None else g[m] + w
        g = sums([(i, moved[i]) for i in XPOS], keep)
        for m in range(4):
            mom[m, x + 1] = g[m]
        g = sums([(i, moved[i]) for i in XNEG], keep)
        for m in range(4):
            mom[m, x - 1] += g[m]
        return carry

    for c in fields:
        c.wait()
    for s in range(N // CHUNK):
        chunks[s].wait()
        lax.fori_loop(max(CHUNK * s, 1), min(CHUNK * s + CHUNK, N - 1), step, 0, unroll=True)
    for c in ends:
        c.wait()


def edge_kernel(px_lo, px_hi, pr_lo, pr_hi, gx_lo, gx_hi, gy_lo, gy_hi, fx_lo, fx_hi, fy_lo, fy_hi, mom0,
                mom, ex_lo, ex_hi, ey_lo, ey_hi, yb_lo, yb_hi):
    row = rows()
    inner = (row >= 1) & (row <= N - 2)
    keep = {0: None, 1: row >= 1, -1: row <= N - 2}
    lines = {}
    for pr, gy, fy, ey, low in ((pr_lo, gy_lo, fy_lo, ey_lo, True), (pr_hi, gy_hi, fy_hi, ey_hi, False)):
        centre = gy[0]
        y_slope = gy[1] - fy[0] if low else fy[0] - gy[1]
        slopes = (roll_y(centre, -1) - roll_y(centre, 1), y_slope, roll_z(centre, -1) - roll_z(centre, 1))
        post, force = post_of([pr[i] for i in range(19)], gy[RING + 2] > 0.0, gy[RING] - gy[RING + 1], slopes)
        for i in range(19):
            v = roll_z(post[i], C[i][2]) if C[i][2] else post[i]
            v = jnp.where(inner, v, 0.0)
            ey[i] = v
            if low and C[i][1] == -1:
                q = YNEG.index(i)
                yb_lo[q * N:(q + 1) * N, :] = v
            if not low and C[i][1] == 1:
                q = YPOS.index(i)
                yb_hi[q * N:(q + 1) * N, :] = v
            post[i] = shift_by(v, C[i][0])
        for cy in (0, 1 if low else -1):
            y = (0 if low else N - 1) + cy
            total = [None] * 4
            for i in range(19):
                if C[i][1] == cy:
                    for m, c in enumerate((1,) + C[i]):
                        if c:
                            w = post[i] if c == 1 else -post[i]
                            total[m] = w if total[m] is None else total[m] + w
            if cy == 0:
                for a in range(3):
                    w = jnp.where(inner, 0.5 * force[a], 0.0)
                    total[a + 1] = w if total[a + 1] is None else total[a + 1] + w
            lines[y] = total
    for x in range(N):
        for m in range(4):
            v = mom0[m, x]
            for y in (0, 1, N - 2, N - 1):
                v = v + jnp.where(row == y, spread(row_of(lines[y][m], x)), 0.0)
            mom[m, x] = v
    for px, gx, fx, ex, low in ((px_lo, gx_lo, fx_lo, ex_lo, True), (px_hi, gx_hi, fx_hi, ex_hi, False)):
        at = 0 if low else N - 1
        centre = gx[0]
        x_slope = gx[1] - fx[0] if low else fx[0] - gx[1]
        y_up = jnp.where(row == N - 1, spread(fy_hi[0, at:at + 1, :]), roll_y(centre, -1))
        y_dn = jnp.where(row == 0, spread(fy_lo[0, at:at + 1, :]), roll_y(centre, 1))
        slopes = (x_slope, y_up - y_dn, roll_z(centre, -1) - roll_z(centre, 1))
        post, force = post_of([px[i] for i in range(19)], gx[RING + 2] > 0.0, gx[RING] - gx[RING + 1], slopes)
        for i in range(19):
            v = roll_z(post[i], C[i][2]) if C[i][2] else post[i]
            if C[i][1] == 1:
                v = roll_y(v, 1)
                at_row = YPOS.index(i) * N + at
                yb_hi[at_row:at_row + 1, :] = row_of(v, 0)
                v = jnp.where(row == 0, 0.0, v)
            elif C[i][1] == -1:
                v = roll_y(v, -1)
                at_row = YNEG.index(i) * N + at
                yb_lo[at_row:at_row + 1, :] = row_of(v, N - 1)
                v = jnp.where(row == N - 1, 0.0, v)
            ex[i] = v
            post[i] = v
        none = {0: None, 1: None, -1: None}
        g = sums([(i, post[i]) for i in range(19) if C[i][0] == 0], none)
        mom[0, at] += g[0]
        for m in (1, 2, 3):
            w = 0.5 * force[m - 1]
            mom[m, at] += w if g[m] is None else g[m] + w
        g = sums([(i, post[i]) for i in (XPOS if low else XNEG)], none)
        for m in range(4):
            mom[m, 1 if low else N - 2] += g[m]
        g = sums([(i, post[i]) for i in (XNEG if low else XPOS)], none)
        k = LINE + (2 if low else 0)
        yb_hi[k:k + 1, :] = row_of(g[0], N - 1)
        yb_hi[k + 1:k + 2, :] = row_of(g[2], N - 1)
        yb_lo[k:k + 1, :] = row_of(g[0], 0)
        yb_lo[k + 1:k + 2, :] = row_of(g[2], 0)
    for x in range(N):
        for q, m in ((5, 0), (6, 2)):
            yb_lo[q * N + x:q * N + x + 1, :] = mom[m, x, 0:1, :]
            yb_hi[q * N + x:q * N + x + 1, :] = mom[m, x, N - 1:N, :]
    yb_lo[LINE + 4:, :] = jnp.zeros((4, Z), F32)
    yb_hi[LINE + 4:, :] = jnp.zeros((4, Z), F32)


def plane(ref, q):
    return ref[q * N:(q + 1) * N, :]


def line(ref, q, x):
    return ref[q * N + x:q * N + x + 1, :]


def y_terms(lo, hi):
    s3, s7, s10, s15, s17 = (plane(lo, q) for q in range(5))
    s7, s10 = shift_up(s7), shift_down(s10)
    total = s3 + s7 + s10 + s15 + s17
    below = (total, s7 - s10, total, s15 - s17)
    s4, s8, s9, s16, s18 = (plane(hi, q) for q in range(5))
    s8, s9 = shift_down(s8), shift_up(s9)
    total = s4 + s8 + s9 + s16 + s18
    return below, (total, s9 - s8, -total, s18 - s16)


def corner_kernel(ex_lo, ex_hi, yh_lo, yh_hi, yb_lo, yb_hi, mom, xb_lo, xb_hi):
    row = rows()
    below, above = y_terms(yh_lo, yh_hi)
    for ex, xb, slots, at in ((ex_hi, xb_hi, XPOS, N - 1), (ex_lo, xb_lo, XNEG, 0)):
        for q, i in enumerate(slots):
            v = ex[i]
            if C[i][1] == 1:
                v = jnp.where(row == 0, spread(line(yh_lo, YPOS.index(i), at)), v)
            elif C[i][1] == -1:
                v = jnp.where(row == N - 1, spread(line(yh_hi, YNEG.index(i), at)), v)
            xb[q * N:(q + 1) * N, :] = v
        for q, m in ((5, 0), (6, 1)):
            v = mom[m, at] + jnp.where(row == 0, spread(row_of(below[m], at)), 0.0)
            xb[q * N:(q + 1) * N, :] = v + jnp.where(row == N - 1, spread(row_of(above[m], at)), 0.0)
        c = 1 if at else -1
        k = LINE if at else LINE + 2
        down = line(yb_lo, YNEG.index(9 if c == 1 else 8), at)
        up = line(yb_hi, YPOS.index(7 if c == 1 else 10), at)
        xb[LINE:LINE + 1, :] = yh_lo[k:k + 1, :] + down
        xb[LINE + 1:LINE + 2, :] = yh_lo[k + 1:k + 2, :] - down
        xb[LINE + 2:LINE + 3, :] = yh_hi[k:k + 1, :] + up
        xb[LINE + 3:LINE + 4, :] = yh_hi[k + 1:k + 2, :] + up
        xb[LINE + 4:, :] = jnp.zeros((4, Z), F32)


def transport_kernel(mom, cond, base, wx, wy, wy_low, wz, wall, yh_lo, yh_hi, xh_lo, xh_hi, yb_lo, yb_hi, xb_lo, xb_hi,
                     fx_lo, fx_hi, fy_lo, fy_hi, conc_out, src, sy_lo, sy_hi, drift, lines, low, dy_hi, own_dy):
    row = rows()
    below, above = y_terms(yh_lo, yh_hi)
    for m in range(4):
        lines[m] = below[m]
        lines[4 + m] = above[m]

    def step(x, extra):
        here = pl.ds(x, 1)

        def full(m):
            v = mom[m, x]
            if extra is not None:
                v = v + extra[m]
            v = v + jnp.where(row == 0, spread(lines[m, here, :]), 0.0)
            return v + jnp.where(row == N - 1, spread(lines[4 + m, here, :]), 0.0)

        scale = jnp.where(cond[x] > 0.0, 1.0 / full(0), 0.0)
        drift[0, x] = full(1) * scale
        v = full(2) * scale
        drift[1, x] = v
        drift[2, x] = full(3) * scale
        own_dy[here, :] = row_of(v, 0)

    a = [plane(xh_lo, q) for q in range(5)]
    total = a[0] + a[1] + a[2] + a[3] + a[4]
    step(0, (total, total, a[1] - a[2], a[3] - a[4]))
    b = [plane(xh_hi, q) for q in range(5)]
    total = b[0] + b[1] + b[2] + b[3] + b[4]
    step(N - 1, (total, -total, b[2] - b[1], b[4] - b[3]))

    def loop(x, carry):
        step(x, None)
        return carry

    lax.fori_loop(1, N - 1, loop, 0, unroll=2)

    def velocity(conductance, density, momentum):
        return jnp.where(conductance > 0.0, momentum / density, 0.0)

    def x_face(fx, xh, xb, sign):
        out = plane(xb, 0) + plane(xb, 1) + plane(xb, 2) + plane(xb, 3) + plane(xb, 4)
        return velocity(fx[RING + 2], plane(xh, 5) + out, plane(xh, 6) + sign * out)

    from_hi, from_lo = y_terms(yb_hi, yb_lo)

    def y_face(fy, yh, terms, k):
        density = plane(yh, 5) + terms[0]
        momentum = plane(yh, 6) + terms[2]
        for xh, x in ((xh_lo, 0), (xh_hi, N - 1)):
            density = density + jnp.where(row == x, spread(xh[k:k + 1, :]), 0.0)
            momentum = momentum + jnp.where(row == x, spread(xh[k + 1:k + 2, :]), 0.0)
        return velocity(fy[RING + 2], density, momentum)

    carried = y_face(fy_lo, yh_lo, from_lo, LINE) + own_dy[...]
    for s in range(2):
        low[s] = wy_low[s] * carried
    dy_hi[...] = y_face(fy_hi, yh_hi, from_hi, LINE + 2)
    carried = x_face(fx_lo, xh_lo, xb_lo, -1.0) + drift[0, 0]
    behind = [wx[s, 0] * carried for s in range(2)]
    last = x_face(fx_hi, xh_hi, xb_hi, 1.0)
    for x in range(N):
        carried = drift[0, x] + (drift[0, x + 1] if x < N - 1 else last)
        ahead = [wx[s, x + 1] * carried for s in range(2)]
        tot = [ahead[s] - behind[s] for s in range(2)]
        behind = ahead
        v = drift[1, x]
        carried = v + jnp.where(row == N - 1, spread(dy_hi[x:x + 1, :]), roll_y(v, -1))
        for s in range(2):
            f = wy[s, x] * carried
            tot[s] = tot[s] + (f - jnp.where(row == 0, spread(low[s, x:x + 1, :]), roll_y(f, 1)))
        v = drift[2, x]
        carried = v + roll_z(v, -1)
        for s in range(2):
            f = wz[s, x] * carried
            tot[s] = tot[s] + (f - roll_z(f, 1))
        c0 = base[0, x] - tot[0]
        c1 = base[1, x] - tot[1]
        conc_out[0, x] = c0
        conc_out[1, x] = c1
        s_val = jnp.where(cond[x] > 0.0, c0 - c1, wall[x])
        src[x] = s_val
        for r in range(RING - 1):
            sy_lo[r, x:x + 1, :] = row_of(s_val, r)
            sy_hi[r, x:x + 1, :] = row_of(s_val, N - 1 - r)


def split(ext, a, b, pairs, shift):
    shape = (N + 2 * OFF, Z)
    mask = (lax.broadcasted_iota(jnp.int32, shape, 0) + lax.broadcasted_iota(jnp.int32, shape, 1)) % 2 == 0
    for k in pairs:
        p, q = ext[2 * k], ext[2 * k + 1]
        a[k + shift] = jnp.where(mask, p, q)
        b[k + shift] = jnp.where(mask, q, p)


def prepare_kernel(pot, src, fy_lo, fy_hi, ys_lo, ys_hi, even, odd, s_even, s_odd, ext):
    for centre, y_lo, y_hi, depth, a, b in ((pot, fy_lo, fy_hi, RING, even, odd), (src, ys_lo, ys_hi, RING - 1, s_even, s_odd)):
        for x in range(N):
            ext[x, OFF:OFF + N] = centre[x]
            for r in range(depth):
                ext[x, OFF - 1 - r:OFF - r, :] = y_lo[r, x:x + 1, :]
                ext[x, OFF + N + r:OFF + N + r + 1, :] = y_hi[r, x:x + 1, :]
        split(ext, a, b, range(N // 2), 0)


def sweep_kernel(even_in, odd_in, s_even_in, s_odd_in, fx_lo, fx_hi, xs_lo, xs_hi, out, ext, even, odd, s_even, s_odd):
    mid = slice(OFF, OFF + N)
    top = RING + N
    half = (N + 2 * RING) // 2
    shape = (N + 2 * OFF, Z)
    mask = (lax.broadcasted_iota(jnp.int32, shape, 0) + lax.broadcasted_iota(jnp.int32, shape, 1)) % 2 == 0
    zero = jnp.zeros(shape, F32)
    for ref in (even, odd):
        ref[0] = zero
        ref[half + 1] = zero
    for ref, given in ((even, even_in), (odd, odd_in), (s_even, s_even_in), (s_odd, s_odd_in)):
        for k in range(N // 2):
            ref[k + 1 + RING // 2] = given[k]
    ends = list(range(RING // 2)) + list(range(RING // 2 + N // 2, half))
    for x_lo, x_hi, depth, listed, a, b in (
            (lambda r: fx_lo[r], lambda r: fx_hi[r], RING, POT_ROWS, even, odd),
            (lambda r: plane(xs_lo, r), lambda r: plane(xs_hi, r), RING - 1, SRC_ROWS, s_even, s_odd)):
        for r in range(depth):
            ext[RING - 1 - r, mid] = x_lo(r)
            ext[top + r, mid] = x_hi(r)
        for at, a_ring, side, b_ring in listed:
            y = OFF + N + b_ring - 1 if side else OFF - b_ring
            ext[RING - a_ring, y:y + 1, :] = xs_lo[at:at + 1, :]
            ext[top + a_ring - 1, y:y + 1, :] = xs_hi[at:at + 1, :]
        split(ext, a, b, ends, 1)

    for h in range(6):
        this, other, s = (even, odd, s_even) if h % 2 == 0 else (odd, even, s_odd)

        def update(k, carry, h=h, this=this, other=other, s=s):
            c = other[k]
            before, after = other[k - 1], other[k + 1]
            far = jnp.where(mask, before, after) if h % 2 == 0 else jnp.where(mask, after, before)
            nb = (c + far) + (roll_y(c, 1) + roll_y(c, -1)) + (roll_z(c, 1) + roll_z(c, -1))
            this[k] = -0.6 * this[k] + (1.6 / 6.0) * (nb + s[k])
            return carry

        lo = (h + 1) // 2
        for k in range(lo + 1, half - lo + 1):
            update(k, 0)

    def last(k, carry):
        p, q = even[k], odd[k]
        out[2 * (k - 1) - RING] = jnp.where(mask, p, q)[OFF:OFF + N]
        out[2 * (k - 1) - RING + 1] = jnp.where(mask, q, p)[OFF:OFF + N]
        return carry

    lax.fori_loop(RING // 2 + 1, RING // 2 + N // 2 + 1, last, 0)


def patch_kernel(buf, ex_lo, ex_hi, ey_lo, ey_hi, yh_lo, yh_hi, xh_lo, xh_hi, out, done, sems):
    row = rows()
    copies = []
    for i in range(19):
        cx, cy, _ = C[i]

        def halo(v, src, i=i, cy=cy):
            if cy == 1:
                return jnp.where(row == 0, spread(yh_lo[pl.ds(YPOS.index(i) * N + src, 1), :]), v)
            if cy == -1:
                return jnp.where(row == N - 1, spread(yh_hi[pl.ds(YNEG.index(i) * N + src, 1), :]), v)
            return v

        def inner(src, carry, i=i, cx=cx, cy=cy, halo=halo):
            here = pl.ds(src, 1)
            v = buf[i, src + cx]
            if cy != -1:
                v = jnp.where(row == cy, spread(ey_lo[i, here, :]), v)
            if cy != 1:
                v = jnp.where(row == N - 1 + cy, spread(ey_hi[i, here, :]), v)
            done[i, src + cx] = halo(v, src)
            return carry

        lax.fori_loop(1, N - 1, inner, 0, unroll=2)
        if cx != -1:
            done[i, cx] = halo(ex_lo[i], 0)
        if cx != 1:
            done[i, N - 1 + cx] = halo(ex_hi[i], N - 1)
        if cx == 1:
            done[i, 0] = plane(xh_lo, XPOS.index(i))
        if cx == -1:
            done[i, N - 1] = plane(xh_hi, XNEG.index(i))
        copy = pltpu.make_async_copy(done.at[i], out.at[i], sems.at[i])
        copy.start()
        copies.append(copy)
    for copy in copies:
        copy.wait()


def flux(a, b):
    link = a[2] * b[2]
    drop = a[3] - b[3]
    rest, weight = [], []
    for s in range(2):
        both = a[s] + b[s]
        rest.append(link * (RATES[s] * ((a[s] - b[s]) + ((0.5 * VAL[s]) * both) * drop)))
        weight.append((0.25 * link) * both)
    return rest, weight


def diffuse_kernel(charge, classes_h, cond, conc, pot, fx_lo, fx_hi, fy_lo, fy_hi, gy_lo,
                   base, wx, wy, wy_low, wz, wall, low, classes, sem):
    fetch = pltpu.make_async_copy(classes_h, classes, sem)
    fetch.start()
    row = rows()

    def faces(ref):
        return tuple(ref[RING + q] for q in range(3)) + (ref[0],)

    rest, weight = flux(faces(fy_lo), faces(gy_lo))
    for s in range(2):
        low[s] = rest[s]
        wy_low[s] = weight[s]
    upper = faces(fy_hi)

    def fields(x):
        return (conc[0, x], conc[1, x], cond[x], pot[x])

    behind, weight = flux(faces(fx_lo), fields(0))
    for s in range(2):
        wx[s, 0] = weight[s]
    fetch.wait()
    for x in range(N):
        me = fields(x)
        ahead, weight = flux(me, fields(x + 1) if x < N - 1 else faces(fx_hi))
        tot = [ahead[s] - behind[s] for s in range(2)]
        behind = ahead
        for s in range(2):
            wx[s, x + 1] = weight[s]
        nxt = tuple(jnp.where(row == N - 1, spread(row_of(upper[q], x)), roll_y(me[q], -1)) for q in range(4))
        rest, weight = flux(me, nxt)
        for s in range(2):
            wy[s, x] = weight[s]
            tot[s] = tot[s] + (rest[s] - jnp.where(row == 0, spread(low[s, x:x + 1, :]), roll_y(rest[s], 1)))
        rest, weight = flux(me, tuple(roll_z(v, -1) for v in me))
        for s in range(2):
            wz[s, x] = weight[s]
            tot[s] = tot[s] + (rest[s] - roll_z(rest[s], 1))
            base[s, x] = me[s] - tot[s]
        cls = classes[x]
        total = jnp.zeros((N, Z), F32)
        for q in range(4):
            total = total + jnp.where(cls == q, charge[q], 0.0)
        wall[x] = total


def ring_rows(depth, total):
    listed = []
    at = depth
    for a in range(1, total):
        for side in (0, 1):
            for b in range(1, total - a + 1):
                listed.append((at, a, side, b))
                at += 1
    return listed


SRC_ROWS = ring_rows((RING - 1) * N, RING - 1)
POT_ROWS = ring_rows(SRC_ROWS[-1][0] + 1, RING)
SRC_LEN = 136


def pack_src_kernel(src, ys_lo, ys_hi, fy_lo, fy_hi, o_hi, o_lo):
    for k in range(RING - 1):
        o_hi[k * N:(k + 1) * N, :] = src[N - 1 - k]
        o_lo[k * N:(k + 1) * N, :] = src[k]
    for listed, lo, hi in ((SRC_ROWS, ys_lo, ys_hi), (POT_ROWS, fy_lo, fy_hi)):
        for at, a, side, b in listed:
            halo = hi if side else lo
            o_hi[at:at + 1, :] = halo[b - 1, N - a:N - a + 1, :]
            o_lo[at:at + 1, :] = halo[b - 1, a - 1:a, :]
    end = POT_ROWS[-1][0] + 1
    o_hi[end:, :] = jnp.zeros((SRC_LEN - end, Z), F32)
    o_lo[end:, :] = jnp.zeros((SRC_LEN - end, Z), F32)


def swap(axis, hi, lo):
    n = lax.axis_size(axis)
    even = lax.axis_index(axis) % 2 == 0
    first = lax.ppermute(jnp.where(even, hi, lo), axis, [(i, i + 1 - 2 * (i % 2)) for i in range(n)])
    second = lax.ppermute(jnp.where(even, lo, hi), axis, [(i, (i - 1 + 2 * (i % 2)) % n) for i in range(n)])
    return jnp.where(even, second, first), jnp.where(even, first, second)


def body(pops, conc, pot, mob, solid, classes, charge):
    cube = sds(N, N, Z)
    msg = sds(ROWS, Z)
    gx_hi, gx_lo, gy_hi, gy_lo, cond = call(
        faces_kernel, [sds(RING + 3, N, Z)] * 4 + [cube], "faces", "hhhh",
        scratch=[VM((N, N, Z), F32), VM((2, N, N, Z), F32), VM((N, N, Z), F32), VM((N, N, Z), jnp.int32),
                 pltpu.SemaphoreType.DMA((4,))], mib=53, moved=2600000)(
        pot, conc, mob, solid)
    fx_lo, fx_hi = swap("gx", gx_hi, gx_lo)
    fy_lo, fy_hi = swap("gy", gy_hi, gy_lo)
    chunks = N // CHUNK
    buf, mom, px_lo, px_hi, pr_lo, pr_hi = call(
        collide_kernel, [sds(19, N, N, Z), sds(4, N, N, Z)] + [sds(19, N, Z)] * 4, "collide", "hhhv",
        scratch=[VM((19, N, N, Z), F32), VM((N, N, Z), F32), VM((2, N, N, Z), F32),
                 pltpu.SemaphoreType.DMA((chunks,)), pltpu.SemaphoreType.DMA((4,))],
        mib=43, flops=20000000, moved=14000000)(pops, pot, conc, cond)
    mom, ex_lo, ex_hi, ey_lo, ey_hi, yb_lo, yb_hi = call(
        edge_kernel, [sds(4, N, N, Z)] + [sds(19, N, Z)] * 4 + [msg, msg], "edge", "v" * 13, moved=3000000)(
        px_lo, px_hi, pr_lo, pr_hi, gx_lo, gx_hi, gy_lo, gy_hi, fx_lo, fx_hi, fy_lo, fy_hi, mom)
    yh_lo, yh_hi = swap("gy", yb_hi, yb_lo)
    xb_lo, xb_hi = call(corner_kernel, [msg, msg], "corner", "v" * 7)(ex_lo, ex_hi, yh_lo, yh_hi, yb_lo, yb_hi, mom)
    xh_lo, xh_hi = swap("gx", xb_hi, xb_lo)
    face = VM((N, Z), F32)
    fy_late, _ = lax.optimization_barrier((fy_lo, yh_lo))
    pair = sds(2, N, N, Z)
    base, wx, wy, wy_low, wz, wall = call(
        diffuse_kernel, [pair, sds(2, N + 1, N, Z), pair, sds(2, N, Z), pair, cube], "diffuse", "sh" + "v" * 8,
        scratch=[VM((2, N, Z), F32), VM((N, N, Z), jnp.int32), pltpu.SemaphoreType.DMA], flops=10000000, moved=6000000)(
        charge, classes, cond, conc, pot, fx_lo, fx_hi, fy_late, fy_hi, gy_lo)
    conc_out, src, sy_lo, sy_hi = call(
        transport_kernel, [pair, cube, sds(RING - 1, N, Z), sds(RING - 1, N, Z)], "transport", "v" * 20,
        scratch=[VM((3, N, N, Z), F32), VM((8, N, Z), F32), VM((2, N, Z), F32), face, face], flops=5000000, moved=4000000)(
        mom, cond, base, wx, wy, wy_low, wz, wall, yh_lo, yh_hi, xh_lo, xh_hi, yb_lo, yb_hi, xb_lo, xb_hi,
        fx_lo, fx_hi, fy_lo, fy_hi)
    ys_lo, ys_hi = swap("gy", sy_hi, sy_lo)
    bs_hi, bs_lo = call(pack_src_kernel, [sds(SRC_LEN, Z)] * 2, "pack_src", "v" * 5)(src, ys_lo, ys_hi, fy_lo, fy_hi)
    xs_lo, xs_hi = swap("gx", bs_hi, bs_lo)
    packed = VM(((N + 2 * RING) // 2 + 2, N + 2 * OFF, Z), F32)
    prepared = call(
        prepare_kernel, [sds(N // 2, N + 2 * OFF, Z)] * 4, "prepare", "v" * 6,
        scratch=[VM((N, N + 2 * OFF, Z), F32)], flops=1000000, moved=4000000)(pot, src, fy_lo, fy_hi, ys_lo, ys_hi)
    potential_out = call(
        sweep_kernel, [cube], "sweep", "v" * 8,
        scratch=[VM((N + 2 * RING, N + 2 * OFF, Z), F32)] + [packed] * 4, flops=20000000, moved=4000000)(
        *prepared, fx_lo, fx_hi, xs_lo, xs_hi)[0]
    pop = call(
        patch_kernel, [sds(19, N, N, Z)], "patch", "v" * 9, out_specs="h",
        scratch=[VM((19, N, N, Z), F32), pltpu.SemaphoreType.DMA((19,))], mib=16, moved=10000000)(
        buf, ex_lo, ex_hi, ey_lo, ey_hi, yh_lo, yh_hi, xh_lo, xh_hi)[0]
    return (pop, conc_out, potential_out)


def solution(mesh):
    lattice = P(None, "gx", "gy", None)
    flat = P("gx", "gy", None)
    return jax.shard_map(
        body, mesh=mesh, in_specs=(lattice, lattice, flat, flat, flat, flat, P()),
        out_specs=(lattice, lattice, flat), check_vma=False)
```

```python
import jax
import jax.numpy as jnp
from jax import lax
from jax.experimental import pallas as pl
from jax.experimental.pallas import tpu as pltpu
from jax.sharding import PartitionSpec as P

C = [(0, 0, 0), (1, 0, 0), (-1, 0, 0), (0, 1, 0), (0, -1, 0), (0, 0, 1), (0, 0, -1),
     (1, 1, 0), (-1, -1, 0), (1, -1, 0), (-1, 1, 0), (1, 0, 1), (-1, 0, -1), (1, 0, -1), (-1, 0, 1),
     (0, 1, 1), (0, -1, -1), (0, 1, -1), (0, -1, 1)]
W = [1.0 / 3.0] + [1.0 / 18.0] * 6 + [1.0 / 36.0] * 12
XPOS = [i for i in range(19) if C[i][0] == 1]
XNEG = [i for i in range(19) if C[i][0] == -1]
YPOS = [i for i in range(19) if C[i][1] == 1]
YNEG = [i for i in range(19) if C[i][1] == -1]
RATES = (0.06, 0.08)
VAL = (1.0, -1.0)
N = 16
Z = 256
CHUNK = 4
RING = 6
OFF = 8
ROWS = 7 * N + 8
LINE = 7 * N
F32 = jnp.float32
VM = pltpu.VMEM


def sds(*shape):
    return jax.ShapeDtypeStruct(shape, F32)


def params(mib):
    return pltpu.CompilerParams(vmem_limit_bytes=mib * 1024 * 1024)


def rows():
    return lax.broadcasted_iota(jnp.int32, (N, Z), 0)


def roll_y(v, s):
    return pltpu.roll(v, s % v.shape[0], 0)


def roll_z(v, s):
    return pltpu.roll(v, s % v.shape[1], 1)


def row_of(v, y):
    return v[y:y + 1, :]


def spread(row):
    return jnp.broadcast_to(row, (N, Z))


def shift_up(v):
    return jnp.where(rows() == 0, 0.0, roll_y(v, 1))


def shift_down(v):
    return jnp.where(rows() == N - 1, 0.0, roll_y(v, -1))


def shift_by(v, c):
    return shift_up(v) if c == 1 else shift_down(v) if c == -1 else v


def call(kernel, outs, name, specs, scratch=(), mib=16, flops=0, out_specs=None, moved=0):
    return pl.pallas_call(
        kernel,
        in_specs=[pl.BlockSpec(memory_space={"v": VM, "h": pltpu.HBM, "s": pltpu.SMEM}[c]) for c in specs],
        out_specs=[pl.BlockSpec(memory_space={"v": VM, "h": pltpu.HBM}[c]) for c in out_specs or "v" * len(outs)],
        out_shape=outs,
        scratch_shapes=list(scratch),
        compiler_params=params(mib),
        cost_estimate=pl.CostEstimate(flops=flops, bytes_accessed=moved, transcendentals=0),
        name=name,
    )


def faces_kernel(pot_h, conc_h, mob_h, solid_h, gx_hi, gx_lo, gy_hi, gy_lo, cond, pot, conc, mob, solid, sems):
    pairs = ((pot_h, pot), (conc_h, conc), (mob_h, mob), (solid_h, solid))
    copies = [pltpu.make_async_copy(a, b, sems.at[q]) for q, (a, b) in enumerate(pairs)]
    for c in copies:
        c.start()
    for c in copies:
        c.wait()

    def step(x, carry):
        here = pl.ds(x, 1)
        cond[x] = jnp.where(solid[x] == 0, jnp.sqrt(mob[x]), 0.0)
        for r in range(RING):
            gy_hi[r, here, :] = pot[x, N - 1 - r:N - r, :]
            gy_lo[r, here, :] = pot[x, r:r + 1, :]
        for q, v in ((0, conc.at[0]), (1, conc.at[1]), (2, cond)):
            gy_hi[RING + q, here, :] = v[x, N - 1:N, :]
            gy_lo[RING + q, here, :] = v[x, 0:1, :]
        return carry

    lax.fori_loop(0, N, step, 0, unroll=True)
    for x, face in ((N - 1, gx_hi), (0, gx_lo)):
        for r in range(RING):
            face[r] = pot[abs(x - r)]
        face[RING] = conc[0, x]
        face[RING + 1] = conc[1, x]
        face[RING + 2] = cond[x]


def post_of(p, fluid, q, slopes):
    pull = jnp.where(fluid, q * (-0.001), 0.0)
    force = [pull * d for d in slopes]
    density = p[0]
    for i in range(1, 19):
        density = density + p[i]
    inv = 1.0 / density
    u = []
    for a in range(3):
        total = 0.9 * force[a]
        for i in range(1, 19, 2):
            if C[i][a]:
                term = p[i] - p[i + 1]
                total = total + term if C[i][a] == 1 else total - term
        u.append(total * inv)
    base = 1.0 - 1.5 * (u[0] * u[0] + u[1] * u[1] + u[2] * u[2])
    scaled = density * (10.0 / 9.0)
    out = [jnp.where(fluid, (W[0] * scaled) * base - p[0] * (1.0 / 9.0), p[0])]
    for i in range(1, 19, 2):
        along = None
        for a in range(3):
            if C[i][a]:
                term = u[a] if C[i][a] == 1 else -u[a]
                along = term if along is None else along + term
        even = base + 4.5 * along * along
        odd = 3.0 * along
        ws = W[i] * scaled
        fwd = ws * (even + odd) - p[i] * (1.0 / 9.0)
        bwd = ws * (even - odd) - p[i + 1] * (1.0 / 9.0)
        out.append(jnp.where(fluid, fwd, p[i + 1]))
        out.append(jnp.where(fluid, bwd, p[i]))
    return out, force


def sums(values, keep):
    total = [None] * 4
    for cy in (0, 1, -1):
        part = [None] * 4
        for i, v in values:
            if C[i][1] != cy:
                continue
            for m, c in enumerate((1,) + C[i]):
                if c and m != 2:
                    w = v if c == 1 else -v
                    part[m] = w if part[m] is None else part[m] + w
        for m in (0, 1, 3):
            if part[m] is None:
                continue
            w = part[m] if keep[cy] is None else jnp.where(keep[cy], part[m], 0.0)
            total[m] = w if total[m] is None else total[m] + w
            if m == 0 and cy:
                w = w if cy == 1 else -w
                total[2] = w if total[2] is None else total[2] + w
    return total


def collide_kernel(pops, pot_h, conc_h, cond, buf, mom, px_lo, px_hi, pr_lo, pr_hi, held, pot, conc, sems, psems):
    chunks = [pltpu.make_async_copy(pops.at[:, pl.ds(CHUNK * s, CHUNK)], held.at[:, pl.ds(CHUNK * s, CHUNK)], sems.at[s])
              for s in range(N // CHUNK)]
    ends = [pltpu.make_async_copy(pops.at[:, 0], px_lo, psems.at[0]),
            pltpu.make_async_copy(pops.at[:, N - 1], px_hi, psems.at[1])]
    fields = [pltpu.make_async_copy(pot_h, pot, psems.at[2]), pltpu.make_async_copy(conc_h, conc, psems.at[3])]
    for c in fields + chunks + ends:
        c.start()
    row = rows()
    zero = jnp.zeros((N, Z), F32)
    keep = {0: (row >= 1) & (row <= N - 2), 1: row >= 2, -1: row <= N - 3}
    for m in range(4):
        mom[m, 0] = zero
        mom[m, 1] = zero

    def step(x, carry):
        here = pl.ds(x, 1)
        p = [held[i, x] for i in range(19)]
        for i in range(19):
            pr_lo[i, here, :] = row_of(p[i], 0)
            pr_hi[i, here, :] = row_of(p[i], N - 1)
        centre = pot[x]
        slopes = (pot[x + 1] - pot[x - 1], roll_y(centre, -1) - roll_y(centre, 1), roll_z(centre, -1) - roll_z(centre, 1))
        post, force = post_of(p, cond[x] > 0.0, conc[0, x] - conc[1, x], slopes)
        moved = []
        for i in range(19):
            v = post[i]
            if C[i][2]:
                v = roll_z(v, C[i][2])
            if C[i][1]:
                v = roll_y(v, C[i][1])
            buf[i, x + C[i][0]] = v
            moved.append(v)
        g = sums([(i, moved[i]) for i in range(19) if C[i][0] == 0], keep)
        mom[0, x] += g[0]
        for m in (1, 2, 3):
            w = jnp.where(keep[0], 0.5 * force[m - 1], 0.0)
            mom[m, x] += w if g[m] is None else g[m] + w
        g = sums([(i, moved[i]) for i in XPOS], keep)
        for m in range(4):
            mom[m, x + 1] = g[m]
        g = sums([(i, moved[i]) for i in XNEG], keep)
        for m in range(4):
            mom[m, x - 1] += g[m]
        return carry

    for c in fields:
        c.wait()
    for s in range(N // CHUNK):
        chunks[s].wait()
        lax.fori_loop(max(CHUNK * s, 1), min(CHUNK * s + CHUNK, N - 1), step, 0, unroll=True)
    for c in ends:
        c.wait()


def edge_kernel(px_lo, px_hi, pr_lo, pr_hi, gx_lo, gx_hi, gy_lo, gy_hi, fx_lo, fx_hi, fy_lo, fy_hi, mom0,
                mom, ex_lo, ex_hi, ey_lo, ey_hi, yb_lo, yb_hi, xb_lo, xb_hi):
    row = rows()
    inner = (row >= 1) & (row <= N - 2)
    keep = {0: None, 1: row >= 1, -1: row <= N - 2}
    lines = {}
    for pr, gy, fy, ey, low in ((pr_lo, gy_lo, fy_lo, ey_lo, True), (pr_hi, gy_hi, fy_hi, ey_hi, False)):
        centre = gy[0]
        y_slope = gy[1] - fy[0] if low else fy[0] - gy[1]
        slopes = (roll_y(centre, -1) - roll_y(centre, 1), y_slope, roll_z(centre, -1) - roll_z(centre, 1))
        post, force = post_of([pr[i] for i in range(19)], gy[RING + 2] > 0.0, gy[RING] - gy[RING + 1], slopes)
        for i in range(19):
            v = roll_z(post[i], C[i][2]) if C[i][2] else post[i]
            v = jnp.where(inner, v, 0.0)
            ey[i] = v
            if low and C[i][1] == -1:
                q = YNEG.index(i)
                yb_lo[q * N:(q + 1) * N, :] = v
            if not low and C[i][1] == 1:
                q = YPOS.index(i)
                yb_hi[q * N:(q + 1) * N, :] = v
            post[i] = shift_by(v, C[i][0])
        for cy in (0, 1 if low else -1):
            y = (0 if low else N - 1) + cy
            total = [None] * 4
            for i in range(19):
                if C[i][1] == cy:
                    for m, c in enumerate((1,) + C[i]):
                        if c:
                            w = post[i] if c == 1 else -post[i]
                            total[m] = w if total[m] is None else total[m] + w
            if cy == 0:
                for a in range(3):
                    w = jnp.where(inner, 0.5 * force[a], 0.0)
                    total[a + 1] = w if total[a + 1] is None else total[a + 1] + w
            lines[y] = total
    for x in range(N):
        for m in range(4):
            v = mom0[m, x]
            for y in (0, 1, N - 2, N - 1):
                v = v + jnp.where(row == y, spread(row_of(lines[y][m], x)), 0.0)
            mom[m, x] = v
    for px, gx, fx, ex, low in ((px_lo, gx_lo, fx_lo, ex_lo, True), (px_hi, gx_hi, fx_hi, ex_hi, False)):
        at = 0 if low else N - 1
        centre = gx[0]
        x_slope = gx[1] - fx[0] if low else fx[0] - gx[1]
        y_up = jnp.where(row == N - 1, spread(fy_hi[0, at:at + 1, :]), roll_y(centre, -1))
        y_dn = jnp.where(row == 0, spread(fy_lo[0, at:at + 1, :]), roll_y(centre, 1))
        slopes = (x_slope, y_up - y_dn, roll_z(centre, -1) - roll_z(centre, 1))
        post, force = post_of([px[i] for i in range(19)], gx[RING + 2] > 0.0, gx[RING] - gx[RING + 1], slopes)
        for i in range(19):
            v = roll_z(post[i], C[i][2]) if C[i][2] else post[i]
            if C[i][1] == 1:
                v = roll_y(v, 1)
                at_row = YPOS.index(i) * N + at
                yb_hi[at_row:at_row + 1, :] = row_of(v, 0)
                v = jnp.where(row == 0, 0.0, v)
            elif C[i][1] == -1:
                v = roll_y(v, -1)
                at_row = YNEG.index(i) * N + at
                yb_lo[at_row:at_row + 1, :] = row_of(v, N - 1)
                v = jnp.where(row == N - 1, 0.0, v)
            ex[i] = v
            post[i] = v
        none = {0: None, 1: None, -1: None}
        g = sums([(i, post[i]) for i in range(19) if C[i][0] == 0], none)
        mom[0, at] += g[0]
        for m in (1, 2, 3):
            w = 0.5 * force[m - 1]
            mom[m, at] += w if g[m] is None else g[m] + w
        g = sums([(i, post[i]) for i in (XPOS if low else XNEG)], none)
        for m in range(4):
            mom[m, 1 if low else N - 2] += g[m]
        g = sums([(i, post[i]) for i in (XNEG if low else XPOS)], none)
        k = LINE + (2 if low else 0)
        yb_hi[k:k + 1, :] = row_of(g[0], N - 1)
        yb_hi[k + 1:k + 2, :] = row_of(g[2], N - 1)
        yb_lo[k:k + 1, :] = row_of(g[0], 0)
        yb_lo[k + 1:k + 2, :] = row_of(g[2], 0)
    for ex, xb, slots, at in ((ex_hi, xb_hi, XPOS, N - 1), (ex_lo, xb_lo, XNEG, 0)):
        for q, i in enumerate(slots):
            xb[q * N:(q + 1) * N, :] = ex[i]
        for q, m in ((5, 0), (6, 1)):
            xb[q * N:(q + 1) * N, :] = mom[m, at]
    for x in range(N):
        for q, m in ((5, 0), (6, 2)):
            yb_lo[q * N + x:q * N + x + 1, :] = mom[m, x, 0:1, :]
            yb_hi[q * N + x:q * N + x + 1, :] = mom[m, x, N - 1:N, :]
    yb_lo[LINE + 4:, :] = jnp.zeros((4, Z), F32)
    yb_hi[LINE + 4:, :] = jnp.zeros((4, Z), F32)


def plane(ref, q):
    return ref[q * N:(q + 1) * N, :]


def line(ref, q, x):
    return ref[q * N + x:q * N + x + 1, :]


def y_terms(lo, hi):
    s3, s7, s10, s15, s17 = (plane(lo, q) for q in range(5))
    s7, s10 = shift_up(s7), shift_down(s10)
    total = s3 + s7 + s10 + s15 + s17
    below = (total, s7 - s10, total, s15 - s17)
    s4, s8, s9, s16, s18 = (plane(hi, q) for q in range(5))
    s8, s9 = shift_down(s8), shift_up(s9)
    total = s4 + s8 + s9 + s16 + s18
    return below, (total, s9 - s8, -total, s18 - s16)


def corner_kernel(yh_lo, yh_hi, yb_lo, yb_hi, xl_lo, xl_hi):
    below, above = y_terms(yh_lo, yh_hi)
    for xl, at, up_slot, down_slot in ((xl_hi, N - 1, 7, 9), (xl_lo, 0, 10, 8)):
        k = LINE if at else LINE + 2
        down = line(yb_lo, YNEG.index(down_slot), at)
        up = line(yb_hi, YPOS.index(up_slot), at)
        listed = (line(yh_lo, YPOS.index(up_slot), at), line(yh_hi, YNEG.index(down_slot), at),
                  row_of(below[0], at), row_of(above[0], at), row_of(below[1], at), row_of(above[1], at),
                  yh_lo[k:k + 1, :] + down, yh_lo[k + 1:k + 2, :] - down, yh_hi[k:k + 1, :] + up, yh_hi[k + 1:k + 2, :] + up)
        for q, v in enumerate(listed):
            xl[q:q + 1, :] = v
        xl[len(listed):, :] = jnp.zeros((N - len(listed), Z), F32)


def with_lines(v, xl, i):
    if C[i][1] == 1:
        return jnp.where(rows() == 0, spread(xl[0:1, :]), v)
    if C[i][1] == -1:
        return jnp.where(rows() == N - 1, spread(xl[1:2, :]), v)
    return v


def plus_lines(v, low, high):
    v = v + jnp.where(rows() == 0, spread(low), 0.0)
    return v + jnp.where(rows() == N - 1, spread(high), 0.0)


def transport_kernel(mom, cond, base, wx, wy, wy_low, wz, wall, yh_lo, yh_hi, xh_lo, xh_hi, yb_lo, yb_hi, xb_lo, xb_hi,
                     xl_lo, xl_hi, ol_lo, ol_hi, fx_lo, fx_hi, fy_lo, fy_hi,
                     conc_out, src, sy_lo, sy_hi, sx_lo, sx_hi, drift, lines, low, dy_hi, own_dy):
    row = rows()
    below, above = y_terms(yh_lo, yh_hi)
    for m in range(4):
        lines[m] = below[m]
        lines[4 + m] = above[m]

    def step(x, extra):
        here = pl.ds(x, 1)

        def full(m):
            v = mom[m, x]
            if extra is not None:
                v = v + extra[m]
            v = v + jnp.where(row == 0, spread(lines[m, here, :]), 0.0)
            return v + jnp.where(row == N - 1, spread(lines[4 + m, here, :]), 0.0)

        scale = jnp.where(cond[x] > 0.0, 1.0 / full(0), 0.0)
        drift[0, x] = full(1) * scale
        v = full(2) * scale
        drift[1, x] = v
        drift[2, x] = full(3) * scale
        own_dy[here, :] = row_of(v, 0)

    a = [with_lines(plane(xh_lo, q), xl_lo, i) for q, i in enumerate(XPOS)]
    total = a[0] + a[1] + a[2] + a[3] + a[4]
    step(0, (total, total, a[1] - a[2], a[3] - a[4]))
    b = [with_lines(plane(xh_hi, q), xl_hi, i) for q, i in enumerate(XNEG)]
    total = b[0] + b[1] + b[2] + b[3] + b[4]
    step(N - 1, (total, -total, b[2] - b[1], b[4] - b[3]))

    def loop(x, carry):
        step(x, None)
        return carry

    lax.fori_loop(1, N - 1, loop, 0, unroll=2)

    def velocity(conductance, density, momentum):
        return jnp.where(conductance > 0.0, momentum / density, 0.0)

    def x_face(fx, xh, xl, xb, ol, sign):
        out = plane(xb, 0) + plane(xb, 1) + plane(xb, 2) + plane(xb, 3) + plane(xb, 4)
        out = plus_lines(out, ol[0:1, :], ol[1:2, :])
        density = plus_lines(plane(xh, 5), xl[2:3, :], xl[3:4, :])
        momentum = plus_lines(plane(xh, 6), xl[4:5, :], xl[5:6, :])
        return velocity(fx[RING + 2], density + out, momentum + sign * out)

    from_hi, from_lo = y_terms(yb_hi, yb_lo)

    def y_face(fy, yh, terms, k):
        density = plane(yh, 5) + terms[0]
        momentum = plane(yh, 6) + terms[2]
        for xl, x in ((xl_lo, 0), (xl_hi, N - 1)):
            density = density + jnp.where(row == x, spread(xl[k:k + 1, :]), 0.0)
            momentum = momentum + jnp.where(row == x, spread(xl[k + 1:k + 2, :]), 0.0)
        return velocity(fy[RING + 2], density, momentum)

    carried = y_face(fy_lo, yh_lo, from_lo, 6) + own_dy[...]
    for s in range(2):
        low[s] = wy_low[s] * carried
    dy_hi[...] = y_face(fy_hi, yh_hi, from_hi, 8)
    carried = x_face(fx_lo, xh_lo, xl_lo, xb_lo, ol_lo, -1.0) + drift[0, 0]
    behind = [wx[s, 0] * carried for s in range(2)]
    last = x_face(fx_hi, xh_hi, xl_hi, xb_hi, ol_hi, 1.0)
    for x in range(N):
        carried = drift[0, x] + (drift[0, x + 1] if x < N - 1 else last)
        ahead = [wx[s, x + 1] * carried for s in range(2)]
        tot = [ahead[s] - behind[s] for s in range(2)]
        behind = ahead
        v = drift[1, x]
        carried = v + jnp.where(row == N - 1, spread(dy_hi[x:x + 1, :]), roll_y(v, -1))
        for s in range(2):
            f = wy[s, x] * carried
            tot[s] = tot[s] + (f - jnp.where(row == 0, spread(low[s, x:x + 1, :]), roll_y(f, 1)))
        v = drift[2, x]
        carried = v + roll_z(v, -1)
        for s in range(2):
            f = wz[s, x] * carried
            tot[s] = tot[s] + (f - roll_z(f, 1))
        c0 = base[0, x] - tot[0]
        c1 = base[1, x] - tot[1]
        conc_out[0, x] = c0
        conc_out[1, x] = c1
        s_val = jnp.where(cond[x] > 0.0, c0 - c1, wall[x])
        src[x] = s_val
        for r in range(RING - 1):
            sy_lo[r, x:x + 1, :] = row_of(s_val, r)
            sy_hi[r, x:x + 1, :] = row_of(s_val, N - 1 - r)
        if x < RING - 1:
            sx_lo[x * N:(x + 1) * N, :] = s_val
        if N - 1 - x < RING - 1:
            sx_hi[(N - 1 - x) * N:(N - x) * N, :] = s_val
    corner_rows(POT_ROWS, fy_lo, fy_hi, sx_lo, sx_hi)


def corner_rows(listed, lo, hi, o_lo, o_hi):
    for at, a, side, b in listed:
        halo = hi if side else lo
        o_hi[at:at + 1, :] = halo[b - 1, N - a:N - a + 1, :]
        o_lo[at:at + 1, :] = halo[b - 1, a - 1:a, :]
    end = listed[-1][0] + 1
    for ref in (o_lo, o_hi):
        ref[end:, :] = jnp.zeros((ref.shape[0] - end, Z), F32)


def split(ext, a, b, pairs, shift):
    shape = (N + 2 * OFF, Z)
    mask = (lax.broadcasted_iota(jnp.int32, shape, 0) + lax.broadcasted_iota(jnp.int32, shape, 1)) % 2 == 0
    for k in pairs:
        p, q = ext[2 * k], ext[2 * k + 1]
        a[k + shift] = jnp.where(mask, p, q)
        b[k + shift] = jnp.where(mask, q, p)


def prepare_kernel(pot, src, fy_lo, fy_hi, ys_lo, ys_hi, even, odd, s_even, s_odd, ext):
    for centre, y_lo, y_hi, depth, a, b in ((pot, fy_lo, fy_hi, RING, even, odd), (src, ys_lo, ys_hi, RING - 1, s_even, s_odd)):
        for x in range(N):
            ext[x, OFF:OFF + N] = centre[x]
            for r in range(depth):
                ext[x, OFF - 1 - r:OFF - r, :] = y_lo[r, x:x + 1, :]
                ext[x, OFF + N + r:OFF + N + r + 1, :] = y_hi[r, x:x + 1, :]
        split(ext, a, b, range(N // 2), 0)


def sweep_kernel(even_in, odd_in, s_even_in, s_odd_in, fx_lo, fx_hi, xs_lo, xs_hi, xc_lo, xc_hi, out, ext, even, odd, s_even, s_odd):
    mid = slice(OFF, OFF + N)
    top = RING + N
    half = (N + 2 * RING) // 2
    shape = (N + 2 * OFF, Z)
    mask = (lax.broadcasted_iota(jnp.int32, shape, 0) + lax.broadcasted_iota(jnp.int32, shape, 1)) % 2 == 0
    zero = jnp.zeros(shape, F32)
    for ref in (even, odd):
        ref[0] = zero
        ref[half + 1] = zero
    for ref, given in ((even, even_in), (odd, odd_in), (s_even, s_even_in), (s_odd, s_odd_in)):
        for k in range(N // 2):
            ref[k + 1 + RING // 2] = given[k]
    ends = list(range(RING // 2)) + list(range(RING // 2 + N // 2, half))
    for x_lo, x_hi, depth, listed, c_lo, c_hi, a, b in (
            (lambda r: fx_lo[r], lambda r: fx_hi[r], RING, POT_ROWS, xs_lo, xs_hi, even, odd),
            (lambda r: plane(xs_lo, r), lambda r: plane(xs_hi, r), RING - 1, SRC_ROWS, xc_lo, xc_hi, s_even, s_odd)):
        for r in range(depth):
            ext[RING - 1 - r, mid] = x_lo(r)
            ext[top + r, mid] = x_hi(r)
        for at, a_ring, side, b_ring in listed:
            y = OFF + N + b_ring - 1 if side else OFF - b_ring
            ext[RING - a_ring, y:y + 1, :] = c_lo[at:at + 1, :]
            ext[top + a_ring - 1, y:y + 1, :] = c_hi[at:at + 1, :]
        split(ext, a, b, ends, 1)

    for h in range(6):
        this, other, s = (even, odd, s_even) if h % 2 == 0 else (odd, even, s_odd)

        def update(k, carry, h=h, this=this, other=other, s=s):
            c = other[k]
            before, after = other[k - 1], other[k + 1]
            far = jnp.where(mask, before, after) if h % 2 == 0 else jnp.where(mask, after, before)
            nb = (c + far) + (roll_y(c, 1) + roll_y(c, -1)) + (roll_z(c, 1) + roll_z(c, -1))
            this[k] = -0.6 * this[k] + (1.6 / 6.0) * (nb + s[k])
            return carry

        lo = (h + 1) // 2
        for k in range(lo + 1, half - lo + 1):
            update(k, 0)

    def last(k, carry):
        p, q = even[k], odd[k]
        out[2 * (k - 1) - RING] = jnp.where(mask, p, q)[OFF:OFF + N]
        out[2 * (k - 1) - RING + 1] = jnp.where(mask, q, p)[OFF:OFF + N]
        return carry

    lax.fori_loop(RING // 2 + 1, RING // 2 + N // 2 + 1, last, 0)


def patch_kernel(buf, ex_lo, ex_hi, ey_lo, ey_hi, yh_lo, yh_hi, xh_lo, xh_hi, xl_lo, xl_hi, out, done, sems):
    row = rows()
    copies = []
    for i in range(19):
        cx, cy, _ = C[i]

        def halo(v, src, i=i, cy=cy):
            if cy == 1:
                return jnp.where(row == 0, spread(yh_lo[pl.ds(YPOS.index(i) * N + src, 1), :]), v)
            if cy == -1:
                return jnp.where(row == N - 1, spread(yh_hi[pl.ds(YNEG.index(i) * N + src, 1), :]), v)
            return v

        def inner(src, carry, i=i, cx=cx, cy=cy, halo=halo):
            here = pl.ds(src, 1)
            v = buf[i, src + cx]
            if cy != -1:
                v = jnp.where(row == cy, spread(ey_lo[i, here, :]), v)
            if cy != 1:
                v = jnp.where(row == N - 1 + cy, spread(ey_hi[i, here, :]), v)
            done[i, src + cx] = halo(v, src)
            return carry

        lax.fori_loop(1, N - 1, inner, 0, unroll=True)
        if cx != -1:
            done[i, cx] = halo(ex_lo[i], 0)
        if cx != 1:
            done[i, N - 1 + cx] = halo(ex_hi[i], N - 1)
        if cx == 1:
            done[i, 0] = with_lines(plane(xh_lo, XPOS.index(i)), xl_lo, i)
        if cx == -1:
            done[i, N - 1] = with_lines(plane(xh_hi, XNEG.index(i)), xl_hi, i)
        copy = pltpu.make_async_copy(done.at[i], out.at[i], sems.at[i])
        copy.start()
        copies.append(copy)
    for copy in copies:
        copy.wait()


def flux(a, b):
    link = a[2] * b[2]
    drop = a[3] - b[3]
    rest, weight = [], []
    for s in range(2):
        both = a[s] + b[s]
        rest.append(link * (RATES[s] * ((a[s] - b[s]) + ((0.5 * VAL[s]) * both) * drop)))
        weight.append((0.25 * link) * both)
    return rest, weight


def diffuse_kernel(charge, classes_h, cond, conc, pot, fx_lo, fx_hi, fy_lo, fy_hi, gy_lo,
                   base, wx, wy, wy_low, wz, wall, low, classes, sem):
    fetch = pltpu.make_async_copy(classes_h, classes, sem)
    fetch.start()
    row = rows()

    def faces(ref):
        return tuple(ref[RING + q] for q in range(3)) + (ref[0],)

    rest, weight = flux(faces(fy_lo), faces(gy_lo))
    for s in range(2):
        low[s] = rest[s]
        wy_low[s] = weight[s]
    upper = faces(fy_hi)

    def fields(x):
        return (conc[0, x], conc[1, x], cond[x], pot[x])

    behind, weight = flux(faces(fx_lo), fields(0))
    for s in range(2):
        wx[s, 0] = weight[s]
    fetch.wait()
    for x in range(N):
        me = fields(x)
        ahead, weight = flux(me, fields(x + 1) if x < N - 1 else faces(fx_hi))
        tot = [ahead[s] - behind[s] for s in range(2)]
        behind = ahead
        for s in range(2):
            wx[s, x + 1] = weight[s]
        nxt = tuple(jnp.where(row == N - 1, spread(row_of(upper[q], x)), roll_y(me[q], -1)) for q in range(4))
        rest, weight = flux(me, nxt)
        for s in range(2):
            wy[s, x] = weight[s]
            tot[s] = tot[s] + (rest[s] - jnp.where(row == 0, spread(low[s, x:x + 1, :]), roll_y(rest[s], 1)))
        rest, weight = flux(me, tuple(roll_z(v, -1) for v in me))
        for s in range(2):
            wz[s, x] = weight[s]
            tot[s] = tot[s] + (rest[s] - roll_z(rest[s], 1))
            base[s, x] = me[s] - tot[s]
        cls = classes[x]
        total = jnp.zeros((N, Z), F32)
        for q in range(4):
            total = total + jnp.where(cls == q, charge[q], 0.0)
        wall[x] = total


def ring_rows(depth, total):
    listed = []
    at = depth
    for a in range(1, total):
        for side in (0, 1):
            for b in range(1, total - a + 1):
                listed.append((at, a, side, b))
                at += 1
    return listed


SRC_ROWS = ring_rows(0, RING - 1)
POT_ROWS = ring_rows((RING - 1) * N, RING)
SRC_LEN = 24


def pack_src_kernel(ys_lo, ys_hi, o_lo, o_hi):
    corner_rows(SRC_ROWS, ys_lo, ys_hi, o_lo, o_hi)


def swap(axis, hi, lo):
    n = lax.axis_size(axis)
    even = lax.axis_index(axis) % 2 == 0
    first = lax.ppermute(jnp.where(even, hi, lo), axis, [(i, i + 1 - 2 * (i % 2)) for i in range(n)])
    second = lax.ppermute(jnp.where(even, lo, hi), axis, [(i, (i - 1 + 2 * (i % 2)) % n) for i in range(n)])
    return jnp.where(even, second, first), jnp.where(even, first, second)


def body(pops, conc, pot, mob, solid, classes, charge):
    cube = sds(N, N, Z)
    msg = sds(ROWS, Z)
    gx_hi, gx_lo, gy_hi, gy_lo, cond = call(
        faces_kernel, [sds(RING + 3, N, Z)] * 4 + [cube], "faces", "hhhh",
        scratch=[VM((N, N, Z), F32), VM((2, N, N, Z), F32), VM((N, N, Z), F32), VM((N, N, Z), jnp.int32),
                 pltpu.SemaphoreType.DMA((4,))], mib=53, moved=2600000)(
        pot, conc, mob, solid)
    fx_lo, fx_hi = swap("gx", gx_hi, gx_lo)
    fy_lo, fy_hi = swap("gy", gy_hi, gy_lo)
    chunks = N // CHUNK
    buf, mom, px_lo, px_hi, pr_lo, pr_hi = call(
        collide_kernel, [sds(19, N, N, Z), sds(4, N, N, Z)] + [sds(19, N, Z)] * 4, "collide", "hhhv",
        scratch=[VM((19, N, N, Z), F32), VM((N, N, Z), F32), VM((2, N, N, Z), F32),
                 pltpu.SemaphoreType.DMA((chunks,)), pltpu.SemaphoreType.DMA((4,))],
        mib=43, flops=20000000, moved=14000000)(pops, pot, conc, cond)
    mom, ex_lo, ex_hi, ey_lo, ey_hi, yb_lo, yb_hi, xb_lo, xb_hi = call(
        edge_kernel, [sds(4, N, N, Z)] + [sds(19, N, Z)] * 4 + [msg, msg, sds(LINE, Z), sds(LINE, Z)], "edge", "v" * 13, moved=3000000)(
        px_lo, px_hi, pr_lo, pr_hi, gx_lo, gx_hi, gy_lo, gy_hi, fx_lo, fx_hi, fy_lo, fy_hi, mom)
    yh_lo, yh_hi = swap("gy", yb_hi, yb_lo)
    xh_lo, xh_hi = swap("gx", xb_hi, xb_lo)
    ol_lo, ol_hi = call(corner_kernel, [sds(N, Z)] * 2, "corner", "vvvv")(yh_lo, yh_hi, yb_lo, yb_hi)
    xl_lo, xl_hi = swap("gx", ol_hi, ol_lo)
    face = VM((N, Z), F32)
    fy_late, _ = lax.optimization_barrier((fy_lo, yh_lo))
    pair = sds(2, N, N, Z)
    base, wx, wy, wy_low, wz, wall = call(
        diffuse_kernel, [pair, sds(2, N + 1, N, Z), pair, sds(2, N, Z), pair, cube], "diffuse", "sh" + "v" * 8,
        scratch=[VM((2, N, Z), F32), VM((N, N, Z), jnp.int32), pltpu.SemaphoreType.DMA], flops=10000000, moved=6000000)(
        charge, classes, cond, conc, pot, fx_lo, fx_hi, fy_late, fy_hi, gy_lo)
    conc_out, src, sy_lo, sy_hi, sx_lo, sx_hi = call(
        transport_kernel, [pair, cube, sds(RING - 1, N, Z), sds(RING - 1, N, Z), sds(LINE, Z), sds(LINE, Z)], "transport", "v" * 24,
        scratch=[VM((3, N, N, Z), F32), VM((8, N, Z), F32), VM((2, N, Z), F32), face, face], flops=5000000, moved=4000000)(
        mom, cond, base, wx, wy, wy_low, wz, wall, yh_lo, yh_hi, xh_lo, xh_hi, yb_lo, yb_hi, xb_lo, xb_hi,
        xl_lo, xl_hi, ol_lo, ol_hi, fx_lo, fx_hi, fy_lo, fy_hi)
    ys_lo, ys_hi = swap("gy", sy_hi, sy_lo)
    xs_lo, xs_hi = swap("gx", sx_hi, sx_lo)
    oc_lo, oc_hi = call(pack_src_kernel, [sds(SRC_LEN, Z)] * 2, "pack_src", "vv")(ys_lo, ys_hi)
    xc_lo, xc_hi = swap("gx", oc_hi, oc_lo)
    packed = VM(((N + 2 * RING) // 2 + 2, N + 2 * OFF, Z), F32)
    prepared = call(
        prepare_kernel, [sds(N // 2, N + 2 * OFF, Z)] * 4, "prepare", "v" * 6,
        scratch=[VM((N, N + 2 * OFF, Z), F32)], flops=1000000, moved=4000000)(pot, src, fy_lo, fy_hi, ys_lo, ys_hi)
    potential_out = call(
        sweep_kernel, [cube], "sweep", "v" * 10,
        scratch=[VM((N + 2 * RING, N + 2 * OFF, Z), F32)] + [packed] * 4, flops=20000000, moved=4000000)(
        *prepared, fx_lo, fx_hi, xs_lo, xs_hi, xc_lo, xc_hi)[0]
    pop = call(
        patch_kernel, [sds(19, N, N, Z)], "patch", "v" * 11, out_specs="h",
        scratch=[VM((19, N, N, Z), F32), pltpu.SemaphoreType.DMA((19,))], mib=16, moved=10000000)(
        buf, ex_lo, ex_hi, ey_lo, ey_hi, yh_lo, yh_hi, xh_lo, xh_hi, xl_lo, xl_hi)[0]
    return (pop, conc_out, potential_out)


def solution(mesh):
    lattice = P(None, "gx", "gy", None)
    flat = P("gx", "gy", None)
    return jax.shard_map(
        body, mesh=mesh, in_specs=(lattice, lattice, flat, flat, flat, flat, P()),
        out_specs=(lattice, lattice, flat), check_vma=False)
```

```python
import jax
import jax.numpy as jnp
from jax import lax
from jax.experimental import pallas as pl
from jax.experimental.pallas import tpu as pltpu
from jax.sharding import PartitionSpec as P

C = [(0, 0, 0), (1, 0, 0), (-1, 0, 0), (0, 1, 0), (0, -1, 0), (0, 0, 1), (0, 0, -1),
     (1, 1, 0), (-1, -1, 0), (1, -1, 0), (-1, 1, 0), (1, 0, 1), (-1, 0, -1), (1, 0, -1), (-1, 0, 1),
     (0, 1, 1), (0, -1, -1), (0, 1, -1), (0, -1, 1)]
W = [1.0 / 3.0] + [1.0 / 18.0] * 6 + [1.0 / 36.0] * 12
XPOS = [i for i in range(19) if C[i][0] == 1]
XNEG = [i for i in range(19) if C[i][0] == -1]
YPOS = [i for i in range(19) if C[i][1] == 1]
YNEG = [i for i in range(19) if C[i][1] == -1]
RATES = (0.06, 0.08)
VAL = (1.0, -1.0)
N = 16
Z = 256
CHUNK = 4
RING = 6
OFF = 8
ROWS = 7 * N + 8
LINE = 7 * N
SOLID = 1.0
F32 = jnp.float32
VM = pltpu.VMEM


def sds(*shape):
    return jax.ShapeDtypeStruct(shape, F32)


def params(mib):
    return pltpu.CompilerParams(vmem_limit_bytes=mib * 1024 * 1024)


def rows():
    return lax.broadcasted_iota(jnp.int32, (N, Z), 0)


def roll_y(v, s):
    return pltpu.roll(v, s % v.shape[0], 0)


def roll_z(v, s):
    return pltpu.roll(v, s % v.shape[1], 1)


def row_of(v, y):
    return v[y:y + 1, :]


def spread(row):
    return jnp.broadcast_to(row, (N, Z))


def shift_up(v):
    return jnp.where(rows() == 0, 0.0, roll_y(v, 1))


def shift_down(v):
    return jnp.where(rows() == N - 1, 0.0, roll_y(v, -1))


def shift_by(v, c):
    return shift_up(v) if c == 1 else shift_down(v) if c == -1 else v


def call(kernel, outs, name, specs, scratch=(), mib=16, flops=0, out_specs=None, moved=0):
    return pl.pallas_call(
        kernel,
        in_specs=[pl.BlockSpec(memory_space={"v": VM, "h": pltpu.HBM, "s": pltpu.SMEM}[c]) for c in specs],
        out_specs=[pl.BlockSpec(memory_space={"v": VM, "h": pltpu.HBM}[c]) for c in out_specs or "v" * len(outs)],
        out_shape=outs,
        scratch_shapes=list(scratch),
        compiler_params=params(mib),
        cost_estimate=pl.CostEstimate(flops=flops, bytes_accessed=moved, transcendentals=0),
        name=name,
    )


def faces_kernel(pot_h, conc_h, mob_h, solid_h, gx_hi, gx_lo, gy_hi, gy_lo, pull, middle, pot, cond, conc, mob, solid, sems):
    pairs = ((pot_h, pot), (conc_h, conc), (mob_h, mob), (solid_h, solid))
    copies = [pltpu.make_async_copy(a, b, sems.at[q]) for q, (a, b) in enumerate(pairs)]
    for c in copies:
        c.start()
    for c in copies:
        c.wait()

    def step(x, carry):
        here = pl.ds(x, 1)
        is_fluid = solid[x] == 0
        cond[x] = jnp.where(is_fluid, jnp.sqrt(mob[x]), 0.0)
        pull[x] = jnp.where(is_fluid, (conc[0, x] - conc[1, x]) * (-0.001), SOLID)
        for r in range(RING):
            gy_hi[r, here, :] = pot[x, N - 1 - r:N - r, :]
            gy_lo[r, here, :] = pot[x, r:r + 1, :]
        for q, v in ((0, conc.at[0]), (1, conc.at[1]), (2, cond)):
            gy_hi[RING + q, here, :] = v[x, N - 1:N, :]
            gy_lo[RING + q, here, :] = v[x, 0:1, :]
        return carry

    lax.fori_loop(0, N, step, 0, unroll=True)
    for x in range(RING, N - RING):
        middle[x - RING] = pot[x]
    for x, face in ((N - 1, gx_hi), (0, gx_lo)):
        for r in range(RING):
            face[r] = pot[abs(x - r)]
        face[RING] = conc[0, x]
        face[RING + 1] = conc[1, x]
        face[RING + 2] = cond[x]


def post_of(p, fluid, q, slopes):
    pull = jnp.where(fluid, q, 0.0)
    force = [pull * d for d in slopes]
    density = p[0]
    for i in range(1, 19):
        density = density + p[i]
    inv = 1.0 / density
    u = []
    for a in range(3):
        total = 0.9 * force[a]
        for i in range(1, 19, 2):
            if C[i][a]:
                term = p[i] - p[i + 1]
                total = total + term if C[i][a] == 1 else total - term
        u.append(total * inv)
    base = 1.0 - 1.5 * (u[0] * u[0] + u[1] * u[1] + u[2] * u[2])
    scaled = density * (10.0 / 9.0)
    out = [jnp.where(fluid, (W[0] * scaled) * base - p[0] * (1.0 / 9.0), p[0])]
    for i in range(1, 19, 2):
        along = None
        for a in range(3):
            if C[i][a]:
                term = u[a] if C[i][a] == 1 else -u[a]
                along = term if along is None else along + term
        even = base + 4.5 * along * along
        odd = 3.0 * along
        ws = W[i] * scaled
        fwd = ws * (even + odd) - p[i] * (1.0 / 9.0)
        bwd = ws * (even - odd) - p[i + 1] * (1.0 / 9.0)
        out.append(jnp.where(fluid, fwd, p[i + 1]))
        out.append(jnp.where(fluid, bwd, p[i]))
    return out, force


def sums(values, keep):
    total = [None] * 4
    for cy in (0, 1, -1):
        part = [None] * 4
        for i, v in values:
            if C[i][1] != cy:
                continue
            for m, c in enumerate((1,) + C[i]):
                if c and m != 2:
                    w = v if c == 1 else -v
                    part[m] = w if part[m] is None else part[m] + w
        for m in (0, 1, 3):
            if part[m] is None:
                continue
            w = part[m] if keep[cy] is None else jnp.where(keep[cy], part[m], 0.0)
            total[m] = w if total[m] is None else total[m] + w
            if m == 0 and cy:
                w = w if cy == 1 else -w
                total[2] = w if total[2] is None else total[2] + w
    return total


def collide_kernel(pops, gx_hi, gx_lo, middle, pull, buf, mom, px_lo, px_hi, pr_lo, pr_hi, held, sems, psems):
    chunks = [pltpu.make_async_copy(pops.at[:, pl.ds(CHUNK * s, CHUNK)], held.at[:, pl.ds(CHUNK * s, CHUNK)], sems.at[s])
              for s in range(N // CHUNK)]
    ends = [pltpu.make_async_copy(pops.at[:, 0], px_lo, psems.at[0]),
            pltpu.make_async_copy(pops.at[:, N - 1], px_hi, psems.at[1])]
    for c in chunks + ends:
        c.start()
    row = rows()
    zero = jnp.zeros((N, Z), F32)
    keep = {0: (row >= 1) & (row <= N - 2), 1: row >= 2, -1: row <= N - 3}
    for m in range(4):
        mom[m, 0] = zero
        mom[m, 1] = zero

    def pot(x):
        return gx_lo[x] if x < RING else gx_hi[N - 1 - x] if x >= N - RING else middle[x - RING]

    def step(x):
        here = pl.ds(x, 1)
        p = [held[i, x] for i in range(19)]
        for i in range(19):
            pr_lo[i, here, :] = row_of(p[i], 0)
            pr_hi[i, here, :] = row_of(p[i], N - 1)
        centre = pot(x)
        slopes = (pot(x + 1) - pot(x - 1), roll_y(centre, -1) - roll_y(centre, 1), roll_z(centre, -1) - roll_z(centre, 1))
        post, force = post_of(p, pull[x] < 0.5 * SOLID, pull[x], slopes)
        moved = []
        for i in range(19):
            v = post[i]
            if C[i][2]:
                v = roll_z(v, C[i][2])
            if C[i][1]:
                v = roll_y(v, C[i][1])
            buf[i, x + C[i][0]] = v
            moved.append(v)
        g = sums([(i, moved[i]) for i in range(19) if C[i][0] == 0], keep)
        mom[0, x] += g[0]
        for m in (1, 2, 3):
            w = jnp.where(keep[0], 0.5 * force[m - 1], 0.0)
            mom[m, x] += w if g[m] is None else g[m] + w
        g = sums([(i, moved[i]) for i in XPOS], keep)
        for m in range(4):
            mom[m, x + 1] = g[m]
        g = sums([(i, moved[i]) for i in XNEG], keep)
        for m in range(4):
            mom[m, x - 1] += g[m]

    for s in range(N // CHUNK):
        chunks[s].wait()
        for x in range(max(CHUNK * s, 1), min(CHUNK * s + CHUNK, N - 1)):
            step(x)
    for c in ends:
        c.wait()


def edge_kernel(px_lo, px_hi, pr_lo, pr_hi, gx_lo, gx_hi, gy_lo, gy_hi, fx_lo, fx_hi, fy_lo, fy_hi, mom0,
                mom, ex_lo, ex_hi, ey_lo, ey_hi, yb_lo, yb_hi):
    row = rows()
    inner = (row >= 1) & (row <= N - 2)
    keep = {0: None, 1: row >= 1, -1: row <= N - 2}
    lines = {}
    for pr, gy, fy, ey, low in ((pr_lo, gy_lo, fy_lo, ey_lo, True), (pr_hi, gy_hi, fy_hi, ey_hi, False)):
        centre = gy[0]
        y_slope = gy[1] - fy[0] if low else fy[0] - gy[1]
        slopes = (roll_y(centre, -1) - roll_y(centre, 1), y_slope, roll_z(centre, -1) - roll_z(centre, 1))
        post, force = post_of([pr[i] for i in range(19)], gy[RING + 2] > 0.0, (gy[RING] - gy[RING + 1]) * (-0.001), slopes)
        for i in range(19):
            v = roll_z(post[i], C[i][2]) if C[i][2] else post[i]
            v = jnp.where(inner, v, 0.0)
            ey[i] = v
            if low and C[i][1] == -1:
                q = YNEG.index(i)
                yb_lo[q * N:(q + 1) * N, :] = v
            if not low and C[i][1] == 1:
                q = YPOS.index(i)
                yb_hi[q * N:(q + 1) * N, :] = v
            post[i] = shift_by(v, C[i][0])
        for cy in (0, 1 if low else -1):
            y = (0 if low else N - 1) + cy
            total = [None] * 4
            for i in range(19):
                if C[i][1] == cy:
                    for m, c in enumerate((1,) + C[i]):
                        if c:
                            w = post[i] if c == 1 else -post[i]
                            total[m] = w if total[m] is None else total[m] + w
            if cy == 0:
                for a in range(3):
                    w = jnp.where(inner, 0.5 * force[a], 0.0)
                    total[a + 1] = w if total[a + 1] is None else total[a + 1] + w
            lines[y] = total
    for x in range(N):
        for m in range(4):
            v = mom0[m, x]
            for y in (0, 1, N - 2, N - 1):
                v = v + jnp.where(row == y, spread(row_of(lines[y][m], x)), 0.0)
            mom[m, x] = v
    for px, gx, fx, ex, low in ((px_lo, gx_lo, fx_lo, ex_lo, True), (px_hi, gx_hi, fx_hi, ex_hi, False)):
        at = 0 if low else N - 1
        centre = gx[0]
        x_slope = gx[1] - fx[0] if low else fx[0] - gx[1]
        y_up = jnp.where(row == N - 1, spread(fy_hi[0, at:at + 1, :]), roll_y(centre, -1))
        y_dn = jnp.where(row == 0, spread(fy_lo[0, at:at + 1, :]), roll_y(centre, 1))
        slopes = (x_slope, y_up - y_dn, roll_z(centre, -1) - roll_z(centre, 1))
        post, force = post_of([px[i] for i in range(19)], gx[RING + 2] > 0.0, (gx[RING] - gx[RING + 1]) * (-0.001), slopes)
        for i in range(19):
            v = roll_z(post[i], C[i][2]) if C[i][2] else post[i]
            if C[i][1] == 1:
                v = roll_y(v, 1)
                at_row = YPOS.index(i) * N + at
                yb_hi[at_row:at_row + 1, :] = row_of(v, 0)
                v = jnp.where(row == 0, 0.0, v)
            elif C[i][1] == -1:
                v = roll_y(v, -1)
                at_row = YNEG.index(i) * N + at
                yb_lo[at_row:at_row + 1, :] = row_of(v, N - 1)
                v = jnp.where(row == N - 1, 0.0, v)
            ex[i] = v
            post[i] = v
        none = {0: None, 1: None, -1: None}
        g = sums([(i, post[i]) for i in range(19) if C[i][0] == 0], none)
        mom[0, at] += g[0]
        for m in (1, 2, 3):
            w = 0.5 * force[m - 1]
            mom[m, at] += w if g[m] is None else g[m] + w
        g = sums([(i, post[i]) for i in (XPOS if low else XNEG)], none)
        for m in range(4):
            mom[m, 1 if low else N - 2] += g[m]
        g = sums([(i, post[i]) for i in (XNEG if low else XPOS)], none)
        k = LINE + (2 if low else 0)
        yb_hi[k:k + 1, :] = row_of(g[0], N - 1)
        yb_hi[k + 1:k + 2, :] = row_of(g[2], N - 1)
        yb_lo[k:k + 1, :] = row_of(g[0], 0)
        yb_lo[k + 1:k + 2, :] = row_of(g[2], 0)
    for x in range(N):
        for q, m in ((5, 0), (6, 2)):
            yb_lo[q * N + x:q * N + x + 1, :] = mom[m, x, 0:1, :]
            yb_hi[q * N + x:q * N + x + 1, :] = mom[m, x, N - 1:N, :]
    yb_lo[LINE + 4:, :] = jnp.zeros((4, Z), F32)
    yb_hi[LINE + 4:, :] = jnp.zeros((4, Z), F32)


def plane(ref, q):
    return ref[q * N:(q + 1) * N, :]


def line(ref, q, x):
    return ref[q * N + x:q * N + x + 1, :]


def y_terms(lo, hi):
    s3, s7, s10, s15, s17 = (plane(lo, q) for q in range(5))
    s7, s10 = shift_up(s7), shift_down(s10)
    total = s3 + s7 + s10 + s15 + s17
    below = (total, s7 - s10, total, s15 - s17)
    s4, s8, s9, s16, s18 = (plane(hi, q) for q in range(5))
    s8, s9 = shift_down(s8), shift_up(s9)
    total = s4 + s8 + s9 + s16 + s18
    return below, (total, s9 - s8, -total, s18 - s16)


def corner_kernel(ex_lo, ex_hi, yh_lo, yh_hi, yb_lo, yb_hi, mom, xb_lo, xb_hi):
    row = rows()
    below, above = y_terms(yh_lo, yh_hi)
    for ex, xb, slots, at in ((ex_hi, xb_hi, XPOS, N - 1), (ex_lo, xb_lo, XNEG, 0)):
        for q, i in enumerate(slots):
            v = ex[i]
            if C[i][1] == 1:
                v = jnp.where(row == 0, spread(line(yh_lo, YPOS.index(i), at)), v)
            elif C[i][1] == -1:
                v = jnp.where(row == N - 1, spread(line(yh_hi, YNEG.index(i), at)), v)
            xb[q * N:(q + 1) * N, :] = v
        for q, m in ((5, 0), (6, 1)):
            v = mom[m, at] + jnp.where(row == 0, spread(row_of(below[m], at)), 0.0)
            xb[q * N:(q + 1) * N, :] = v + jnp.where(row == N - 1, spread(row_of(above[m], at)), 0.0)
        c = 1 if at else -1
        k = LINE if at else LINE + 2
        down = line(yb_lo, YNEG.index(9 if c == 1 else 8), at)
        up = line(yb_hi, YPOS.index(7 if c == 1 else 10), at)
        xb[LINE:LINE + 1, :] = yh_lo[k:k + 1, :] + down
        xb[LINE + 1:LINE + 2, :] = yh_lo[k + 1:k + 2, :] - down
        xb[LINE + 2:LINE + 3, :] = yh_hi[k:k + 1, :] + up
        xb[LINE + 3:LINE + 4, :] = yh_hi[k + 1:k + 2, :] + up
        xb[LINE + 4:, :] = jnp.zeros((4, Z), F32)


def transport_kernel(mom, cond, base, wx, wy, wy_low, wz, wall, yh_lo, yh_hi, xh_lo, xh_hi, yb_lo, yb_hi, xb_lo, xb_hi,
                     fx_lo, fx_hi, fy_lo, fy_hi, conc_out, src, sy_lo, sy_hi, drift, lines, low, dy_hi, own_dy):
    row = rows()
    below, above = y_terms(yh_lo, yh_hi)
    for m in range(4):
        lines[m] = below[m]
        lines[4 + m] = above[m]

    def step(x, extra):
        here = pl.ds(x, 1)

        def full(m):
            v = mom[m, x]
            if extra is not None:
                v = v + extra[m]
            v = v + jnp.where(row == 0, spread(lines[m, here, :]), 0.0)
            return v + jnp.where(row == N - 1, spread(lines[4 + m, here, :]), 0.0)

        scale = jnp.where(cond[x] > 0.0, 1.0 / full(0), 0.0)
        drift[0, x] = full(1) * scale
        v = full(2) * scale
        drift[1, x] = v
        drift[2, x] = full(3) * scale
        own_dy[here, :] = row_of(v, 0)

    a = [plane(xh_lo, q) for q in range(5)]
    total = a[0] + a[1] + a[2] + a[3] + a[4]
    step(0, (total, total, a[1] - a[2], a[3] - a[4]))
    b = [plane(xh_hi, q) for q in range(5)]
    total = b[0] + b[1] + b[2] + b[3] + b[4]
    step(N - 1, (total, -total, b[2] - b[1], b[4] - b[3]))

    def loop(x, carry):
        step(x, None)
        return carry

    lax.fori_loop(1, N - 1, loop, 0, unroll=2)

    def velocity(conductance, density, momentum):
        return jnp.where(conductance > 0.0, momentum / density, 0.0)

    def x_face(fx, xh, xb, sign):
        out = plane(xb, 0) + plane(xb, 1) + plane(xb, 2) + plane(xb, 3) + plane(xb, 4)
        return velocity(fx[RING + 2], plane(xh, 5) + out, plane(xh, 6) + sign * out)

    from_hi, from_lo = y_terms(yb_hi, yb_lo)

    def y_face(fy, yh, terms, k):
        density = plane(yh, 5) + terms[0]
        momentum = plane(yh, 6) + terms[2]
        for xh, x in ((xh_lo, 0), (xh_hi, N - 1)):
            density = density + jnp.where(row == x, spread(xh[k:k + 1, :]), 0.0)
            momentum = momentum + jnp.where(row == x, spread(xh[k + 1:k + 2, :]), 0.0)
        return velocity(fy[RING + 2], density, momentum)

    carried = y_face(fy_lo, yh_lo, from_lo, LINE) + own_dy[...]
    for s in range(2):
        low[s] = wy_low[s] * carried
    dy_hi[...] = y_face(fy_hi, yh_hi, from_hi, LINE + 2)
    carried = x_face(fx_lo, xh_lo, xb_lo, -1.0) + drift[0, 0]
    behind = [wx[s, 0] * carried for s in range(2)]
    last = x_face(fx_hi, xh_hi, xb_hi, 1.0)
    for x in range(N):
        carried = drift[0, x] + (drift[0, x + 1] if x < N - 1 else last)
        ahead = [wx[s, x + 1] * carried for s in range(2)]
        tot = [ahead[s] - behind[s] for s in range(2)]
        behind = ahead
        v = drift[1, x]
        carried = v + jnp.where(row == N - 1, spread(dy_hi[x:x + 1, :]), roll_y(v, -1))
        for s in range(2):
            f = wy[s, x] * carried
            tot[s] = tot[s] + (f - jnp.where(row == 0, spread(low[s, x:x + 1, :]), roll_y(f, 1)))
        v = drift[2, x]
        carried = v + roll_z(v, -1)
        for s in range(2):
            f = wz[s, x] * carried
            tot[s] = tot[s] + (f - roll_z(f, 1))
        c0 = base[0, x] - tot[0]
        c1 = base[1, x] - tot[1]
        conc_out[0, x] = c0
        conc_out[1, x] = c1
        s_val = jnp.where(cond[x] > 0.0, c0 - c1, wall[x])
        src[x] = s_val
        for r in range(RING - 1):
            sy_lo[r, x:x + 1, :] = row_of(s_val, r)
            sy_hi[r, x:x + 1, :] = row_of(s_val, N - 1 - r)


def split(ext, a, b, pairs, shift):
    shape = (N + 2 * OFF, Z)
    mask = (lax.broadcasted_iota(jnp.int32, shape, 0) + lax.broadcasted_iota(jnp.int32, shape, 1)) % 2 == 0
    for k in pairs:
        p, q = ext[2 * k], ext[2 * k + 1]
        a[k + shift] = jnp.where(mask, p, q)
        b[k + shift] = jnp.where(mask, q, p)


def prepare_kernel(pot, src, fy_lo, fy_hi, ys_lo, ys_hi, even, odd, s_even, s_odd, ext):
    for centre, y_lo, y_hi, depth, a, b in ((pot, fy_lo, fy_hi, RING, even, odd), (src, ys_lo, ys_hi, RING - 1, s_even, s_odd)):
        for x in range(N):
            ext[x, OFF:OFF + N] = centre[x]
            for r in range(depth):
                ext[x, OFF - 1 - r:OFF - r, :] = y_lo[r, x:x + 1, :]
                ext[x, OFF + N + r:OFF + N + r + 1, :] = y_hi[r, x:x + 1, :]
        split(ext, a, b, range(N // 2), 0)


def sweep_kernel(even_in, odd_in, s_even_in, s_odd_in, fx_lo, fx_hi, xs_lo, xs_hi, out, ext, even, odd, s_even, s_odd):
    mid = slice(OFF, OFF + N)
    top = RING + N
    half = (N + 2 * RING) // 2
    shape = (N + 2 * OFF, Z)
    mask = (lax.broadcasted_iota(jnp.int32, shape, 0) + lax.broadcasted_iota(jnp.int32, shape, 1)) % 2 == 0
    zero = jnp.zeros(shape, F32)
    for ref in (even, odd):
        ref[0] = zero
        ref[half + 1] = zero
    for ref, given in ((even, even_in), (odd, odd_in), (s_even, s_even_in), (s_odd, s_odd_in)):
        for k in range(N // 2):
            ref[k + 1 + RING // 2] = given[k]
    ends = list(range(RING // 2)) + list(range(RING // 2 + N // 2, half))
    for x_lo, x_hi, depth, listed, a, b in (
            (lambda r: fx_lo[r], lambda r: fx_hi[r], RING, POT_ROWS, even, odd),
            (lambda r: plane(xs_lo, r), lambda r: plane(xs_hi, r), RING - 1, SRC_ROWS, s_even, s_odd)):
        for r in range(depth):
            ext[RING - 1 - r, mid] = x_lo(r)
            ext[top + r, mid] = x_hi(r)
        for at, a_ring, side, b_ring in listed:
            y = OFF + N + b_ring - 1 if side else OFF - b_ring
            ext[RING - a_ring, y:y + 1, :] = xs_lo[at:at + 1, :]
            ext[top + a_ring - 1, y:y + 1, :] = xs_hi[at:at + 1, :]
        split(ext, a, b, ends, 1)

    for h in range(6):
        this, other, s = (even, odd, s_even) if h % 2 == 0 else (odd, even, s_odd)

        def update(k, carry, h=h, this=this, other=other, s=s):
            c = other[k]
            before, after = other[k - 1], other[k + 1]
            far = jnp.where(mask, before, after) if h % 2 == 0 else jnp.where(mask, after, before)
            nb = (c + far) + (roll_y(c, 1) + roll_y(c, -1)) + (roll_z(c, 1) + roll_z(c, -1))
            this[k] = -0.6 * this[k] + (1.6 / 6.0) * (nb + s[k])
            return carry

        lo = (h + 1) // 2
        for k in range(lo + 1, half - lo + 1):
            update(k, 0)

    def last(k, carry):
        p, q = even[k], odd[k]
        out[2 * (k - 1) - RING] = jnp.where(mask, p, q)[OFF:OFF + N]
        out[2 * (k - 1) - RING + 1] = jnp.where(mask, q, p)[OFF:OFF + N]
        return carry

    lax.fori_loop(RING // 2 + 1, RING // 2 + N // 2 + 1, last, 0)


def patch_kernel(buf, ex_lo, ex_hi, ey_lo, ey_hi, yh_lo, yh_hi, xh_lo, xh_hi, out, done, sems):
    row = rows()
    copies = []
    for i in range(19):
        cx, cy, _ = C[i]

        def halo(v, src, i=i, cy=cy):
            if cy == 1:
                return jnp.where(row == 0, spread(yh_lo[pl.ds(YPOS.index(i) * N + src, 1), :]), v)
            if cy == -1:
                return jnp.where(row == N - 1, spread(yh_hi[pl.ds(YNEG.index(i) * N + src, 1), :]), v)
            return v

        def inner(src, carry, i=i, cx=cx, cy=cy, halo=halo):
            here = pl.ds(src, 1)
            v = buf[i, src + cx]
            if cy != -1:
                v = jnp.where(row == cy, spread(ey_lo[i, here, :]), v)
            if cy != 1:
                v = jnp.where(row == N - 1 + cy, spread(ey_hi[i, here, :]), v)
            done[i, src + cx] = halo(v, src)
            return carry

        lax.fori_loop(1, N - 1, inner, 0, unroll=True)
        if cx != -1:
            done[i, cx] = halo(ex_lo[i], 0)
        if cx != 1:
            done[i, N - 1 + cx] = halo(ex_hi[i], N - 1)
        if cx == 1:
            done[i, 0] = plane(xh_lo, XPOS.index(i))
        if cx == -1:
            done[i, N - 1] = plane(xh_hi, XNEG.index(i))
        copy = pltpu.make_async_copy(done.at[i], out.at[i], sems.at[i])
        copy.start()
        copies.append(copy)
    for copy in copies:
        copy.wait()


def flux(a, b):
    link = a[2] * b[2]
    drop = a[3] - b[3]
    rest, weight = [], []
    for s in range(2):
        both = a[s] + b[s]
        rest.append(link * (RATES[s] * ((a[s] - b[s]) + ((0.5 * VAL[s]) * both) * drop)))
        weight.append((0.25 * link) * both)
    return rest, weight


def diffuse_kernel(charge, classes_h, mob, solid, conc, pot, fx_lo, fx_hi, fy_lo, fy_hi, gy_lo,
                   base, wx, wy, wy_low, wz, wall, cond, low, classes, sem):
    fetch = pltpu.make_async_copy(classes_h, classes, sem)
    fetch.start()
    row = rows()

    def faces(ref):
        return tuple(ref[RING + q] for q in range(3)) + (ref[0],)

    rest, weight = flux(faces(fy_lo), faces(gy_lo))
    for s in range(2):
        low[s] = rest[s]
        wy_low[s] = weight[s]
    upper = faces(fy_hi)
    for x in range(N):
        cond[x] = jnp.where(solid[x] == 0, jnp.sqrt(mob[x]), 0.0)

    def fields(x):
        return (conc[0, x], conc[1, x], cond[x], pot[x])

    behind, weight = flux(faces(fx_lo), fields(0))
    for s in range(2):
        wx[s, 0] = weight[s]
    fetch.wait()
    for x in range(N):
        me = fields(x)
        ahead, weight = flux(me, fields(x + 1) if x < N - 1 else faces(fx_hi))
        tot = [ahead[s] - behind[s] for s in range(2)]
        behind = ahead
        for s in range(2):
            wx[s, x + 1] = weight[s]
        nxt = tuple(jnp.where(row == N - 1, spread(row_of(upper[q], x)), roll_y(me[q], -1)) for q in range(4))
        rest, weight = flux(me, nxt)
        for s in range(2):
            wy[s, x] = weight[s]
            tot[s] = tot[s] + (rest[s] - jnp.where(row == 0, spread(low[s, x:x + 1, :]), roll_y(rest[s], 1)))
        rest, weight = flux(me, tuple(roll_z(v, -1) for v in me))
        for s in range(2):
            wz[s, x] = weight[s]
            tot[s] = tot[s] + (rest[s] - roll_z(rest[s], 1))
            base[s, x] = me[s] - tot[s]
        cls = classes[x]
        total = jnp.zeros((N, Z), F32)
        for q in range(4):
            total = total + jnp.where(cls == q, charge[q], 0.0)
        wall[x] = total


def ring_rows(depth, total):
    listed = []
    at = depth
    for a in range(1, total):
        for side in (0, 1):
            for b in range(1, total - a + 1):
                listed.append((at, a, side, b))
                at += 1
    return listed


SRC_ROWS = ring_rows((RING - 1) * N, RING - 1)
POT_ROWS = ring_rows(SRC_ROWS[-1][0] + 1, RING)
SRC_LEN = 136


def pack_src_kernel(src, ys_lo, ys_hi, fy_lo, fy_hi, o_hi, o_lo):
    for k in range(RING - 1):
        o_hi[k * N:(k + 1) * N, :] = src[N - 1 - k]
        o_lo[k * N:(k + 1) * N, :] = src[k]
    for listed, lo, hi in ((SRC_ROWS, ys_lo, ys_hi), (POT_ROWS, fy_lo, fy_hi)):
        for at, a, side, b in listed:
            halo = hi if side else lo
            o_hi[at:at + 1, :] = halo[b - 1, N - a:N - a + 1, :]
            o_lo[at:at + 1, :] = halo[b - 1, a - 1:a, :]
    end = POT_ROWS[-1][0] + 1
    o_hi[end:, :] = jnp.zeros((SRC_LEN - end, Z), F32)
    o_lo[end:, :] = jnp.zeros((SRC_LEN - end, Z), F32)


def swap(axis, hi, lo):
    n = lax.axis_size(axis)
    even = lax.axis_index(axis) % 2 == 0
    first = lax.ppermute(jnp.where(even, hi, lo), axis, [(i, i + 1 - 2 * (i % 2)) for i in range(n)])
    second = lax.ppermute(jnp.where(even, lo, hi), axis, [(i, (i - 1 + 2 * (i % 2)) % n) for i in range(n)])
    return jnp.where(even, second, first), jnp.where(even, first, second)


def body(pops, conc, pot, mob, solid, classes, charge):
    cube = sds(N, N, Z)
    msg = sds(ROWS, Z)
    gx_hi, gx_lo, gy_hi, gy_lo, pull, middle = call(
        faces_kernel, [sds(RING + 3, N, Z)] * 4 + [cube, sds(N - 2 * RING, N, Z)], "faces", "hhhh",
        scratch=[VM((N, N, Z), F32), VM((N, N, Z), F32), VM((2, N, N, Z), F32), VM((N, N, Z), F32),
                 VM((N, N, Z), jnp.int32),
                 pltpu.SemaphoreType.DMA((4,))], mib=53, moved=2600000)(
        pot, conc, mob, solid)
    fx_lo, fx_hi = swap("gx", gx_hi, gx_lo)
    fy_lo, fy_hi = swap("gy", gy_hi, gy_lo)
    chunks = N // CHUNK
    buf, mom, px_lo, px_hi, pr_lo, pr_hi = call(
        collide_kernel, [sds(19, N, N, Z), sds(4, N, N, Z)] + [sds(19, N, Z)] * 4, "collide", "hvvvv",
        scratch=[VM((19, N, N, Z), F32), pltpu.SemaphoreType.DMA((chunks,)), pltpu.SemaphoreType.DMA((2,))],
        mib=43, flops=20000000, moved=14000000)(pops, gx_hi, gx_lo, middle, pull)
    mom, ex_lo, ex_hi, ey_lo, ey_hi, yb_lo, yb_hi = call(
        edge_kernel, [sds(4, N, N, Z)] + [sds(19, N, Z)] * 4 + [msg, msg], "edge", "v" * 13, moved=3000000)(
        px_lo, px_hi, pr_lo, pr_hi, gx_lo, gx_hi, gy_lo, gy_hi, fx_lo, fx_hi, fy_lo, fy_hi, mom)
    yh_lo, yh_hi = swap("gy", yb_hi, yb_lo)
    xb_lo, xb_hi = call(corner_kernel, [msg, msg], "corner", "v" * 7)(ex_lo, ex_hi, yh_lo, yh_hi, yb_lo, yb_hi, mom)
    xh_lo, xh_hi = swap("gx", xb_hi, xb_lo)
    face = VM((N, Z), F32)
    fy_late, _ = lax.optimization_barrier((fy_lo, yh_lo))
    pair = sds(2, N, N, Z)
    base, wx, wy, wy_low, wz, wall, cond = call(
        diffuse_kernel, [pair, sds(2, N + 1, N, Z), pair, sds(2, N, Z), pair, cube, cube], "diffuse", "sh" + "v" * 9,
        scratch=[VM((2, N, Z), F32), VM((N, N, Z), jnp.int32), pltpu.SemaphoreType.DMA], flops=10000000, moved=6000000)(
        charge, classes, mob, solid, conc, pot, fx_lo, fx_hi, fy_late, fy_hi, gy_lo)
    conc_out, src, sy_lo, sy_hi = call(
        transport_kernel, [pair, cube, sds(RING - 1, N, Z), sds(RING - 1, N, Z)], "transport", "v" * 20,
        scratch=[VM((3, N, N, Z), F32), VM((8, N, Z), F32), VM((2, N, Z), F32), face, face], flops=5000000, moved=4000000)(
        mom, cond, base, wx, wy, wy_low, wz, wall, yh_lo, yh_hi, xh_lo, xh_hi, yb_lo, yb_hi, xb_lo, xb_hi,
        fx_lo, fx_hi, fy_lo, fy_hi)
    ys_lo, ys_hi = swap("gy", sy_hi, sy_lo)
    bs_hi, bs_lo = call(pack_src_kernel, [sds(SRC_LEN, Z)] * 2, "pack_src", "v" * 5)(src, ys_lo, ys_hi, fy_lo, fy_hi)
    xs_lo, xs_hi = swap("gx", bs_hi, bs_lo)
    packed = VM(((N + 2 * RING) // 2 + 2, N + 2 * OFF, Z), F32)
    prepared = call(
        prepare_kernel, [sds(N // 2, N + 2 * OFF, Z)] * 4, "prepare", "v" * 6,
        scratch=[VM((N, N + 2 * OFF, Z), F32)], flops=1000000, moved=4000000)(pot, src, fy_lo, fy_hi, ys_lo, ys_hi)
    potential_out = call(
        sweep_kernel, [cube], "sweep", "v" * 8,
        scratch=[VM((N + 2 * RING, N + 2 * OFF, Z), F32)] + [packed] * 4, flops=20000000, moved=4000000)(
        *prepared, fx_lo, fx_hi, xs_lo, xs_hi)[0]
    pop = call(
        patch_kernel, [sds(19, N, N, Z)], "patch", "v" * 9, out_specs="h",
        scratch=[VM((19, N, N, Z), F32), pltpu.SemaphoreType.DMA((19,))], mib=16, moved=10000000)(
        buf, ex_lo, ex_hi, ey_lo, ey_hi, yh_lo, yh_hi, xh_lo, xh_hi)[0]
    return (pop, conc_out, potential_out)


def solution(mesh):
    lattice = P(None, "gx", "gy", None)
    flat = P("gx", "gy", None)
    return jax.shard_map(
        body, mesh=mesh, in_specs=(lattice, lattice, flat, flat, flat, flat, P()),
        out_specs=(lattice, lattice, flat), check_vma=False)
```

```python
import jax
import jax.numpy as jnp
from jax import lax
from jax.experimental import pallas as pl
from jax.experimental.pallas import tpu as pltpu
from jax.sharding import PartitionSpec as P

C = [(0, 0, 0), (1, 0, 0), (-1, 0, 0), (0, 1, 0), (0, -1, 0), (0, 0, 1), (0, 0, -1),
     (1, 1, 0), (-1, -1, 0), (1, -1, 0), (-1, 1, 0), (1, 0, 1), (-1, 0, -1), (1, 0, -1), (-1, 0, 1),
     (0, 1, 1), (0, -1, -1), (0, 1, -1), (0, -1, 1)]
W = [1.0 / 3.0] + [1.0 / 18.0] * 6 + [1.0 / 36.0] * 12
XPOS = [i for i in range(19) if C[i][0] == 1]
XNEG = [i for i in range(19) if C[i][0] == -1]
YPOS = [i for i in range(19) if C[i][1] == 1]
YNEG = [i for i in range(19) if C[i][1] == -1]
RATES = (0.06, 0.08)
VAL = (1.0, -1.0)
N = 16
Z = 256
CHUNK = 4
RING = 6
OFF = 8
ROWS = 7 * N + 8
LINE = 7 * N
SOLID = 1.0
F32 = jnp.float32
VM = pltpu.VMEM


def sds(*shape):
    return jax.ShapeDtypeStruct(shape, F32)


def params(mib):
    return pltpu.CompilerParams(vmem_limit_bytes=mib * 1024 * 1024)


def rows():
    return lax.broadcasted_iota(jnp.int32, (N, Z), 0)


def roll_y(v, s):
    return pltpu.roll(v, s % v.shape[0], 0)


def roll_z(v, s):
    return pltpu.roll(v, s % v.shape[1], 1)


def row_of(v, y):
    return v[y:y + 1, :]


def spread(row):
    return jnp.broadcast_to(row, (N, Z))


def shift_up(v):
    return jnp.where(rows() == 0, 0.0, roll_y(v, 1))


def shift_down(v):
    return jnp.where(rows() == N - 1, 0.0, roll_y(v, -1))


def shift_by(v, c):
    return shift_up(v) if c == 1 else shift_down(v) if c == -1 else v


def call(kernel, outs, name, specs, scratch=(), mib=16, flops=0, out_specs=None, moved=0):
    return pl.pallas_call(
        kernel,
        in_specs=[pl.BlockSpec(memory_space={"v": VM, "h": pltpu.HBM, "s": pltpu.SMEM}[c]) for c in specs],
        out_specs=[pl.BlockSpec(memory_space={"v": VM, "h": pltpu.HBM}[c]) for c in out_specs or "v" * len(outs)],
        out_shape=outs,
        scratch_shapes=list(scratch),
        compiler_params=params(mib),
        cost_estimate=pl.CostEstimate(flops=flops, bytes_accessed=moved, transcendentals=0),
        name=name,
    )


def faces_kernel(pot_h, conc_h, mob_h, solid_h, gx_hi, gx_lo, gy_hi, gy_lo, pull, middle, pot, cond, conc, mob, solid, sems):
    pairs = ((pot_h, pot), (conc_h, conc), (mob_h, mob), (solid_h, solid))
    copies = [pltpu.make_async_copy(a, b, sems.at[q]) for q, (a, b) in enumerate(pairs)]
    for c in copies:
        c.start()
    for c in copies:
        c.wait()

    def step(x, carry):
        here = pl.ds(x, 1)
        is_fluid = solid[x] == 0
        cond[x] = jnp.where(is_fluid, jnp.sqrt(mob[x]), 0.0)
        pull[x] = jnp.where(is_fluid, (conc[0, x] - conc[1, x]) * (-0.001), SOLID)
        for r in range(RING):
            gy_hi[r, here, :] = pot[x, N - 1 - r:N - r, :]
            gy_lo[r, here, :] = pot[x, r:r + 1, :]
        for q, v in ((0, conc.at[0]), (1, conc.at[1]), (2, cond)):
            gy_hi[RING + q, here, :] = v[x, N - 1:N, :]
            gy_lo[RING + q, here, :] = v[x, 0:1, :]
        return carry

    lax.fori_loop(0, N, step, 0, unroll=True)
    for x in range(RING, N - RING):
        middle[x - RING] = pot[x]
    for x, face in ((N - 1, gx_hi), (0, gx_lo)):
        for r in range(RING):
            face[r] = pot[abs(x - r)]
        face[RING] = conc[0, x]
        face[RING + 1] = conc[1, x]
        face[RING + 2] = cond[x]


def post_of(p, fluid, q, slopes):
    pull = jnp.where(fluid, q, 0.0)
    force = [pull * d for d in slopes]
    density = p[0]
    for i in range(1, 19):
        density = density + p[i]
    inv = 1.0 / density
    u = []
    for a in range(3):
        total = 0.9 * force[a]
        for i in range(1, 19, 2):
            if C[i][a]:
                term = p[i] - p[i + 1]
                total = total + term if C[i][a] == 1 else total - term
        u.append(total * inv)
    base = 1.0 - 1.5 * (u[0] * u[0] + u[1] * u[1] + u[2] * u[2])
    scaled = density * (10.0 / 9.0)
    out = [jnp.where(fluid, (W[0] * scaled) * base - p[0] * (1.0 / 9.0), p[0])]
    for i in range(1, 19, 2):
        along = None
        for a in range(3):
            if C[i][a]:
                term = u[a] if C[i][a] == 1 else -u[a]
                along = term if along is None else along + term
        even = base + 4.5 * along * along
        odd = 3.0 * along
        ws = W[i] * scaled
        fwd = ws * (even + odd) - p[i] * (1.0 / 9.0)
        bwd = ws * (even - odd) - p[i + 1] * (1.0 / 9.0)
        out.append(jnp.where(fluid, fwd, p[i + 1]))
        out.append(jnp.where(fluid, bwd, p[i]))
    return out, force


def sums(values, keep):
    total = [None] * 4
    for cy in (0, 1, -1):
        part = [None] * 4
        for i, v in values:
            if C[i][1] != cy:
                continue
            for m, c in enumerate((1,) + C[i]):
                if c and m != 2:
                    w = v if c == 1 else -v
                    part[m] = w if part[m] is None else part[m] + w
        for m in (0, 1, 3):
            if part[m] is None:
                continue
            w = part[m] if keep[cy] is None else jnp.where(keep[cy], part[m], 0.0)
            total[m] = w if total[m] is None else total[m] + w
            if m == 0 and cy:
                w = w if cy == 1 else -w
                total[2] = w if total[2] is None else total[2] + w
    return total


def collide_kernel(pops, gx_hi, gx_lo, middle, pull, buf, mom, px_lo, px_hi, pr_lo, pr_hi, held, sems, psems):
    chunks = [pltpu.make_async_copy(pops.at[:, pl.ds(CHUNK * s, CHUNK)], held.at[:, pl.ds(CHUNK * s, CHUNK)], sems.at[s])
              for s in range(N // CHUNK)]
    ends = [pltpu.make_async_copy(pops.at[:, 0], px_lo, psems.at[0]),
            pltpu.make_async_copy(pops.at[:, N - 1], px_hi, psems.at[1])]
    for c in chunks + ends:
        c.start()
    row = rows()
    zero = jnp.zeros((N, Z), F32)
    keep = {0: (row >= 1) & (row <= N - 2), 1: row >= 2, -1: row <= N - 3}
    for m in range(4):
        mom[m, 0] = zero
        mom[m, 1] = zero

    def pot(x):
        return gx_lo[x] if x < RING else gx_hi[N - 1 - x] if x >= N - RING else middle[x - RING]

    def step(x):
        here = pl.ds(x, 1)
        p = [held[i, x] for i in range(19)]
        for i in range(19):
            pr_lo[i, here, :] = row_of(p[i], 0)
            pr_hi[i, here, :] = row_of(p[i], N - 1)
        centre = pot(x)
        slopes = (pot(x + 1) - pot(x - 1), roll_y(centre, -1) - roll_y(centre, 1), roll_z(centre, -1) - roll_z(centre, 1))
        post, force = post_of(p, pull[x] < 0.5 * SOLID, pull[x], slopes)
        moved = []
        for i in range(19):
            v = post[i]
            if C[i][2]:
                v = roll_z(v, C[i][2])
            if C[i][1]:
                v = roll_y(v, C[i][1])
            buf[i, x + C[i][0]] = v
            moved.append(v)
        g = sums([(i, moved[i]) for i in range(19) if C[i][0] == 0], keep)
        mom[0, x] += g[0]
        for m in (1, 2, 3):
            w = jnp.where(keep[0], 0.5 * force[m - 1], 0.0)
            mom[m, x] += w if g[m] is None else g[m] + w
        g = sums([(i, moved[i]) for i in XPOS], keep)
        for m in range(4):
            mom[m, x + 1] = g[m]
        g = sums([(i, moved[i]) for i in XNEG], keep)
        for m in range(4):
            mom[m, x - 1] += g[m]

    for s in range(N // CHUNK):
        chunks[s].wait()
        for x in range(max(CHUNK * s, 1), min(CHUNK * s + CHUNK, N - 1)):
            step(x)
    for c in ends:
        c.wait()


def edge_kernel(px_lo, px_hi, pr_lo, pr_hi, gx_lo, gx_hi, gy_lo, gy_hi, fx_lo, fx_hi, fy_lo, fy_hi, mom0,
                mom, ex_lo, ex_hi, ey_lo, ey_hi, yb_lo, yb_hi):
    row = rows()
    inner = (row >= 1) & (row <= N - 2)
    keep = {0: None, 1: row >= 1, -1: row <= N - 2}
    lines = {}
    for pr, gy, fy, ey, low in ((pr_lo, gy_lo, fy_lo, ey_lo, True), (pr_hi, gy_hi, fy_hi, ey_hi, False)):
        centre = gy[0]
        y_slope = gy[1] - fy[0] if low else fy[0] - gy[1]
        slopes = (roll_y(centre, -1) - roll_y(centre, 1), y_slope, roll_z(centre, -1) - roll_z(centre, 1))
        post, force = post_of([pr[i] for i in range(19)], gy[RING + 2] > 0.0, (gy[RING] - gy[RING + 1]) * (-0.001), slopes)
        for i in range(19):
            v = roll_z(post[i], C[i][2]) if C[i][2] else post[i]
            v = jnp.where(inner, v, 0.0)
            ey[i] = v
            if low and C[i][1] == -1:
                q = YNEG.index(i)
                yb_lo[q * N:(q + 1) * N, :] = v
            if not low and C[i][1] == 1:
                q = YPOS.index(i)
                yb_hi[q * N:(q + 1) * N, :] = v
            post[i] = shift_by(v, C[i][0])
        for cy in (0, 1 if low else -1):
            y = (0 if low else N - 1) + cy
            total = [None] * 4
            for i in range(19):
                if C[i][1] == cy:
                    for m, c in enumerate((1,) + C[i]):
                        if c:
                            w = post[i] if c == 1 else -post[i]
                            total[m] = w if total[m] is None else total[m] + w
            if cy == 0:
                for a in range(3):
                    w = jnp.where(inner, 0.5 * force[a], 0.0)
                    total[a + 1] = w if total[a + 1] is None else total[a + 1] + w
            lines[y] = total
    for x in range(N):
        for m in range(4):
            v = mom0[m, x]
            for y in (0, 1, N - 2, N - 1):
                v = v + jnp.where(row == y, spread(row_of(lines[y][m], x)), 0.0)
            mom[m, x] = v
    for px, gx, fx, ex, low in ((px_lo, gx_lo, fx_lo, ex_lo, True), (px_hi, gx_hi, fx_hi, ex_hi, False)):
        at = 0 if low else N - 1
        centre = gx[0]
        x_slope = gx[1] - fx[0] if low else fx[0] - gx[1]
        y_up = jnp.where(row == N - 1, spread(fy_hi[0, at:at + 1, :]), roll_y(centre, -1))
        y_dn = jnp.where(row == 0, spread(fy_lo[0, at:at + 1, :]), roll_y(centre, 1))
        slopes = (x_slope, y_up - y_dn, roll_z(centre, -1) - roll_z(centre, 1))
        post, force = post_of([px[i] for i in range(19)], gx[RING + 2] > 0.0, (gx[RING] - gx[RING + 1]) * (-0.001), slopes)
        for i in range(19):
            v = roll_z(post[i], C[i][2]) if C[i][2] else post[i]
            if C[i][1] == 1:
                v = roll_y(v, 1)
                at_row = YPOS.index(i) * N + at
                yb_hi[at_row:at_row + 1, :] = row_of(v, 0)
                v = jnp.where(row == 0, 0.0, v)
            elif C[i][1] == -1:
                v = roll_y(v, -1)
                at_row = YNEG.index(i) * N + at
                yb_lo[at_row:at_row + 1, :] = row_of(v, N - 1)
                v = jnp.where(row == N - 1, 0.0, v)
            ex[i] = v
            post[i] = v
        none = {0: None, 1: None, -1: None}
        g = sums([(i, post[i]) for i in range(19) if C[i][0] == 0], none)
        mom[0, at] += g[0]
        for m in (1, 2, 3):
            w = 0.5 * force[m - 1]
            mom[m, at] += w if g[m] is None else g[m] + w
        g = sums([(i, post[i]) for i in (XPOS if low else XNEG)], none)
        for m in range(4):
            mom[m, 1 if low else N - 2] += g[m]
        g = sums([(i, post[i]) for i in (XNEG if low else XPOS)], none)
        k = LINE + (2 if low else 0)
        yb_hi[k:k + 1, :] = row_of(g[0], N - 1)
        yb_hi[k + 1:k + 2, :] = row_of(g[2], N - 1)
        yb_lo[k:k + 1, :] = row_of(g[0], 0)
        yb_lo[k + 1:k + 2, :] = row_of(g[2], 0)
    for x in range(N):
        for q, m in ((5, 0), (6, 2)):
            yb_lo[q * N + x:q * N + x + 1, :] = mom[m, x, 0:1, :]
            yb_hi[q * N + x:q * N + x + 1, :] = mom[m, x, N - 1:N, :]
    yb_lo[LINE + 4:, :] = jnp.zeros((4, Z), F32)
    yb_hi[LINE + 4:, :] = jnp.zeros((4, Z), F32)


def plane(ref, q):
    return ref[q * N:(q + 1) * N, :]


def line(ref, q, x):
    return ref[q * N + x:q * N + x + 1, :]


def y_terms(lo, hi):
    s3, s7, s10, s15, s17 = (plane(lo, q) for q in range(5))
    s7, s10 = shift_up(s7), shift_down(s10)
    total = s3 + s7 + s10 + s15 + s17
    below = (total, s7 - s10, total, s15 - s17)
    s4, s8, s9, s16, s18 = (plane(hi, q) for q in range(5))
    s8, s9 = shift_down(s8), shift_up(s9)
    total = s4 + s8 + s9 + s16 + s18
    return below, (total, s9 - s8, -total, s18 - s16)


def corner_kernel(ex_lo, ex_hi, yh_lo, yh_hi, yb_lo, yb_hi, mom, xb_lo, xb_hi):
    row = rows()
    below, above = y_terms(yh_lo, yh_hi)
    for ex, xb, slots, at in ((ex_hi, xb_hi, XPOS, N - 1), (ex_lo, xb_lo, XNEG, 0)):
        for q, i in enumerate(slots):
            v = ex[i]
            if C[i][1] == 1:
                v = jnp.where(row == 0, spread(line(yh_lo, YPOS.index(i), at)), v)
            elif C[i][1] == -1:
                v = jnp.where(row == N - 1, spread(line(yh_hi, YNEG.index(i), at)), v)
            xb[q * N:(q + 1) * N, :] = v
        for q, m in ((5, 0), (6, 1)):
            v = mom[m, at] + jnp.where(row == 0, spread(row_of(below[m], at)), 0.0)
            xb[q * N:(q + 1) * N, :] = v + jnp.where(row == N - 1, spread(row_of(above[m], at)), 0.0)
        c = 1 if at else -1
        k = LINE if at else LINE + 2
        down = line(yb_lo, YNEG.index(9 if c == 1 else 8), at)
        up = line(yb_hi, YPOS.index(7 if c == 1 else 10), at)
        xb[LINE:LINE + 1, :] = yh_lo[k:k + 1, :] + down
        xb[LINE + 1:LINE + 2, :] = yh_lo[k + 1:k + 2, :] - down
        xb[LINE + 2:LINE + 3, :] = yh_hi[k:k + 1, :] + up
        xb[LINE + 3:LINE + 4, :] = yh_hi[k + 1:k + 2, :] + up
        xb[LINE + 4:, :] = jnp.zeros((4, Z), F32)


def velocity(conductance, density, momentum):
    return jnp.where(conductance > 0.0, momentum / density, 0.0)


def full_moment(mom, m, x, below, above):
    v = mom[m, x] + jnp.where(rows() == 0, spread(row_of(below[m], x)), 0.0)
    return v + jnp.where(rows() == N - 1, spread(row_of(above[m], x)), 0.0)


def inner_kernel(charge, classes_h, mob, solid, conc, pot, fx_lo, fx_hi, fy_lo, fy_hi, gy_lo, mom, yh_lo, yh_hi, yb_lo, yb_hi,
                 base, wx, wy, wy_low, wz, wall, cond, drift, src, sy_lo, sy_hi, low, adv, classes, sem):
    fetch = pltpu.make_async_copy(classes_h, classes, sem)
    fetch.start()
    row = rows()

    def faces(ref):
        return tuple(ref[RING + q] for q in range(3)) + (ref[0],)

    rest, weight = flux(faces(fy_lo), faces(gy_lo))
    for s in range(2):
        low[s] = rest[s]
        wy_low[s] = weight[s]
    upper = faces(fy_hi)
    for x in range(N):
        cond[x] = jnp.where(solid[x] == 0, jnp.sqrt(mob[x]), 0.0)
    below, above = y_terms(yh_lo, yh_hi)
    for x in range(1, N - 1):
        scale = jnp.where(cond[x] > 0.0, 1.0 / full_moment(mom, 0, x, below, above), 0.0)
        for a in range(3):
            drift[a, x] = full_moment(mom, a + 1, x, below, above) * scale
    from_hi, from_lo = y_terms(yb_hi, yb_lo)
    dy_lo = velocity(fy_lo[RING + 2], plane(yh_lo, 5) + from_lo[0], plane(yh_lo, 6) + from_lo[2])
    dy_hi = velocity(fy_hi[RING + 2], plane(yh_hi, 5) + from_hi[0], plane(yh_hi, 6) + from_hi[2])
    for x in range(1, N - 1):
        carried = row_of(dy_lo, x) + drift[1, x, 0:1, :]
        for s in range(2):
            adv[s, x:x + 1, :] = wy_low[s, x:x + 1, :] * carried

    def fields(x):
        return (conc[0, x], conc[1, x], cond[x], pot[x])

    behind, weight = flux(faces(fx_lo), fields(0))
    for s in range(2):
        wx[s, 0] = weight[s]
    fetch.wait()
    for x in range(N):
        known = 1 <= x <= N - 2
        me = fields(x)
        ahead, weight = flux(me, fields(x + 1) if x < N - 1 else faces(fx_hi))
        if 1 <= x <= N - 3:
            carried = drift[0, x] + drift[0, x + 1]
            ahead = [ahead[s] + weight[s] * carried for s in range(2)]
        elif x in (0, N - 2):
            for s in range(2):
                wx[s, 1 if x == 0 else 2] = weight[s]
        else:
            for s in range(2):
                wx[s, 3] = weight[s]
        tot = [ahead[s] - behind[s] for s in range(2)]
        behind = ahead
        nxt = tuple(jnp.where(row == N - 1, spread(row_of(upper[q], x)), roll_y(me[q], -1)) for q in range(4))
        rest, weight = flux(me, nxt)
        first = [low[s, x:x + 1, :] for s in range(2)]
        if known:
            v = drift[1, x]
            carried = v + jnp.where(row == N - 1, spread(row_of(dy_hi, x)), roll_y(v, -1))
            rest = [rest[s] + weight[s] * carried for s in range(2)]
            first = [first[s] + adv[s, x:x + 1, :] for s in range(2)]
        else:
            for s in range(2):
                wy[s, x // (N - 1)] = weight[s]
        for s in range(2):
            tot[s] = tot[s] + (rest[s] - jnp.where(row == 0, spread(first[s]), roll_y(rest[s], 1)))
        rest, weight = flux(me, tuple(roll_z(v, -1) for v in me))
        if known:
            v = drift[2, x]
            carried = v + roll_z(v, -1)
            rest = [rest[s] + weight[s] * carried for s in range(2)]
        else:
            for s in range(2):
                wz[s, x // (N - 1)] = weight[s]
        for s in range(2):
            tot[s] = tot[s] + (rest[s] - roll_z(rest[s], 1))
            base[s, x] = me[s] - tot[s]
        cls = classes[x]
        total = jnp.zeros((N, Z), F32)
        for q in range(4):
            total = total + jnp.where(cls == q, charge[q], 0.0)
        if 2 <= x <= N - 3:
            source_plane(x, jnp.where(cond[x] > 0.0, me[0] - tot[0] - (me[1] - tot[1]), total), src, sy_lo, sy_hi)
        else:
            wall[x] = total


def source_plane(x, v, src, sy_lo, sy_hi):
    src[x] = v
    for r in range(RING - 1):
        sy_lo[r, x:x + 1, :] = row_of(v, r)
        sy_hi[r, x:x + 1, :] = row_of(v, N - 1 - r)


def transport_kernel(mom, cond, base, wx, wy, wy_low, wz, wall, drift, src0, sy_lo0, sy_hi0,
                     yh_lo, yh_hi, xh_lo, xh_hi, yb_lo, yb_hi, xb_lo, xb_hi,
                     fx_lo, fx_hi, fy_lo, fy_hi, conc_out, src, sy_lo, sy_hi):
    row = rows()
    below, above = y_terms(yh_lo, yh_hi)
    sy_lo[...] = sy_lo0[...]
    sy_hi[...] = sy_hi0[...]
    for x in range(2, N - 2):
        src[x] = src0[x]
        for s in range(2):
            conc_out[s, x] = base[s, x]
    from_hi, from_lo = y_terms(yb_hi, yb_lo)

    def y_line(fy, yh, terms, k, xh, x):
        density = line(yh, 5, x) + row_of(terms[0], x) + xh[k:k + 1, :]
        momentum = line(yh, 6, x) + row_of(terms[2], x) + xh[k + 1:k + 2, :]
        return velocity(fy[RING + 2, x:x + 1, :], density, momentum)

    for x, near, xh, xb, fx, sign in ((0, 1, xh_lo, xb_lo, fx_lo, 1.0), (N - 1, N - 2, xh_hi, xb_hi, fx_hi, -1.0)):
        a = [plane(xh, q) for q in range(5)]
        total = a[0] + a[1] + a[2] + a[3] + a[4]
        extra = (total, sign * total, sign * (a[1] - a[2]), sign * (a[3] - a[4]))
        full = [full_moment(mom, m, x, below, above) + extra[m] for m in range(4)]
        scale = jnp.where(cond[x] > 0.0, 1.0 / full[0], 0.0)
        d = [full[m] * scale for m in (1, 2, 3)]
        out = plane(xb, 0) + plane(xb, 1) + plane(xb, 2) + plane(xb, 3) + plane(xb, 4)
        beyond = velocity(fx[RING + 2], plane(xh, 5) + out, plane(xh, 6) - sign * out)
        e = x // (N - 1)
        outer = 3 * e
        dy_lo = y_line(fy_lo, yh_lo, from_lo, LINE, xh, x)
        dy_hi = y_line(fy_hi, yh_hi, from_hi, LINE + 2, xh, x)
        c, c_near = [], []
        up = d[1] + jnp.where(row == N - 1, spread(dy_hi), roll_y(d[1], -1))
        turn = d[2] + roll_z(d[2], -1)
        for s in range(2):
            far = wx[s, outer] * (beyond + d[0])
            close = wx[s, 1 + e] * (d[0] + drift[0, near])
            f = wy[s, e] * up
            first = wy_low[s, x:x + 1, :] * (dy_lo + row_of(d[1], 0))
            g = wz[s, e] * turn
            tot = sign * (close - far) + (f - jnp.where(row == 0, spread(first), roll_y(f, 1))) + (g - roll_z(g, 1))
            c.append(base[s, x] - tot)
            c_near.append(base[s, near] + sign * close)
            conc_out[s, x] = c[s]
            conc_out[s, near] = c_near[s]
        source_plane(x, jnp.where(cond[x] > 0.0, c[0] - c[1], wall[x]), src, sy_lo, sy_hi)
        source_plane(near, jnp.where(cond[near] > 0.0, c_near[0] - c_near[1], wall[near]), src, sy_lo, sy_hi)


def split(ext, a, b, pairs, shift):
    shape = (N + 2 * OFF, Z)
    mask = (lax.broadcasted_iota(jnp.int32, shape, 0) + lax.broadcasted_iota(jnp.int32, shape, 1)) % 2 == 0
    for k in pairs:
        p, q = ext[2 * k], ext[2 * k + 1]
        a[k + shift] = jnp.where(mask, p, q)
        b[k + shift] = jnp.where(mask, q, p)


def prepare_kernel(pot, src, fy_lo, fy_hi, ys_lo, ys_hi, even, odd, s_even, s_odd, ext):
    for centre, y_lo, y_hi, depth, a, b in ((pot, fy_lo, fy_hi, RING, even, odd), (src, ys_lo, ys_hi, RING - 1, s_even, s_odd)):
        for x in range(N):
            ext[x, OFF:OFF + N] = centre[x]
            for r in range(depth):
                ext[x, OFF - 1 - r:OFF - r, :] = y_lo[r, x:x + 1, :]
                ext[x, OFF + N + r:OFF + N + r + 1, :] = y_hi[r, x:x + 1, :]
        split(ext, a, b, range(N // 2), 0)


def sweep_kernel(even_in, odd_in, s_even_in, s_odd_in, fx_lo, fx_hi, xs_lo, xs_hi, out, ext, even, odd, s_even, s_odd):
    mid = slice(OFF, OFF + N)
    top = RING + N
    half = (N + 2 * RING) // 2
    shape = (N + 2 * OFF, Z)
    mask = (lax.broadcasted_iota(jnp.int32, shape, 0) + lax.broadcasted_iota(jnp.int32, shape, 1)) % 2 == 0
    zero = jnp.zeros(shape, F32)
    for ref in (even, odd):
        ref[0] = zero
        ref[half + 1] = zero
    for ref, given in ((even, even_in), (odd, odd_in), (s_even, s_even_in), (s_odd, s_odd_in)):
        for k in range(N // 2):
            ref[k + 1 + RING // 2] = given[k]
    ends = list(range(RING // 2)) + list(range(RING // 2 + N // 2, half))
    for x_lo, x_hi, depth, listed, a, b in (
            (lambda r: fx_lo[r], lambda r: fx_hi[r], RING, POT_ROWS, even, odd),
            (lambda r: plane(xs_lo, r), lambda r: plane(xs_hi, r), RING - 1, SRC_ROWS, s_even, s_odd)):
        for r in range(depth):
            ext[RING - 1 - r, mid] = x_lo(r)
            ext[top + r, mid] = x_hi(r)
        for at, a_ring, side, b_ring in listed:
            y = OFF + N + b_ring - 1 if side else OFF - b_ring
            ext[RING - a_ring, y:y + 1, :] = xs_lo[at:at + 1, :]
            ext[top + a_ring - 1, y:y + 1, :] = xs_hi[at:at + 1, :]
        split(ext, a, b, ends, 1)

    for h in range(6):
        this, other, s = (even, odd, s_even) if h % 2 == 0 else (odd, even, s_odd)

        def update(k, carry, h=h, this=this, other=other, s=s):
            c = other[k]
            before, after = other[k - 1], other[k + 1]
            far = jnp.where(mask, before, after) if h % 2 == 0 else jnp.where(mask, after, before)
            nb = (c + far) + (roll_y(c, 1) + roll_y(c, -1)) + (roll_z(c, 1) + roll_z(c, -1))
            this[k] = -0.6 * this[k] + (1.6 / 6.0) * (nb + s[k])
            return carry

        lo = (h + 1) // 2
        for k in range(lo + 1, half - lo + 1):
            update(k, 0)

    def last(k, carry):
        p, q = even[k], odd[k]
        out[2 * (k - 1) - RING] = jnp.where(mask, p, q)[OFF:OFF + N]
        out[2 * (k - 1) - RING + 1] = jnp.where(mask, q, p)[OFF:OFF + N]
        return carry

    lax.fori_loop(RING // 2 + 1, RING // 2 + N // 2 + 1, last, 0)


def patch_kernel(buf, ex_lo, ex_hi, ey_lo, ey_hi, yh_lo, yh_hi, xh_lo, xh_hi, conc, out, conc_out, done, sems):
    row = rows()
    copies = [pltpu.make_async_copy(conc, conc_out, sems.at[19])]
    copies[0].start()
    for i in range(19):
        cx, cy, _ = C[i]

        def halo(v, src, i=i, cy=cy):
            if cy == 1:
                return jnp.where(row == 0, spread(yh_lo[pl.ds(YPOS.index(i) * N + src, 1), :]), v)
            if cy == -1:
                return jnp.where(row == N - 1, spread(yh_hi[pl.ds(YNEG.index(i) * N + src, 1), :]), v)
            return v

        def inner(src, carry, i=i, cx=cx, cy=cy, halo=halo):
            here = pl.ds(src, 1)
            v = buf[i, src + cx]
            if cy != -1:
                v = jnp.where(row == cy, spread(ey_lo[i, here, :]), v)
            if cy != 1:
                v = jnp.where(row == N - 1 + cy, spread(ey_hi[i, here, :]), v)
            done[i, src + cx] = halo(v, src)
            return carry

        lax.fori_loop(1, N - 1, inner, 0, unroll=True)
        if cx != -1:
            done[i, cx] = halo(ex_lo[i], 0)
        if cx != 1:
            done[i, N - 1 + cx] = halo(ex_hi[i], N - 1)
        if cx == 1:
            done[i, 0] = plane(xh_lo, XPOS.index(i))
        if cx == -1:
            done[i, N - 1] = plane(xh_hi, XNEG.index(i))
        copy = pltpu.make_async_copy(done.at[i], out.at[i], sems.at[i])
        copy.start()
        copies.append(copy)
    for copy in copies:
        copy.wait()


def flux(a, b):
    link = a[2] * b[2]
    drop = a[3] - b[3]
    rest, weight = [], []
    for s in range(2):
        both = a[s] + b[s]
        rest.append(link * (RATES[s] * ((a[s] - b[s]) + ((0.5 * VAL[s]) * both) * drop)))
        weight.append((0.25 * link) * both)
    return rest, weight


def ring_rows(depth, total):
    listed = []
    at = depth
    for a in range(1, total):
        for side in (0, 1):
            for b in range(1, total - a + 1):
                listed.append((at, a, side, b))
                at += 1
    return listed


SRC_ROWS = ring_rows((RING - 1) * N, RING - 1)
POT_ROWS = ring_rows(SRC_ROWS[-1][0] + 1, RING)
SRC_LEN = 136


def pack_src_kernel(src, ys_lo, ys_hi, fy_lo, fy_hi, o_hi, o_lo):
    for k in range(RING - 1):
        o_hi[k * N:(k + 1) * N, :] = src[N - 1 - k]
        o_lo[k * N:(k + 1) * N, :] = src[k]
    for listed, lo, hi in ((SRC_ROWS, ys_lo, ys_hi), (POT_ROWS, fy_lo, fy_hi)):
        for at, a, side, b in listed:
            halo = hi if side else lo
            o_hi[at:at + 1, :] = halo[b - 1, N - a:N - a + 1, :]
            o_lo[at:at + 1, :] = halo[b - 1, a - 1:a, :]
    end = POT_ROWS[-1][0] + 1
    o_hi[end:, :] = jnp.zeros((SRC_LEN - end, Z), F32)
    o_lo[end:, :] = jnp.zeros((SRC_LEN - end, Z), F32)


def swap(axis, hi, lo):
    n = lax.axis_size(axis)
    even = lax.axis_index(axis) % 2 == 0
    first = lax.ppermute(jnp.where(even, hi, lo), axis, [(i, i + 1 - 2 * (i % 2)) for i in range(n)])
    second = lax.ppermute(jnp.where(even, lo, hi), axis, [(i, (i - 1 + 2 * (i % 2)) % n) for i in range(n)])
    return jnp.where(even, second, first), jnp.where(even, first, second)


def body(pops, conc, pot, mob, solid, classes, charge):
    cube = sds(N, N, Z)
    msg = sds(ROWS, Z)
    gx_hi, gx_lo, gy_hi, gy_lo, pull, middle = call(
        faces_kernel, [sds(RING + 3, N, Z)] * 4 + [cube, sds(N - 2 * RING, N, Z)], "faces", "hhhh",
        scratch=[VM((N, N, Z), F32), VM((N, N, Z), F32), VM((2, N, N, Z), F32), VM((N, N, Z), F32),
                 VM((N, N, Z), jnp.int32),
                 pltpu.SemaphoreType.DMA((4,))], mib=53, moved=2600000)(
        pot, conc, mob, solid)
    fx_lo, fx_hi = swap("gx", gx_hi, gx_lo)
    fy_lo, fy_hi = swap("gy", gy_hi, gy_lo)
    chunks = N // CHUNK
    buf, mom, px_lo, px_hi, pr_lo, pr_hi = call(
        collide_kernel, [sds(19, N, N, Z), sds(4, N, N, Z)] + [sds(19, N, Z)] * 4, "collide", "hvvvv",
        scratch=[VM((19, N, N, Z), F32), pltpu.SemaphoreType.DMA((chunks,)), pltpu.SemaphoreType.DMA((2,))],
        mib=43, flops=20000000, moved=14000000)(pops, gx_hi, gx_lo, middle, pull)
    mom, ex_lo, ex_hi, ey_lo, ey_hi, yb_lo, yb_hi = call(
        edge_kernel, [sds(4, N, N, Z)] + [sds(19, N, Z)] * 4 + [msg, msg], "edge", "v" * 13, moved=3000000)(
        px_lo, px_hi, pr_lo, pr_hi, gx_lo, gx_hi, gy_lo, gy_hi, fx_lo, fx_hi, fy_lo, fy_hi, mom)
    yh_lo, yh_hi = swap("gy", yb_hi, yb_lo)
    xb_lo, xb_hi = call(corner_kernel, [msg, msg], "corner", "v" * 7)(ex_lo, ex_hi, yh_lo, yh_hi, yb_lo, yb_hi, mom)
    xh_lo, xh_hi = swap("gx", xb_hi, xb_lo)
    fy_late, _ = lax.optimization_barrier((fy_lo, yh_lo))
    pair = sds(2, N, N, Z)
    ring = sds(RING - 1, N, Z)
    base, wx, wy, wy_low, wz, wall, cond, drift, src, sy_lo, sy_hi = call(
        inner_kernel, [pair, sds(2, 4, N, Z), sds(2, 2, N, Z), sds(2, N, Z), sds(2, 2, N, Z), cube, cube, sds(3, N, N, Z), cube, ring, ring],
        "inner", "sh" + "v" * 14,
        scratch=[VM((2, N, Z), F32), VM((2, N, Z), F32), VM((N, N, Z), jnp.int32), pltpu.SemaphoreType.DMA],
        flops=10000000, moved=6000000)(
        charge, classes, mob, solid, conc, pot, fx_lo, fx_hi, fy_late, fy_hi, gy_lo, mom, yh_lo, yh_hi, yb_lo, yb_hi)
    conc_new, src, sy_lo, sy_hi = call(
        transport_kernel, [pair, cube, ring, ring], "transport", "v" * 24, flops=3000000, moved=4000000)(
        mom, cond, base, wx, wy, wy_low, wz, wall, drift, src, sy_lo, sy_hi,
        yh_lo, yh_hi, xh_lo, xh_hi, yb_lo, yb_hi, xb_lo, xb_hi, fx_lo, fx_hi, fy_lo, fy_hi)
    ys_lo, ys_hi = swap("gy", sy_hi, sy_lo)
    bs_hi, bs_lo = call(pack_src_kernel, [sds(SRC_LEN, Z)] * 2, "pack_src", "v" * 5)(src, ys_lo, ys_hi, fy_lo, fy_hi)
    xs_lo, xs_hi = swap("gx", bs_hi, bs_lo)
    packed = VM(((N + 2 * RING) // 2 + 2, N + 2 * OFF, Z), F32)
    prepared = call(
        prepare_kernel, [sds(N // 2, N + 2 * OFF, Z)] * 4, "prepare", "v" * 6,
        scratch=[VM((N, N + 2 * OFF, Z), F32)], flops=1000000, moved=4000000)(pot, src, fy_lo, fy_hi, ys_lo, ys_hi)
    potential_out = call(
        sweep_kernel, [cube], "sweep", "v" * 8,
        scratch=[VM((N + 2 * RING, N + 2 * OFF, Z), F32)] + [packed] * 4, flops=20000000, moved=4000000)(
        *prepared, fx_lo, fx_hi, xs_lo, xs_hi)[0]
    pop, conc_out = call(
        patch_kernel, [sds(19, N, N, Z), pair], "patch", "v" * 10, out_specs="hh",
        scratch=[VM((19, N, N, Z), F32), pltpu.SemaphoreType.DMA((20,))], mib=16, moved=10000000)(
        buf, ex_lo, ex_hi, ey_lo, ey_hi, yh_lo, yh_hi, xh_lo, xh_hi, conc_new)
    return (pop, conc_out, potential_out)


def solution(mesh):
    lattice = P(None, "gx", "gy", None)
    flat = P("gx", "gy", None)
    return jax.shard_map(
        body, mesh=mesh, in_specs=(lattice, lattice, flat, flat, flat, flat, P()),
        out_specs=(lattice, lattice, flat), check_vma=False)
```

```python
import jax
import jax.numpy as jnp
from jax import lax
from jax.experimental import pallas as pl
from jax.experimental.pallas import tpu as pltpu
from jax.sharding import PartitionSpec as P

C = [(0, 0, 0), (1, 0, 0), (-1, 0, 0), (0, 1, 0), (0, -1, 0), (0, 0, 1), (0, 0, -1),
     (1, 1, 0), (-1, -1, 0), (1, -1, 0), (-1, 1, 0), (1, 0, 1), (-1, 0, -1), (1, 0, -1), (-1, 0, 1),
     (0, 1, 1), (0, -1, -1), (0, 1, -1), (0, -1, 1)]
W = [1.0 / 3.0] + [1.0 / 18.0] * 6 + [1.0 / 36.0] * 12
XPOS = [i for i in range(19) if C[i][0] == 1]
XNEG = [i for i in range(19) if C[i][0] == -1]
YPOS = [i for i in range(19) if C[i][1] == 1]
YNEG = [i for i in range(19) if C[i][1] == -1]
RATES = (0.06, 0.08)
VAL = (1.0, -1.0)
N = 16
Z = 256
CHUNK = 4
RING = 6
OFF = 8
ROWS = 7 * N + 8
LINE = 7 * N
SOLID = 1.0
F32 = jnp.float32
VM = pltpu.VMEM


def sds(*shape):
    return jax.ShapeDtypeStruct(shape, F32)


def params(mib):
    return pltpu.CompilerParams(vmem_limit_bytes=mib * 1024 * 1024)


def rows():
    return lax.broadcasted_iota(jnp.int32, (N, Z), 0)


def roll_y(v, s):
    return pltpu.roll(v, s % v.shape[0], 0)


def roll_z(v, s):
    return pltpu.roll(v, s % v.shape[1], 1)


def row_of(v, y):
    return v[y:y + 1, :]


def spread(row):
    return jnp.broadcast_to(row, (N, Z))


def shift_up(v):
    return jnp.where(rows() == 0, 0.0, roll_y(v, 1))


def shift_down(v):
    return jnp.where(rows() == N - 1, 0.0, roll_y(v, -1))


def shift_by(v, c):
    return shift_up(v) if c == 1 else shift_down(v) if c == -1 else v


def call(kernel, outs, name, specs, scratch=(), mib=16, flops=0, out_specs=None, moved=0):
    return pl.pallas_call(
        kernel,
        in_specs=[pl.BlockSpec(memory_space={"v": VM, "h": pltpu.HBM, "s": pltpu.SMEM}[c]) for c in specs],
        out_specs=[pl.BlockSpec(memory_space={"v": VM, "h": pltpu.HBM}[c]) for c in out_specs or "v" * len(outs)],
        out_shape=outs,
        scratch_shapes=list(scratch),
        compiler_params=params(mib),
        cost_estimate=pl.CostEstimate(flops=flops, bytes_accessed=moved, transcendentals=0),
        name=name,
    )


def faces_kernel(pot_h, conc_h, mob_h, solid_h, gx_hi, gx_lo, gy_hi, gy_lo, pull, middle, pot, cond, conc, mob, solid, sems):
    pairs = ((pot_h, pot), (conc_h, conc), (mob_h, mob), (solid_h, solid))
    copies = [pltpu.make_async_copy(a, b, sems.at[q]) for q, (a, b) in enumerate(pairs)]
    for c in copies:
        c.start()
    for c in copies:
        c.wait()

    def step(x, carry):
        here = pl.ds(x, 1)
        is_fluid = solid[x] == 0
        cond[x] = jnp.where(is_fluid, jnp.sqrt(mob[x]), 0.0)
        pull[x] = jnp.where(is_fluid, (conc[0, x] - conc[1, x]) * (-0.001), SOLID)
        for r in range(RING):
            gy_hi[r, here, :] = pot[x, N - 1 - r:N - r, :]
            gy_lo[r, here, :] = pot[x, r:r + 1, :]
        for q, v in ((0, conc.at[0]), (1, conc.at[1]), (2, cond)):
            gy_hi[RING + q, here, :] = v[x, N - 1:N, :]
            gy_lo[RING + q, here, :] = v[x, 0:1, :]
        return carry

    lax.fori_loop(0, N, step, 0, unroll=True)
    for x in range(RING, N - RING):
        middle[x - RING] = pot[x]
    for x, face in ((N - 1, gx_hi), (0, gx_lo)):
        for r in range(RING):
            face[r] = pot[abs(x - r)]
        face[RING] = conc[0, x]
        face[RING + 1] = conc[1, x]
        face[RING + 2] = cond[x]


def post_of(p, fluid, q, slopes):
    pull = jnp.where(fluid, q, 0.0)
    force = [pull * d for d in slopes]
    density = p[0]
    for i in range(1, 19):
        density = density + p[i]
    inv = 1.0 / density
    u = []
    for a in range(3):
        total = 0.9 * force[a]
        for i in range(1, 19, 2):
            if C[i][a]:
                term = p[i] - p[i + 1]
                total = total + term if C[i][a] == 1 else total - term
        u.append(total * inv)
    base = 1.0 - 1.5 * (u[0] * u[0] + u[1] * u[1] + u[2] * u[2])
    scaled = density * (10.0 / 9.0)
    out = [jnp.where(fluid, (W[0] * scaled) * base - p[0] * (1.0 / 9.0), p[0])]
    for i in range(1, 19, 2):
        along = None
        for a in range(3):
            if C[i][a]:
                term = u[a] if C[i][a] == 1 else -u[a]
                along = term if along is None else along + term
        even = base + 4.5 * along * along
        odd = 3.0 * along
        ws = W[i] * scaled
        fwd = ws * (even + odd) - p[i] * (1.0 / 9.0)
        bwd = ws * (even - odd) - p[i + 1] * (1.0 / 9.0)
        out.append(jnp.where(fluid, fwd, p[i + 1]))
        out.append(jnp.where(fluid, bwd, p[i]))
    return out, force


def sums(values, keep):
    total = [None] * 4
    for cy in (0, 1, -1):
        part = [None] * 4
        for i, v in values:
            if C[i][1] != cy:
                continue
            for m, c in enumerate((1,) + C[i]):
                if c and m != 2:
                    w = v if c == 1 else -v
                    part[m] = w if part[m] is None else part[m] + w
        for m in (0, 1, 3):
            if part[m] is None:
                continue
            w = part[m] if keep[cy] is None else jnp.where(keep[cy], part[m], 0.0)
            total[m] = w if total[m] is None else total[m] + w
            if m == 0 and cy:
                w = w if cy == 1 else -w
                total[2] = w if total[2] is None else total[2] + w
    return total


def collide_kernel(pops, gx_hi, gx_lo, middle, pull, buf, mom, px_lo, px_hi, pr_lo, pr_hi, held, sems, psems):
    chunks = [pltpu.make_async_copy(pops.at[:, pl.ds(CHUNK * s, CHUNK)], held.at[:, pl.ds(CHUNK * s, CHUNK)], sems.at[s])
              for s in range(N // CHUNK)]
    ends = [pltpu.make_async_copy(pops.at[:, 0], px_lo, psems.at[0]),
            pltpu.make_async_copy(pops.at[:, N - 1], px_hi, psems.at[1])]
    for c in chunks + ends:
        c.start()
    row = rows()
    zero = jnp.zeros((N, Z), F32)
    keep = {0: (row >= 1) & (row <= N - 2), 1: row >= 2, -1: row <= N - 3}
    for m in range(4):
        mom[m, 0] = zero
        mom[m, 1] = zero

    def pot(x):
        return gx_lo[x] if x < RING else gx_hi[N - 1 - x] if x >= N - RING else middle[x - RING]

    def step(x):
        here = pl.ds(x, 1)
        p = [held[i, x] for i in range(19)]
        for i in range(19):
            pr_lo[i, here, :] = row_of(p[i], 0)
            pr_hi[i, here, :] = row_of(p[i], N - 1)
        centre = pot(x)
        slopes = (pot(x + 1) - pot(x - 1), roll_y(centre, -1) - roll_y(centre, 1), roll_z(centre, -1) - roll_z(centre, 1))
        post, force = post_of(p, pull[x] < 0.5 * SOLID, pull[x], slopes)
        moved = []
        for i in range(19):
            v = post[i]
            if C[i][2]:
                v = roll_z(v, C[i][2])
            if C[i][1]:
                v = roll_y(v, C[i][1])
            buf[i, x + C[i][0]] = v
            moved.append(v)
        g = sums([(i, moved[i]) for i in range(19) if C[i][0] == 0], keep)
        mom[0, x] += g[0]
        for m in (1, 2, 3):
            w = jnp.where(keep[0], 0.5 * force[m - 1], 0.0)
            mom[m, x] += w if g[m] is None else g[m] + w
        g = sums([(i, moved[i]) for i in XPOS], keep)
        for m in range(4):
            mom[m, x + 1] = g[m]
        g = sums([(i, moved[i]) for i in XNEG], keep)
        for m in range(4):
            mom[m, x - 1] += g[m]

    for s in range(N // CHUNK):
        chunks[s].wait()
        for x in range(max(CHUNK * s, 1), min(CHUNK * s + CHUNK, N - 1)):
            step(x)
    for c in ends:
        c.wait()


def edge_kernel(px_lo, px_hi, pr_lo, pr_hi, gx_lo, gx_hi, gy_lo, gy_hi, fx_lo, fx_hi, fy_lo, fy_hi, mom0,
                mom, ex_lo, ex_hi, ey_lo, ey_hi, yb_lo, yb_hi):
    row = rows()
    inner = (row >= 1) & (row <= N - 2)
    keep = {0: None, 1: row >= 1, -1: row <= N - 2}
    lines = {}
    for pr, gy, fy, ey, low in ((pr_lo, gy_lo, fy_lo, ey_lo, True), (pr_hi, gy_hi, fy_hi, ey_hi, False)):
        centre = gy[0]
        y_slope = gy[1] - fy[0] if low else fy[0] - gy[1]
        slopes = (roll_y(centre, -1) - roll_y(centre, 1), y_slope, roll_z(centre, -1) - roll_z(centre, 1))
        post, force = post_of([pr[i] for i in range(19)], gy[RING + 2] > 0.0, (gy[RING] - gy[RING + 1]) * (-0.001), slopes)
        for i in range(19):
            v = roll_z(post[i], C[i][2]) if C[i][2] else post[i]
            v = jnp.where(inner, v, 0.0)
            ey[i] = v
            if low and C[i][1] == -1:
                q = YNEG.index(i)
                yb_lo[q * N:(q + 1) * N, :] = v
            if not low and C[i][1] == 1:
                q = YPOS.index(i)
                yb_hi[q * N:(q + 1) * N, :] = v
            post[i] = shift_by(v, C[i][0])
        for cy in (0, 1 if low else -1):
            y = (0 if low else N - 1) + cy
            total = [None] * 4
            for i in range(19):
                if C[i][1] == cy:
                    for m, c in enumerate((1,) + C[i]):
                        if c:
                            w = post[i] if c == 1 else -post[i]
                            total[m] = w if total[m] is None else total[m] + w
            if cy == 0:
                for a in range(3):
                    w = jnp.where(inner, 0.5 * force[a], 0.0)
                    total[a + 1] = w if total[a + 1] is None else total[a + 1] + w
            lines[y] = total
    for x in range(N):
        for m in range(4):
            v = mom0[m, x]
            for y in (0, 1, N - 2, N - 1):
                v = v + jnp.where(row == y, spread(row_of(lines[y][m], x)), 0.0)
            mom[m, x] = v
    for px, gx, fx, ex, low in ((px_lo, gx_lo, fx_lo, ex_lo, True), (px_hi, gx_hi, fx_hi, ex_hi, False)):
        at = 0 if low else N - 1
        centre = gx[0]
        x_slope = gx[1] - fx[0] if low else fx[0] - gx[1]
        y_up = jnp.where(row == N - 1, spread(fy_hi[0, at:at + 1, :]), roll_y(centre, -1))
        y_dn = jnp.where(row == 0, spread(fy_lo[0, at:at + 1, :]), roll_y(centre, 1))
        slopes = (x_slope, y_up - y_dn, roll_z(centre, -1) - roll_z(centre, 1))
        post, force = post_of([px[i] for i in range(19)], gx[RING + 2] > 0.0, (gx[RING] - gx[RING + 1]) * (-0.001), slopes)
        for i in range(19):
            v = roll_z(post[i], C[i][2]) if C[i][2] else post[i]
            if C[i][1] == 1:
                v = roll_y(v, 1)
                at_row = YPOS.index(i) * N + at
                yb_hi[at_row:at_row + 1, :] = row_of(v, 0)
                v = jnp.where(row == 0, 0.0, v)
            elif C[i][1] == -1:
                v = roll_y(v, -1)
                at_row = YNEG.index(i) * N + at
                yb_lo[at_row:at_row + 1, :] = row_of(v, N - 1)
                v = jnp.where(row == N - 1, 0.0, v)
            ex[i] = v
            post[i] = v
        none = {0: None, 1: None, -1: None}
        g = sums([(i, post[i]) for i in range(19) if C[i][0] == 0], none)
        mom[0, at] += g[0]
        for m in (1, 2, 3):
            w = 0.5 * force[m - 1]
            mom[m, at] += w if g[m] is None else g[m] + w
        g = sums([(i, post[i]) for i in (XPOS if low else XNEG)], none)
        for m in range(4):
            mom[m, 1 if low else N - 2] += g[m]
        g = sums([(i, post[i]) for i in (XNEG if low else XPOS)], none)
        k = LINE + (2 if low else 0)
        yb_hi[k:k + 1, :] = row_of(g[0], N - 1)
        yb_hi[k + 1:k + 2, :] = row_of(g[2], N - 1)
        yb_lo[k:k + 1, :] = row_of(g[0], 0)
        yb_lo[k + 1:k + 2, :] = row_of(g[2], 0)
    for x in range(N):
        for q, m in ((5, 0), (6, 2)):
            yb_lo[q * N + x:q * N + x + 1, :] = mom[m, x, 0:1, :]
            yb_hi[q * N + x:q * N + x + 1, :] = mom[m, x, N - 1:N, :]
    yb_lo[LINE + 4:, :] = jnp.zeros((4, Z), F32)
    yb_hi[LINE + 4:, :] = jnp.zeros((4, Z), F32)


def plane(ref, q):
    return ref[q * N:(q + 1) * N, :]


def line(ref, q, x):
    return ref[q * N + x:q * N + x + 1, :]


def y_terms(lo, hi):
    s3, s7, s10, s15, s17 = (plane(lo, q) for q in range(5))
    s7, s10 = shift_up(s7), shift_down(s10)
    total = s3 + s7 + s10 + s15 + s17
    below = (total, s7 - s10, total, s15 - s17)
    s4, s8, s9, s16, s18 = (plane(hi, q) for q in range(5))
    s8, s9 = shift_down(s8), shift_up(s9)
    total = s4 + s8 + s9 + s16 + s18
    return below, (total, s9 - s8, -total, s18 - s16)


def corner_kernel(ex_lo, ex_hi, yh_lo, yh_hi, yb_lo, yb_hi, mom, xb_lo, xb_hi):
    row = rows()
    below, above = y_terms(yh_lo, yh_hi)
    for ex, xb, slots, at in ((ex_hi, xb_hi, XPOS, N - 1), (ex_lo, xb_lo, XNEG, 0)):
        for q, i in enumerate(slots):
            v = ex[i]
            if C[i][1] == 1:
                v = jnp.where(row == 0, spread(line(yh_lo, YPOS.index(i), at)), v)
            elif C[i][1] == -1:
                v = jnp.where(row == N - 1, spread(line(yh_hi, YNEG.index(i), at)), v)
            xb[q * N:(q + 1) * N, :] = v
        for q, m in ((5, 0), (6, 1)):
            v = mom[m, at] + jnp.where(row == 0, spread(row_of(below[m], at)), 0.0)
            xb[q * N:(q + 1) * N, :] = v + jnp.where(row == N - 1, spread(row_of(above[m], at)), 0.0)
        c = 1 if at else -1
        k = LINE if at else LINE + 2
        down = line(yb_lo, YNEG.index(9 if c == 1 else 8), at)
        up = line(yb_hi, YPOS.index(7 if c == 1 else 10), at)
        xb[LINE:LINE + 1, :] = yh_lo[k:k + 1, :] + down
        xb[LINE + 1:LINE + 2, :] = yh_lo[k + 1:k + 2, :] - down
        xb[LINE + 2:LINE + 3, :] = yh_hi[k:k + 1, :] + up
        xb[LINE + 3:LINE + 4, :] = yh_hi[k + 1:k + 2, :] + up
        xb[LINE + 4:, :] = jnp.zeros((4, Z), F32)


def velocity(conductance, density, momentum):
    return jnp.where(conductance > 0.0, momentum / density, 0.0)


def full_moment(mom, m, x, below, above):
    v = mom[m, x] + jnp.where(rows() == 0, spread(row_of(below[m], x)), 0.0)
    return v + jnp.where(rows() == N - 1, spread(row_of(above[m], x)), 0.0)


def inner_kernel(charge, classes_h, mob, solid, conc, pot, fx_lo, fx_hi, fy_lo, fy_hi, gy_lo, mom, yh_lo, yh_hi, yb_lo, yb_hi,
                 base, wx, wy, wy_low, wz, wall, cond, drift, src, sy_lo, sy_hi, low, adv, classes, sem):
    fetch = pltpu.make_async_copy(classes_h, classes, sem)
    fetch.start()
    row = rows()

    def faces(ref):
        return tuple(ref[RING + q] for q in range(3)) + (ref[0],)

    rest, weight = flux(faces(fy_lo), faces(gy_lo))
    for s in range(2):
        low[s] = rest[s]
        wy_low[s] = weight[s]
    upper = faces(fy_hi)
    for x in range(N):
        cond[x] = jnp.where(solid[x] == 0, jnp.sqrt(mob[x]), 0.0)
    below, above = y_terms(yh_lo, yh_hi)
    for x in range(1, N - 1):
        scale = jnp.where(cond[x] > 0.0, 1.0 / full_moment(mom, 0, x, below, above), 0.0)
        for a in range(3):
            drift[a, x] = full_moment(mom, a + 1, x, below, above) * scale
    from_hi, from_lo = y_terms(yb_hi, yb_lo)
    dy_lo = velocity(fy_lo[RING + 2], plane(yh_lo, 5) + from_lo[0], plane(yh_lo, 6) + from_lo[2])
    dy_hi = velocity(fy_hi[RING + 2], plane(yh_hi, 5) + from_hi[0], plane(yh_hi, 6) + from_hi[2])
    for x in range(1, N - 1):
        carried = row_of(dy_lo, x) + drift[1, x, 0:1, :]
        for s in range(2):
            adv[s, x:x + 1, :] = wy_low[s, x:x + 1, :] * carried

    def fields(x):
        return (conc[0, x], conc[1, x], cond[x], pot[x])

    behind, weight = flux(faces(fx_lo), fields(0))
    for s in range(2):
        wx[s, 0] = weight[s]
    fetch.wait()
    for x in range(N):
        known = 1 <= x <= N - 2
        me = fields(x)
        ahead, weight = flux(me, fields(x + 1) if x < N - 1 else faces(fx_hi))
        if 1 <= x <= N - 3:
            carried = drift[0, x] + drift[0, x + 1]
            ahead = [ahead[s] + weight[s] * carried for s in range(2)]
        elif x in (0, N - 2):
            for s in range(2):
                wx[s, 1 if x == 0 else 2] = weight[s]
        else:
            for s in range(2):
                wx[s, 3] = weight[s]
        tot = [ahead[s] - behind[s] for s in range(2)]
        behind = ahead
        nxt = tuple(jnp.where(row == N - 1, spread(row_of(upper[q], x)), roll_y(me[q], -1)) for q in range(4))
        rest, weight = flux(me, nxt)
        first = [low[s, x:x + 1, :] for s in range(2)]
        if known:
            v = drift[1, x]
            carried = v + jnp.where(row == N - 1, spread(row_of(dy_hi, x)), roll_y(v, -1))
            rest = [rest[s] + weight[s] * carried for s in range(2)]
            first = [first[s] + adv[s, x:x + 1, :] for s in range(2)]
        else:
            for s in range(2):
                wy[s, x // (N - 1)] = weight[s]
        for s in range(2):
            tot[s] = tot[s] + (rest[s] - jnp.where(row == 0, spread(first[s]), roll_y(rest[s], 1)))
        rest, weight = flux(me, tuple(roll_z(v, -1) for v in me))
        if known:
            v = drift[2, x]
            carried = v + roll_z(v, -1)
            rest = [rest[s] + weight[s] * carried for s in range(2)]
        else:
            for s in range(2):
                wz[s, x // (N - 1)] = weight[s]
        for s in range(2):
            tot[s] = tot[s] + (rest[s] - roll_z(rest[s], 1))
            base[s, x] = me[s] - tot[s]
        cls = classes[x]
        total = jnp.zeros((N, Z), F32)
        for q in range(4):
            total = total + jnp.where(cls == q, charge[q], 0.0)
        if 2 <= x <= N - 3:
            source_plane(x, jnp.where(cond[x] > 0.0, me[0] - tot[0] - (me[1] - tot[1]), total), src, sy_lo, sy_hi)
        else:
            wall[x] = total


def source_plane(x, v, src, sy_lo, sy_hi):
    src[x] = v
    for r in range(RING - 1):
        sy_lo[r, x:x + 1, :] = row_of(v, r)
        sy_hi[r, x:x + 1, :] = row_of(v, N - 1 - r)


def transport_kernel(mom, cond, base, wx, wy, wy_low, wz, wall, drift, src0, sy_lo0, sy_hi0,
                     yh_lo, yh_hi, xh_lo, xh_hi, yb_lo, yb_hi, xb_lo, xb_hi,
                     fx_lo, fx_hi, fy_lo, fy_hi, conc_out, src, sy_lo, sy_hi):
    row = rows()
    below, above = y_terms(yh_lo, yh_hi)
    sy_lo[...] = sy_lo0[...]
    sy_hi[...] = sy_hi0[...]
    for x in range(2, N - 2):
        src[x] = src0[x]
        for s in range(2):
            conc_out[s, x] = base[s, x]
    from_hi, from_lo = y_terms(yb_hi, yb_lo)

    def y_line(fy, yh, terms, k, xh, x):
        density = line(yh, 5, x) + row_of(terms[0], x) + xh[k:k + 1, :]
        momentum = line(yh, 6, x) + row_of(terms[2], x) + xh[k + 1:k + 2, :]
        return velocity(fy[RING + 2, x:x + 1, :], density, momentum)

    for x, near, xh, xb, fx, sign in ((0, 1, xh_lo, xb_lo, fx_lo, 1.0), (N - 1, N - 2, xh_hi, xb_hi, fx_hi, -1.0)):
        a = [plane(xh, q) for q in range(5)]
        total = a[0] + a[1] + a[2] + a[3] + a[4]
        extra = (total, sign * total, sign * (a[1] - a[2]), sign * (a[3] - a[4]))
        full = [full_moment(mom, m, x, below, above) + extra[m] for m in range(4)]
        scale = jnp.where(cond[x] > 0.0, 1.0 / full[0], 0.0)
        d = [full[m] * scale for m in (1, 2, 3)]
        out = plane(xb, 0) + plane(xb, 1) + plane(xb, 2) + plane(xb, 3) + plane(xb, 4)
        beyond = velocity(fx[RING + 2], plane(xh, 5) + out, plane(xh, 6) - sign * out)
        e = x // (N - 1)
        outer = 3 * e
        dy_lo = y_line(fy_lo, yh_lo, from_lo, LINE, xh, x)
        dy_hi = y_line(fy_hi, yh_hi, from_hi, LINE + 2, xh, x)
        c, c_near = [], []
        up = d[1] + jnp.where(row == N - 1, spread(dy_hi), roll_y(d[1], -1))
        turn = d[2] + roll_z(d[2], -1)
        for s in range(2):
            far = wx[s, outer] * (beyond + d[0])
            close = wx[s, 1 + e] * (d[0] + drift[0, near])
            f = wy[s, e] * up
            first = wy_low[s, x:x + 1, :] * (dy_lo + row_of(d[1], 0))
            g = wz[s, e] * turn
            tot = sign * (close - far) + (f - jnp.where(row == 0, spread(first), roll_y(f, 1))) + (g - roll_z(g, 1))
            c.append(base[s, x] - tot)
            c_near.append(base[s, near] + sign * close)
            conc_out[s, x] = c[s]
            conc_out[s, near] = c_near[s]
        source_plane(x, jnp.where(cond[x] > 0.0, c[0] - c[1], wall[x]), src, sy_lo, sy_hi)
        source_plane(near, jnp.where(cond[near] > 0.0, c_near[0] - c_near[1], wall[near]), src, sy_lo, sy_hi)


def split(ext, a, b, pairs, shift):
    shape = (N + 2 * OFF, Z)
    mask = (lax.broadcasted_iota(jnp.int32, shape, 0) + lax.broadcasted_iota(jnp.int32, shape, 1)) % 2 == 0
    for k in pairs:
        p, q = ext[2 * k], ext[2 * k + 1]
        a[k + shift] = jnp.where(mask, p, q)
        b[k + shift] = jnp.where(mask, q, p)


def prepare_kernel(pot, src, fy_lo, fy_hi, ys_lo, ys_hi, even, odd, s_even, s_odd, ext):
    for centre, y_lo, y_hi, depth, a, b in ((pot, fy_lo, fy_hi, RING, even, odd), (src, ys_lo, ys_hi, RING - 1, s_even, s_odd)):
        for x in range(N):
            ext[x, OFF:OFF + N] = centre[x]
            for r in range(depth):
                ext[x, OFF - 1 - r:OFF - r, :] = y_lo[r, x:x + 1, :]
                ext[x, OFF + N + r:OFF + N + r + 1, :] = y_hi[r, x:x + 1, :]
        split(ext, a, b, range(N // 2), 0)


def sweep_kernel(even_in, odd_in, s_even_in, s_odd_in, fx_lo, fx_hi, xs_lo, xs_hi, out, ext, even, odd, s_even, s_odd):
    mid = slice(OFF, OFF + N)
    top = RING + N
    half = (N + 2 * RING) // 2
    shape = (N + 2 * OFF, Z)
    mask = (lax.broadcasted_iota(jnp.int32, shape, 0) + lax.broadcasted_iota(jnp.int32, shape, 1)) % 2 == 0
    zero = jnp.zeros(shape, F32)
    for ref in (even, odd):
        ref[0] = zero
        ref[half + 1] = zero
    for ref, given in ((even, even_in), (odd, odd_in), (s_even, s_even_in), (s_odd, s_odd_in)):
        for k in range(N // 2):
            ref[k + 1 + RING // 2] = given[k]
    ends = list(range(RING // 2)) + list(range(RING // 2 + N // 2, half))
    def far(ref):
        v = ref[FAR:FAR + N // 2, :]
        return jnp.concatenate([v, roll_z(v, -1)], axis=0)

    for x_lo, x_hi, depth, single, shared, a, b in (
            (lambda r: fx_lo[r], lambda r: fx_hi[r], RING, POT_ROWS, POT_SHARED, even, odd),
            (lambda r: plane(xs_lo, r) if r < RING - 2 else far(xs_lo), lambda r: plane(xs_hi, r) if r < RING - 2 else far(xs_hi),
             RING - 1, SRC_ROWS, SRC_SHARED, s_even, s_odd)):
        for r in range(depth):
            ext[RING - 1 - r, mid] = x_lo(r)
            ext[top + r, mid] = x_hi(r)
        for at, a_ring, side, b_ring in single + [(at, p, side, q) for at, p, q in shared for side in (0, 1)]:
            y = OFF + N + b_ring - 1 if side else OFF - b_ring
            ext[RING - a_ring, y:y + 1, :] = xs_lo[at:at + 1, :]
            ext[top + a_ring - 1, y:y + 1, :] = xs_hi[at:at + 1, :]
        split(ext, a, b, ends, 1)

    for h in range(6):
        this, other, s = (even, odd, s_even) if h % 2 == 0 else (odd, even, s_odd)

        def update(k, carry, h=h, this=this, other=other, s=s):
            c = other[k]
            before, after = other[k - 1], other[k + 1]
            far = jnp.where(mask, before, after) if h % 2 == 0 else jnp.where(mask, after, before)
            nb = (c + far) + (roll_y(c, 1) + roll_y(c, -1)) + (roll_z(c, 1) + roll_z(c, -1))
            this[k] = -0.6 * this[k] + (1.6 / 6.0) * (nb + s[k])
            return carry

        lo = (h + 1) // 2
        for k in range(lo + 1, half - lo + 1):
            update(k, 0)

    def last(k, carry):
        p, q = even[k], odd[k]
        out[2 * (k - 1) - RING] = jnp.where(mask, p, q)[OFF:OFF + N]
        out[2 * (k - 1) - RING + 1] = jnp.where(mask, q, p)[OFF:OFF + N]
        return carry

    lax.fori_loop(RING // 2 + 1, RING // 2 + N // 2 + 1, last, 0)


def patch_kernel(buf, ex_lo, ex_hi, ey_lo, ey_hi, yh_lo, yh_hi, xh_lo, xh_hi, conc, out, conc_out, done, sems):
    row = rows()
    copies = [pltpu.make_async_copy(conc, conc_out, sems.at[19])]
    copies[0].start()
    for i in range(19):
        cx, cy, _ = C[i]

        def halo(v, src, i=i, cy=cy):
            if cy == 1:
                return jnp.where(row == 0, spread(yh_lo[pl.ds(YPOS.index(i) * N + src, 1), :]), v)
            if cy == -1:
                return jnp.where(row == N - 1, spread(yh_hi[pl.ds(YNEG.index(i) * N + src, 1), :]), v)
            return v

        def inner(src, carry, i=i, cx=cx, cy=cy, halo=halo):
            here = pl.ds(src, 1)
            v = buf[i, src + cx]
            if cy != -1:
                v = jnp.where(row == cy, spread(ey_lo[i, here, :]), v)
            if cy != 1:
                v = jnp.where(row == N - 1 + cy, spread(ey_hi[i, here, :]), v)
            done[i, src + cx] = halo(v, src)
            return carry

        lax.fori_loop(1, N - 1, inner, 0, unroll=True)
        if cx != -1:
            done[i, cx] = halo(ex_lo[i], 0)
        if cx != 1:
            done[i, N - 1 + cx] = halo(ex_hi[i], N - 1)
        if cx == 1:
            done[i, 0] = plane(xh_lo, XPOS.index(i))
        if cx == -1:
            done[i, N - 1] = plane(xh_hi, XNEG.index(i))
        copy = pltpu.make_async_copy(done.at[i], out.at[i], sems.at[i])
        copy.start()
        copies.append(copy)
    for copy in copies:
        copy.wait()


def flux(a, b):
    link = a[2] * b[2]
    drop = a[3] - b[3]
    rest, weight = [], []
    for s in range(2):
        both = a[s] + b[s]
        rest.append(link * (RATES[s] * ((a[s] - b[s]) + ((0.5 * VAL[s]) * both) * drop)))
        weight.append((0.25 * link) * both)
    return rest, weight


def ring_rows(at, total):
    single, shared = [], []
    for a in range(1, total):
        for b in range(1, total - a):
            for side in (0, 1):
                single.append((at, a, side, b))
                at += 1
    for a in range(1, total):
        shared.append((at, a, total - a))
        at += 1
    return single, shared, at


FAR = (RING - 2) * N
SRC_ROWS, SRC_SHARED, POT_START = ring_rows(FAR + N // 2, RING - 1)
POT_ROWS, POT_SHARED, SRC_END = ring_rows(POT_START, RING)
SRC_LEN = -(-SRC_END // 8) * 8


def pack_src_kernel(src, ys_lo, ys_hi, fy_lo, fy_hi, o_hi, o_lo):
    lane = lax.broadcasted_iota(jnp.int32, (1, Z), 1) % 2
    half = (N // 2, Z)
    shade = (lax.broadcasted_iota(jnp.int32, half, 0) + lax.broadcasted_iota(jnp.int32, half, 1)) % 2
    for o, high in ((o_hi, True), (o_lo, False)):
        def at_x(a, high=high):
            return N - a if high else a - 1

        for k in range(RING - 2):
            o[k * N:(k + 1) * N, :] = src[at_x(k + 1)]
        x = at_x(RING - 1)
        v = src[x]
        o[FAR:FAR + N // 2, :] = jnp.where(shade == x % 2, v[:N // 2], roll_z(v[N // 2:], 1))
        for single, shared, lo, hi, odd in ((SRC_ROWS, SRC_SHARED, ys_lo, ys_hi, 0), (POT_ROWS, POT_SHARED, fy_lo, fy_hi, 1)):
            for at, a, side, b in single:
                halo = hi if side else lo
                o[at:at + 1, :] = halo[b - 1, at_x(a):at_x(a) + 1, :]
            for at, a, b in shared:
                x = at_x(a)
                o[at:at + 1, :] = jnp.where(lane == (x + b + odd) % 2, lo[b - 1, x:x + 1, :], hi[b - 1, x:x + 1, :])
        o[SRC_END:, :] = jnp.zeros((SRC_LEN - SRC_END, Z), F32)


def swap(axis, hi, lo):
    n = lax.axis_size(axis)
    even = lax.axis_index(axis) % 2 == 0
    first = lax.ppermute(jnp.where(even, hi, lo), axis, [(i, i + 1 - 2 * (i % 2)) for i in range(n)])
    second = lax.ppermute(jnp.where(even, lo, hi), axis, [(i, (i - 1 + 2 * (i % 2)) % n) for i in range(n)])
    return jnp.where(even, second, first), jnp.where(even, first, second)


def body(pops, conc, pot, mob, solid, classes, charge):
    cube = sds(N, N, Z)
    msg = sds(ROWS, Z)
    gx_hi, gx_lo, gy_hi, gy_lo, pull, middle = call(
        faces_kernel, [sds(RING + 3, N, Z)] * 4 + [cube, sds(N - 2 * RING, N, Z)], "faces", "hhhh",
        scratch=[VM((N, N, Z), F32), VM((N, N, Z), F32), VM((2, N, N, Z), F32), VM((N, N, Z), F32),
                 VM((N, N, Z), jnp.int32),
                 pltpu.SemaphoreType.DMA((4,))], mib=53, moved=2600000)(
        pot, conc, mob, solid)
    fx_lo, fx_hi = swap("gx", gx_hi, gx_lo)
    fy_lo, fy_hi = swap("gy", gy_hi, gy_lo)
    chunks = N // CHUNK
    buf, mom, px_lo, px_hi, pr_lo, pr_hi = call(
        collide_kernel, [sds(19, N, N, Z), sds(4, N, N, Z)] + [sds(19, N, Z)] * 4, "collide", "hvvvv",
        scratch=[VM((19, N, N, Z), F32), pltpu.SemaphoreType.DMA((chunks,)), pltpu.SemaphoreType.DMA((2,))],
        mib=43, flops=20000000, moved=14000000)(pops, gx_hi, gx_lo, middle, pull)
    mom, ex_lo, ex_hi, ey_lo, ey_hi, yb_lo, yb_hi = call(
        edge_kernel, [sds(4, N, N, Z)] + [sds(19, N, Z)] * 4 + [msg, msg], "edge", "v" * 13, moved=3000000)(
        px_lo, px_hi, pr_lo, pr_hi, gx_lo, gx_hi, gy_lo, gy_hi, fx_lo, fx_hi, fy_lo, fy_hi, mom)
    yh_lo, yh_hi = swap("gy", yb_hi, yb_lo)
    xb_lo, xb_hi = call(corner_kernel, [msg, msg], "corner", "v" * 7)(ex_lo, ex_hi, yh_lo, yh_hi, yb_lo, yb_hi, mom)
    xh_lo, xh_hi = swap("gx", xb_hi, xb_lo)
    fy_late, _ = lax.optimization_barrier((fy_lo, yh_lo))
    pair = sds(2, N, N, Z)
    ring = sds(RING - 1, N, Z)
    base, wx, wy, wy_low, wz, wall, cond, drift, src, sy_lo, sy_hi = call(
        inner_kernel, [pair, sds(2, 4, N, Z), sds(2, 2, N, Z), sds(2, N, Z), sds(2, 2, N, Z), cube, cube, sds(3, N, N, Z), cube, ring, ring],
        "inner", "sh" + "v" * 14,
        scratch=[VM((2, N, Z), F32), VM((2, N, Z), F32), VM((N, N, Z), jnp.int32), pltpu.SemaphoreType.DMA],
        flops=10000000, moved=6000000)(
        charge, classes, mob, solid, conc, pot, fx_lo, fx_hi, fy_late, fy_hi, gy_lo, mom, yh_lo, yh_hi, yb_lo, yb_hi)
    conc_new, src, sy_lo, sy_hi = call(
        transport_kernel, [pair, cube, ring, ring], "transport", "v" * 24, flops=3000000, moved=4000000)(
        mom, cond, base, wx, wy, wy_low, wz, wall, drift, src, sy_lo, sy_hi,
        yh_lo, yh_hi, xh_lo, xh_hi, yb_lo, yb_hi, xb_lo, xb_hi, fx_lo, fx_hi, fy_lo, fy_hi)
    ys_lo, ys_hi = swap("gy", sy_hi, sy_lo)
    bs_hi, bs_lo = call(pack_src_kernel, [sds(SRC_LEN, Z)] * 2, "pack_src", "v" * 5)(src, ys_lo, ys_hi, fy_lo, fy_hi)
    xs_lo, xs_hi = swap("gx", bs_hi, bs_lo)
    packed = VM(((N + 2 * RING) // 2 + 2, N + 2 * OFF, Z), F32)
    prepared = call(
        prepare_kernel, [sds(N // 2, N + 2 * OFF, Z)] * 4, "prepare", "v" * 6,
        scratch=[VM((N, N + 2 * OFF, Z), F32)], flops=1000000, moved=4000000)(pot, src, fy_lo, fy_hi, ys_lo, ys_hi)
    potential_out = call(
        sweep_kernel, [cube], "sweep", "v" * 8,
        scratch=[VM((N + 2 * RING, N + 2 * OFF, Z), F32)] + [packed] * 4, flops=20000000, moved=4000000)(
        *prepared, fx_lo, fx_hi, xs_lo, xs_hi)[0]
    pop, conc_out = call(
        patch_kernel, [sds(19, N, N, Z), pair], "patch", "v" * 10, out_specs="hh",
        scratch=[VM((19, N, N, Z), F32), pltpu.SemaphoreType.DMA((20,))], mib=16, moved=10000000)(
        buf, ex_lo, ex_hi, ey_lo, ey_hi, yh_lo, yh_hi, xh_lo, xh_hi, conc_new)
    return (pop, conc_out, potential_out)


def solution(mesh):
    lattice = P(None, "gx", "gy", None)
    flat = P("gx", "gy", None)
    return jax.shard_map(
        body, mesh=mesh, in_specs=(lattice, lattice, flat, flat, flat, flat, P()),
        out_specs=(lattice, lattice, flat), check_vma=False)
```

```python
import jax
import jax.numpy as jnp
from jax import lax
from jax.experimental import pallas as pl
from jax.experimental.pallas import tpu as pltpu
from jax.sharding import PartitionSpec as P

C = [(0, 0, 0), (1, 0, 0), (-1, 0, 0), (0, 1, 0), (0, -1, 0), (0, 0, 1), (0, 0, -1),
     (1, 1, 0), (-1, -1, 0), (1, -1, 0), (-1, 1, 0), (1, 0, 1), (-1, 0, -1), (1, 0, -1), (-1, 0, 1),
     (0, 1, 1), (0, -1, -1), (0, 1, -1), (0, -1, 1)]
W = [1.0 / 3.0] + [1.0 / 18.0] * 6 + [1.0 / 36.0] * 12
XPOS = [i for i in range(19) if C[i][0] == 1]
XNEG = [i for i in range(19) if C[i][0] == -1]
YPOS = [i for i in range(19) if C[i][1] == 1]
YNEG = [i for i in range(19) if C[i][1] == -1]
RATES = (0.06, 0.08)
VAL = (1.0, -1.0)
N = 16
Z = 256
CHUNK = 4
RING = 6
OFF = 8
ROWS = 7 * N + 8
LINE = 7 * N
SOLID = 1.0
F32 = jnp.float32
VM = pltpu.VMEM


def sds(*shape):
    return jax.ShapeDtypeStruct(shape, F32)


def params(mib):
    return pltpu.CompilerParams(vmem_limit_bytes=mib * 1024 * 1024)


def rows():
    return lax.broadcasted_iota(jnp.int32, (N, Z), 0)


def roll_y(v, s):
    return pltpu.roll(v, s % v.shape[0], 0)


def roll_z(v, s):
    return pltpu.roll(v, s % v.shape[1], 1)


def row_of(v, y):
    return v[y:y + 1, :]


def spread(row):
    return jnp.broadcast_to(row, (N, Z))


def shift_up(v):
    return jnp.where(rows() == 0, 0.0, roll_y(v, 1))


def shift_down(v):
    return jnp.where(rows() == N - 1, 0.0, roll_y(v, -1))


def shift_by(v, c):
    return shift_up(v) if c == 1 else shift_down(v) if c == -1 else v


def call(kernel, outs, name, specs, scratch=(), mib=16, flops=0, out_specs=None, moved=0):
    return pl.pallas_call(
        kernel,
        in_specs=[pl.BlockSpec(memory_space={"v": VM, "h": pltpu.HBM, "s": pltpu.SMEM}[c]) for c in specs],
        out_specs=[pl.BlockSpec(memory_space={"v": VM, "h": pltpu.HBM}[c]) for c in out_specs or "v" * len(outs)],
        out_shape=outs,
        scratch_shapes=list(scratch),
        compiler_params=params(mib),
        cost_estimate=pl.CostEstimate(flops=flops, bytes_accessed=moved, transcendentals=0),
        name=name,
    )


def faces_kernel(pot_h, conc_h, mob_h, solid_h, gx_hi, gx_lo, gy_hi, gy_lo, pull, middle, pot, conc, mob, solid, sems):
    pairs = ((pot_h, pot), (conc_h, conc), (mob_h, mob), (solid_h, solid))
    copies = [pltpu.make_async_copy(a, b, sems.at[q]) for q, (a, b) in enumerate(pairs)]
    for c in copies:
        c.start()
    copies[0].wait()
    for x in range(N):
        for r in range(RING):
            gy_hi[r, x:x + 1, :] = pot[x, N - 1 - r:N - r, :]
            gy_lo[r, x:x + 1, :] = pot[x, r:r + 1, :]
    for r in range(RING):
        gx_hi[r] = pot[N - 1 - r]
        gx_lo[r] = pot[r]
    for x in range(RING, N - RING):
        middle[x - RING] = pot[x]
    copies[1].wait()
    for s in range(2):
        for x in range(N):
            gy_hi[RING + s, x:x + 1, :] = conc[s, x, N - 1:N, :]
            gy_lo[RING + s, x:x + 1, :] = conc[s, x, 0:1, :]
        gx_hi[RING + s] = conc[s, N - 1]
        gx_lo[RING + s] = conc[s, 0]
    copies[2].wait()
    copies[3].wait()
    for x in range(N):
        is_fluid = solid[x] == 0
        v = jnp.where(is_fluid, jnp.sqrt(mob[x]), 0.0)
        pull[x] = jnp.where(is_fluid, (conc[0, x] - conc[1, x]) * (-0.001), SOLID)
        gy_hi[RING + 2, x:x + 1, :] = row_of(v, N - 1)
        gy_lo[RING + 2, x:x + 1, :] = row_of(v, 0)
        if x == 0:
            gx_lo[RING + 2] = v
        if x == N - 1:
            gx_hi[RING + 2] = v


def post_of(p, fluid, q, slopes):
    pull = jnp.where(fluid, q, 0.0)
    force = [pull * d for d in slopes]
    density = p[0]
    for i in range(1, 19):
        density = density + p[i]
    inv = 1.0 / density
    u = []
    for a in range(3):
        total = 0.9 * force[a]
        for i in range(1, 19, 2):
            if C[i][a]:
                term = p[i] - p[i + 1]
                total = total + term if C[i][a] == 1 else total - term
        u.append(total * inv)
    base = 1.0 - 1.5 * (u[0] * u[0] + u[1] * u[1] + u[2] * u[2])
    scaled = density * (10.0 / 9.0)
    out = [jnp.where(fluid, (W[0] * scaled) * base - p[0] * (1.0 / 9.0), p[0])]
    for i in range(1, 19, 2):
        along = None
        for a in range(3):
            if C[i][a]:
                term = u[a] if C[i][a] == 1 else -u[a]
                along = term if along is None else along + term
        even = base + 4.5 * along * along
        odd = 3.0 * along
        ws = W[i] * scaled
        fwd = ws * (even + odd) - p[i] * (1.0 / 9.0)
        bwd = ws * (even - odd) - p[i + 1] * (1.0 / 9.0)
        out.append(jnp.where(fluid, fwd, p[i + 1]))
        out.append(jnp.where(fluid, bwd, p[i]))
    return out, force


def sums(values, keep):
    total = [None] * 4
    for cy in (0, 1, -1):
        part = [None] * 4
        for i, v in values:
            if C[i][1] != cy:
                continue
            for m, c in enumerate((1,) + C[i]):
                if c and m != 2:
                    w = v if c == 1 else -v
                    part[m] = w if part[m] is None else part[m] + w
        for m in (0, 1, 3):
            if part[m] is None:
                continue
            w = part[m] if keep[cy] is None else jnp.where(keep[cy], part[m], 0.0)
            total[m] = w if total[m] is None else total[m] + w
            if m == 0 and cy:
                w = w if cy == 1 else -w
                total[2] = w if total[2] is None else total[2] + w
    return total


def collide_kernel(pops, gx_hi, gx_lo, middle, pull, buf, mom, px_lo, px_hi, pr_lo, pr_hi, held, sems, psems):
    chunks = [pltpu.make_async_copy(pops.at[:, pl.ds(CHUNK * s, CHUNK)], held.at[:, pl.ds(CHUNK * s, CHUNK)], sems.at[s])
              for s in range(N // CHUNK)]
    ends = [pltpu.make_async_copy(pops.at[:, 0], px_lo, psems.at[0]),
            pltpu.make_async_copy(pops.at[:, N - 1], px_hi, psems.at[1])]
    for c in chunks + ends:
        c.start()
    row = rows()
    zero = jnp.zeros((N, Z), F32)
    keep = {0: (row >= 1) & (row <= N - 2), 1: row >= 2, -1: row <= N - 3}
    for m in range(4):
        mom[m, 0] = zero
        mom[m, 1] = zero

    def pot(x):
        return gx_lo[x] if x < RING else gx_hi[N - 1 - x] if x >= N - RING else middle[x - RING]

    def step(x):
        here = pl.ds(x, 1)
        p = [held[i, x] for i in range(19)]
        for i in range(19):
            pr_lo[i, here, :] = row_of(p[i], 0)
            pr_hi[i, here, :] = row_of(p[i], N - 1)
        centre = pot(x)
        slopes = (pot(x + 1) - pot(x - 1), roll_y(centre, -1) - roll_y(centre, 1), roll_z(centre, -1) - roll_z(centre, 1))
        post, force = post_of(p, pull[x] < 0.5 * SOLID, pull[x], slopes)
        moved = []
        for i in range(19):
            v = post[i]
            if C[i][2]:
                v = roll_z(v, C[i][2])
            if C[i][1]:
                v = roll_y(v, C[i][1])
            buf[i, x + C[i][0]] = v
            moved.append(v)
        g = sums([(i, moved[i]) for i in range(19) if C[i][0] == 0], keep)
        mom[0, x] += g[0]
        for m in (1, 2, 3):
            w = jnp.where(keep[0], 0.5 * force[m - 1], 0.0)
            mom[m, x] += w if g[m] is None else g[m] + w
        g = sums([(i, moved[i]) for i in XPOS], keep)
        for m in range(4):
            mom[m, x + 1] = g[m]
        g = sums([(i, moved[i]) for i in XNEG], keep)
        for m in range(4):
            mom[m, x - 1] += g[m]

    for s in range(N // CHUNK):
        chunks[s].wait()
        for x in range(max(CHUNK * s, 1), min(CHUNK * s + CHUNK, N - 1)):
            step(x)
    for c in ends:
        c.wait()


def edge_kernel(px_lo, px_hi, pr_lo, pr_hi, gx_lo, gx_hi, gy_lo, gy_hi, fx_lo, fx_hi, fy_lo, fy_hi, mom0,
                mom, ex_lo, ex_hi, ey_lo, ey_hi, yb_lo, yb_hi):
    row = rows()
    inner = (row >= 1) & (row <= N - 2)
    keep = {0: None, 1: row >= 1, -1: row <= N - 2}
    lines = {}
    for pr, gy, fy, ey, low in ((pr_lo, gy_lo, fy_lo, ey_lo, True), (pr_hi, gy_hi, fy_hi, ey_hi, False)):
        centre = gy[0]
        y_slope = gy[1] - fy[0] if low else fy[0] - gy[1]
        slopes = (roll_y(centre, -1) - roll_y(centre, 1), y_slope, roll_z(centre, -1) - roll_z(centre, 1))
        post, force = post_of([pr[i] for i in range(19)], gy[RING + 2] > 0.0, (gy[RING] - gy[RING + 1]) * (-0.001), slopes)
        for i in range(19):
            v = roll_z(post[i], C[i][2]) if C[i][2] else post[i]
            v = jnp.where(inner, v, 0.0)
            ey[i] = v
            if low and C[i][1] == -1:
                q = YNEG.index(i)
                yb_lo[q * N:(q + 1) * N, :] = v
            if not low and C[i][1] == 1:
                q = YPOS.index(i)
                yb_hi[q * N:(q + 1) * N, :] = v
            post[i] = shift_by(v, C[i][0])
        for cy in (0, 1 if low else -1):
            y = (0 if low else N - 1) + cy
            total = [None] * 4
            for i in range(19):
                if C[i][1] == cy:
                    for m, c in enumerate((1,) + C[i]):
                        if c:
                            w = post[i] if c == 1 else -post[i]
                            total[m] = w if total[m] is None else total[m] + w
            if cy == 0:
                for a in range(3):
                    w = jnp.where(inner, 0.5 * force[a], 0.0)
                    total[a + 1] = w if total[a + 1] is None else total[a + 1] + w
            lines[y] = total
    for x in range(N):
        for m in range(4):
            v = mom0[m, x]
            for y in (0, 1, N - 2, N - 1):
                v = v + jnp.where(row == y, spread(row_of(lines[y][m], x)), 0.0)
            mom[m, x] = v
    for px, gx, fx, ex, low in ((px_lo, gx_lo, fx_lo, ex_lo, True), (px_hi, gx_hi, fx_hi, ex_hi, False)):
        at = 0 if low else N - 1
        centre = gx[0]
        x_slope = gx[1] - fx[0] if low else fx[0] - gx[1]
        y_up = jnp.where(row == N - 1, spread(fy_hi[0, at:at + 1, :]), roll_y(centre, -1))
        y_dn = jnp.where(row == 0, spread(fy_lo[0, at:at + 1, :]), roll_y(centre, 1))
        slopes = (x_slope, y_up - y_dn, roll_z(centre, -1) - roll_z(centre, 1))
        post, force = post_of([px[i] for i in range(19)], gx[RING + 2] > 0.0, (gx[RING] - gx[RING + 1]) * (-0.001), slopes)
        for i in range(19):
            v = roll_z(post[i], C[i][2]) if C[i][2] else post[i]
            if C[i][1] == 1:
                v = roll_y(v, 1)
                at_row = YPOS.index(i) * N + at
                yb_hi[at_row:at_row + 1, :] = row_of(v, 0)
                v = jnp.where(row == 0, 0.0, v)
            elif C[i][1] == -1:
                v = roll_y(v, -1)
                at_row = YNEG.index(i) * N + at
                yb_lo[at_row:at_row + 1, :] = row_of(v, N - 1)
                v = jnp.where(row == N - 1, 0.0, v)
            ex[i] = v
            post[i] = v
        none = {0: None, 1: None, -1: None}
        g = sums([(i, post[i]) for i in range(19) if C[i][0] == 0], none)
        mom[0, at] += g[0]
        for m in (1, 2, 3):
            w = 0.5 * force[m - 1]
            mom[m, at] += w if g[m] is None else g[m] + w
        g = sums([(i, post[i]) for i in (XPOS if low else XNEG)], none)
        for m in range(4):
            mom[m, 1 if low else N - 2] += g[m]
        g = sums([(i, post[i]) for i in (XNEG if low else XPOS)], none)
        k = LINE + (2 if low else 0)
        yb_hi[k:k + 1, :] = row_of(g[0], N - 1)
        yb_hi[k + 1:k + 2, :] = row_of(g[2], N - 1)
        yb_lo[k:k + 1, :] = row_of(g[0], 0)
        yb_lo[k + 1:k + 2, :] = row_of(g[2], 0)
    for x in range(N):
        for q, m in ((5, 0), (6, 2)):
            yb_lo[q * N + x:q * N + x + 1, :] = mom[m, x, 0:1, :]
            yb_hi[q * N + x:q * N + x + 1, :] = mom[m, x, N - 1:N, :]
    yb_lo[LINE + 4:, :] = jnp.zeros((4, Z), F32)
    yb_hi[LINE + 4:, :] = jnp.zeros((4, Z), F32)


def plane(ref, q):
    return ref[q * N:(q + 1) * N, :]


def line(ref, q, x):
    return ref[q * N + x:q * N + x + 1, :]


def y_terms(lo, hi):
    s3, s7, s10, s15, s17 = (plane(lo, q) for q in range(5))
    s7, s10 = shift_up(s7), shift_down(s10)
    total = s3 + s7 + s10 + s15 + s17
    below = (total, s7 - s10, total, s15 - s17)
    s4, s8, s9, s16, s18 = (plane(hi, q) for q in range(5))
    s8, s9 = shift_down(s8), shift_up(s9)
    total = s4 + s8 + s9 + s16 + s18
    return below, (total, s9 - s8, -total, s18 - s16)


def corner_kernel(ex_lo, ex_hi, yh_lo, yh_hi, yb_lo, yb_hi, mom, xb_lo, xb_hi):
    row = rows()
    below, above = y_terms(yh_lo, yh_hi)
    for ex, xb, slots, at in ((ex_hi, xb_hi, XPOS, N - 1), (ex_lo, xb_lo, XNEG, 0)):
        for q, i in enumerate(slots):
            v = ex[i]
            if C[i][1] == 1:
                v = jnp.where(row == 0, spread(line(yh_lo, YPOS.index(i), at)), v)
            elif C[i][1] == -1:
                v = jnp.where(row == N - 1, spread(line(yh_hi, YNEG.index(i), at)), v)
            xb[q * N:(q + 1) * N, :] = v
        for q, m in ((5, 0), (6, 1)):
            v = mom[m, at] + jnp.where(row == 0, spread(row_of(below[m], at)), 0.0)
            xb[q * N:(q + 1) * N, :] = v + jnp.where(row == N - 1, spread(row_of(above[m], at)), 0.0)
        c = 1 if at else -1
        k = LINE if at else LINE + 2
        down = line(yb_lo, YNEG.index(9 if c == 1 else 8), at)
        up = line(yb_hi, YPOS.index(7 if c == 1 else 10), at)
        xb[LINE:LINE + 1, :] = yh_lo[k:k + 1, :] + down
        xb[LINE + 1:LINE + 2, :] = yh_lo[k + 1:k + 2, :] - down
        xb[LINE + 2:LINE + 3, :] = yh_hi[k:k + 1, :] + up
        xb[LINE + 3:LINE + 4, :] = yh_hi[k + 1:k + 2, :] + up
        xb[LINE + 4:, :] = jnp.zeros((4, Z), F32)


def velocity(conductance, density, momentum):
    return jnp.where(conductance > 0.0, momentum / density, 0.0)


def full_moment(mom, m, x, below, above):
    v = mom[m, x] + jnp.where(rows() == 0, spread(row_of(below[m], x)), 0.0)
    return v + jnp.where(rows() == N - 1, spread(row_of(above[m], x)), 0.0)


def inner_kernel(charge, classes_h, mob, solid, conc, pot, fx_lo, fx_hi, fy_lo, fy_hi, gy_lo, mom, yh_lo, yh_hi, yb_lo, yb_hi,
                 base, wx, wy, wy_low, wz, wall, cond, drift, src, sy_lo, sy_hi, low, adv, classes, sem):
    fetch = pltpu.make_async_copy(classes_h, classes, sem)
    fetch.start()
    row = rows()

    def faces(ref):
        return tuple(ref[RING + q] for q in range(3)) + (ref[0],)

    rest, weight = flux(faces(fy_lo), faces(gy_lo))
    for s in range(2):
        low[s] = rest[s]
        wy_low[s] = weight[s]
    upper = faces(fy_hi)
    for x in range(N):
        cond[x] = jnp.where(solid[x] == 0, jnp.sqrt(mob[x]), 0.0)
    below, above = y_terms(yh_lo, yh_hi)
    for x in range(1, N - 1):
        scale = jnp.where(cond[x] > 0.0, 1.0 / full_moment(mom, 0, x, below, above), 0.0)
        for a in range(3):
            drift[a, x] = full_moment(mom, a + 1, x, below, above) * scale
    from_hi, from_lo = y_terms(yb_hi, yb_lo)
    dy_lo = velocity(fy_lo[RING + 2], plane(yh_lo, 5) + from_lo[0], plane(yh_lo, 6) + from_lo[2])
    dy_hi = velocity(fy_hi[RING + 2], plane(yh_hi, 5) + from_hi[0], plane(yh_hi, 6) + from_hi[2])
    for x in range(1, N - 1):
        carried = row_of(dy_lo, x) + drift[1, x, 0:1, :]
        for s in range(2):
            adv[s, x:x + 1, :] = wy_low[s, x:x + 1, :] * carried

    def fields(x):
        return (conc[0, x], conc[1, x], cond[x], pot[x])

    behind, weight = flux(faces(fx_lo), fields(0))
    for s in range(2):
        wx[s, 0] = weight[s]
    fetch.wait()
    for x in range(N):
        known = 1 <= x <= N - 2
        me = fields(x)
        ahead, weight = flux(me, fields(x + 1) if x < N - 1 else faces(fx_hi))
        if 1 <= x <= N - 3:
            carried = drift[0, x] + drift[0, x + 1]
            ahead = [ahead[s] + weight[s] * carried for s in range(2)]
        elif x in (0, N - 2):
            for s in range(2):
                wx[s, 1 if x == 0 else 2] = weight[s]
        else:
            for s in range(2):
                wx[s, 3] = weight[s]
        tot = [ahead[s] - behind[s] for s in range(2)]
        behind = ahead
        nxt = tuple(jnp.where(row == N - 1, spread(row_of(upper[q], x)), roll_y(me[q], -1)) for q in range(4))
        rest, weight = flux(me, nxt)
        first = [low[s, x:x + 1, :] for s in range(2)]
        if known:
            v = drift[1, x]
            carried = v + jnp.where(row == N - 1, spread(row_of(dy_hi, x)), roll_y(v, -1))
            rest = [rest[s] + weight[s] * carried for s in range(2)]
            first = [first[s] + adv[s, x:x + 1, :] for s in range(2)]
        else:
            for s in range(2):
                wy[s, x // (N - 1)] = weight[s]
        for s in range(2):
            tot[s] = tot[s] + (rest[s] - jnp.where(row == 0, spread(first[s]), roll_y(rest[s], 1)))
        rest, weight = flux(me, tuple(roll_z(v, -1) for v in me))
        if known:
            v = drift[2, x]
            carried = v + roll_z(v, -1)
            rest = [rest[s] + weight[s] * carried for s in range(2)]
        else:
            for s in range(2):
                wz[s, x // (N - 1)] = weight[s]
        for s in range(2):
            tot[s] = tot[s] + (rest[s] - roll_z(rest[s], 1))
            base[s, x] = me[s] - tot[s]
        cls = classes[x]
        total = jnp.zeros((N, Z), F32)
        for q in range(4):
            total = total + jnp.where(cls == q, charge[q], 0.0)
        if 2 <= x <= N - 3:
            source_plane(x, jnp.where(cond[x] > 0.0, me[0] - tot[0] - (me[1] - tot[1]), total), src, sy_lo, sy_hi)
        else:
            wall[x] = total


def source_plane(x, v, src, sy_lo, sy_hi):
    src[x] = v
    for r in range(RING - 1):
        sy_lo[r, x:x + 1, :] = row_of(v, r)
        sy_hi[r, x:x + 1, :] = row_of(v, N - 1 - r)


def transport_kernel(mom, cond, base, wx, wy, wy_low, wz, wall, drift, src0, sy_lo0, sy_hi0,
                     yh_lo, yh_hi, xh_lo, xh_hi, yb_lo, yb_hi, xb_lo, xb_hi,
                     fx_lo, fx_hi, fy_lo, fy_hi, conc_out, src, sy_lo, sy_hi):
    row = rows()
    below, above = y_terms(yh_lo, yh_hi)
    sy_lo[...] = sy_lo0[...]
    sy_hi[...] = sy_hi0[...]
    for x in range(2, N - 2):
        src[x] = src0[x]
        for s in range(2):
            conc_out[s, x] = base[s, x]
    from_hi, from_lo = y_terms(yb_hi, yb_lo)

    def y_line(fy, yh, terms, k, xh, x):
        density = line(yh, 5, x) + row_of(terms[0], x) + xh[k:k + 1, :]
        momentum = line(yh, 6, x) + row_of(terms[2], x) + xh[k + 1:k + 2, :]
        return velocity(fy[RING + 2, x:x + 1, :], density, momentum)

    for x, near, xh, xb, fx, sign in ((0, 1, xh_lo, xb_lo, fx_lo, 1.0), (N - 1, N - 2, xh_hi, xb_hi, fx_hi, -1.0)):
        a = [plane(xh, q) for q in range(5)]
        total = a[0] + a[1] + a[2] + a[3] + a[4]
        extra = (total, sign * total, sign * (a[1] - a[2]), sign * (a[3] - a[4]))
        full = [full_moment(mom, m, x, below, above) + extra[m] for m in range(4)]
        scale = jnp.where(cond[x] > 0.0, 1.0 / full[0], 0.0)
        d = [full[m] * scale for m in (1, 2, 3)]
        out = plane(xb, 0) + plane(xb, 1) + plane(xb, 2) + plane(xb, 3) + plane(xb, 4)
        beyond = velocity(fx[RING + 2], plane(xh, 5) + out, plane(xh, 6) - sign * out)
        e = x // (N - 1)
        outer = 3 * e
        dy_lo = y_line(fy_lo, yh_lo, from_lo, LINE, xh, x)
        dy_hi = y_line(fy_hi, yh_hi, from_hi, LINE + 2, xh, x)
        c, c_near = [], []
        up = d[1] + jnp.where(row == N - 1, spread(dy_hi), roll_y(d[1], -1))
        turn = d[2] + roll_z(d[2], -1)
        for s in range(2):
            far = wx[s, outer] * (beyond + d[0])
            close = wx[s, 1 + e] * (d[0] + drift[0, near])
            f = wy[s, e] * up
            first = wy_low[s, x:x + 1, :] * (dy_lo + row_of(d[1], 0))
            g = wz[s, e] * turn
            tot = sign * (close - far) + (f - jnp.where(row == 0, spread(first), roll_y(f, 1))) + (g - roll_z(g, 1))
            c.append(base[s, x] - tot)
            c_near.append(base[s, near] + sign * close)
            conc_out[s, x] = c[s]
            conc_out[s, near] = c_near[s]
        source_plane(x, jnp.where(cond[x] > 0.0, c[0] - c[1], wall[x]), src, sy_lo, sy_hi)
        source_plane(near, jnp.where(cond[near] > 0.0, c_near[0] - c_near[1], wall[near]), src, sy_lo, sy_hi)


def split(ext, a, b, pairs, shift):
    shape = (N + 2 * OFF, Z)
    mask = (lax.broadcasted_iota(jnp.int32, shape, 0) + lax.broadcasted_iota(jnp.int32, shape, 1)) % 2 == 0
    for k in pairs:
        p, q = ext[2 * k], ext[2 * k + 1]
        a[k + shift] = jnp.where(mask, p, q)
        b[k + shift] = jnp.where(mask, q, p)


def prepare_kernel(pot, src, fy_lo, fy_hi, ys_lo, ys_hi, even, odd, s_even, s_odd, ext):
    for centre, y_lo, y_hi, depth, a, b in ((pot, fy_lo, fy_hi, RING, even, odd), (src, ys_lo, ys_hi, RING - 1, s_even, s_odd)):
        for x in range(N):
            ext[x, OFF:OFF + N] = centre[x]
            for r in range(depth):
                ext[x, OFF - 1 - r:OFF - r, :] = y_lo[r, x:x + 1, :]
                ext[x, OFF + N + r:OFF + N + r + 1, :] = y_hi[r, x:x + 1, :]
        split(ext, a, b, range(N // 2), 0)


def sweep_kernel(even_in, odd_in, s_even_in, s_odd_in, fx_lo, fx_hi, xs_lo, xs_hi, out, ext, even, odd, s_even, s_odd):
    mid = slice(OFF, OFF + N)
    top = RING + N
    half = (N + 2 * RING) // 2
    shape = (N + 2 * OFF, Z)
    mask = (lax.broadcasted_iota(jnp.int32, shape, 0) + lax.broadcasted_iota(jnp.int32, shape, 1)) % 2 == 0
    zero = jnp.zeros(shape, F32)
    for ref in (even, odd):
        ref[0] = zero
        ref[half + 1] = zero
    for ref, given in ((even, even_in), (odd, odd_in), (s_even, s_even_in), (s_odd, s_odd_in)):
        for k in range(N // 2):
            ref[k + 1 + RING // 2] = given[k]
    ends = list(range(RING // 2)) + list(range(RING // 2 + N // 2, half))
    def far(ref):
        v = ref[FAR:FAR + N // 2, :]
        return jnp.concatenate([v, roll_z(v, -1)], axis=0)

    for x_lo, x_hi, depth, single, shared, a, b in (
            (lambda r: fx_lo[r], lambda r: fx_hi[r], RING, POT_ROWS, POT_SHARED, even, odd),
            (lambda r: plane(xs_lo, r) if r < RING - 2 else far(xs_lo), lambda r: plane(xs_hi, r) if r < RING - 2 else far(xs_hi),
             RING - 1, SRC_ROWS, SRC_SHARED, s_even, s_odd)):
        for r in range(depth):
            ext[RING - 1 - r, mid] = x_lo(r)
            ext[top + r, mid] = x_hi(r)
        for at, a_ring, side, b_ring in single + [(at, p, side, q) for at, p, q in shared for side in (0, 1)]:
            y = OFF + N + b_ring - 1 if side else OFF - b_ring
            ext[RING - a_ring, y:y + 1, :] = xs_lo[at:at + 1, :]
            ext[top + a_ring - 1, y:y + 1, :] = xs_hi[at:at + 1, :]
        split(ext, a, b, ends, 1)

    for h in range(6):
        this, other, s = (even, odd, s_even) if h % 2 == 0 else (odd, even, s_odd)

        def update(k, carry, h=h, this=this, other=other, s=s):
            c = other[k]
            before, after = other[k - 1], other[k + 1]
            far = jnp.where(mask, before, after) if h % 2 == 0 else jnp.where(mask, after, before)
            nb = (c + far) + (roll_y(c, 1) + roll_y(c, -1)) + (roll_z(c, 1) + roll_z(c, -1))
            this[k] = -0.6 * this[k] + (1.6 / 6.0) * (nb + s[k])
            return carry

        lo = (h + 1) // 2
        for k in range(lo + 1, half - lo + 1):
            update(k, 0)

    def last(k, carry):
        p, q = even[k], odd[k]
        out[2 * (k - 1) - RING] = jnp.where(mask, p, q)[OFF:OFF + N]
        out[2 * (k - 1) - RING + 1] = jnp.where(mask, q, p)[OFF:OFF + N]
        return carry

    lax.fori_loop(RING // 2 + 1, RING // 2 + N // 2 + 1, last, 0)


def patch_kernel(buf, ex_lo, ex_hi, ey_lo, ey_hi, yh_lo, yh_hi, xh_lo, xh_hi, conc, out, conc_out, done, sems):
    row = rows()
    copies = [pltpu.make_async_copy(conc, conc_out, sems.at[19])]
    copies[0].start()
    for i in range(19):
        cx, cy, _ = C[i]

        def halo(v, src, i=i, cy=cy):
            if cy == 1:
                return jnp.where(row == 0, spread(yh_lo[pl.ds(YPOS.index(i) * N + src, 1), :]), v)
            if cy == -1:
                return jnp.where(row == N - 1, spread(yh_hi[pl.ds(YNEG.index(i) * N + src, 1), :]), v)
            return v

        def inner(src, carry, i=i, cx=cx, cy=cy, halo=halo):
            here = pl.ds(src, 1)
            v = buf[i, src + cx]
            if cy != -1:
                v = jnp.where(row == cy, spread(ey_lo[i, here, :]), v)
            if cy != 1:
                v = jnp.where(row == N - 1 + cy, spread(ey_hi[i, here, :]), v)
            done[i, src + cx] = halo(v, src)
            return carry

        lax.fori_loop(1, N - 1, inner, 0, unroll=True)
        if cx != -1:
            done[i, cx] = halo(ex_lo[i], 0)
        if cx != 1:
            done[i, N - 1 + cx] = halo(ex_hi[i], N - 1)
        if cx == 1:
            done[i, 0] = plane(xh_lo, XPOS.index(i))
        if cx == -1:
            done[i, N - 1] = plane(xh_hi, XNEG.index(i))
        copy = pltpu.make_async_copy(done.at[i], out.at[i], sems.at[i])
        copy.start()
        copies.append(copy)
    for copy in copies:
        copy.wait()


def flux(a, b):
    link = a[2] * b[2]
    drop = a[3] - b[3]
    rest, weight = [], []
    for s in range(2):
        both = a[s] + b[s]
        rest.append(link * (RATES[s] * ((a[s] - b[s]) + ((0.5 * VAL[s]) * both) * drop)))
        weight.append((0.25 * link) * both)
    return rest, weight


def ring_rows(at, total):
    single, shared = [], []
    for a in range(1, total):
        for b in range(1, total - a):
            for side in (0, 1):
                single.append((at, a, side, b))
                at += 1
    for a in range(1, total):
        shared.append((at, a, total - a))
        at += 1
    return single, shared, at


FAR = (RING - 2) * N
SRC_ROWS, SRC_SHARED, POT_START = ring_rows(FAR + N // 2, RING - 1)
POT_ROWS, POT_SHARED, SRC_END = ring_rows(POT_START, RING)
SRC_LEN = -(-SRC_END // 8) * 8


def pack_src_kernel(src, ys_lo, ys_hi, fy_lo, fy_hi, o_hi, o_lo):
    lane = lax.broadcasted_iota(jnp.int32, (1, Z), 1) % 2
    half = (N // 2, Z)
    shade = (lax.broadcasted_iota(jnp.int32, half, 0) + lax.broadcasted_iota(jnp.int32, half, 1)) % 2
    for o, high in ((o_hi, True), (o_lo, False)):
        def at_x(a, high=high):
            return N - a if high else a - 1

        for k in range(RING - 2):
            o[k * N:(k + 1) * N, :] = src[at_x(k + 1)]
        x = at_x(RING - 1)
        v = src[x]
        o[FAR:FAR + N // 2, :] = jnp.where(shade == x % 2, v[:N // 2], roll_z(v[N // 2:], 1))
        for single, shared, lo, hi, odd in ((SRC_ROWS, SRC_SHARED, ys_lo, ys_hi, 0), (POT_ROWS, POT_SHARED, fy_lo, fy_hi, 1)):
            for at, a, side, b in single:
                halo = hi if side else lo
                o[at:at + 1, :] = halo[b - 1, at_x(a):at_x(a) + 1, :]
            for at, a, b in shared:
                x = at_x(a)
                o[at:at + 1, :] = jnp.where(lane == (x + b + odd) % 2, lo[b - 1, x:x + 1, :], hi[b - 1, x:x + 1, :])
        o[SRC_END:, :] = jnp.zeros((SRC_LEN - SRC_END, Z), F32)


def swap(axis, hi, lo):
    n = lax.axis_size(axis)
    even = lax.axis_index(axis) % 2 == 0
    first = lax.ppermute(jnp.where(even, hi, lo), axis, [(i, i + 1 - 2 * (i % 2)) for i in range(n)])
    second = lax.ppermute(jnp.where(even, lo, hi), axis, [(i, (i - 1 + 2 * (i % 2)) % n) for i in range(n)])
    return jnp.where(even, second, first), jnp.where(even, first, second)


def body(pops, conc, pot, mob, solid, classes, charge):
    cube = sds(N, N, Z)
    msg = sds(ROWS, Z)
    gx_hi, gx_lo, gy_hi, gy_lo, pull, middle = call(
        faces_kernel, [sds(RING + 3, N, Z)] * 4 + [cube, sds(N - 2 * RING, N, Z)], "faces", "hhhh",
        scratch=[VM((N, N, Z), F32), VM((2, N, N, Z), F32), VM((N, N, Z), F32),
                 VM((N, N, Z), jnp.int32),
                 pltpu.SemaphoreType.DMA((4,))], mib=53, moved=2600000)(
        pot, conc, mob, solid)
    fx_lo, fx_hi = swap("gx", gx_hi, gx_lo)
    fy_lo, fy_hi = swap("gy", gy_hi, gy_lo)
    chunks = N // CHUNK
    buf, mom, px_lo, px_hi, pr_lo, pr_hi = call(
        collide_kernel, [sds(19, N, N, Z), sds(4, N, N, Z)] + [sds(19, N, Z)] * 4, "collide", "hvvvv",
        scratch=[VM((19, N, N, Z), F32), pltpu.SemaphoreType.DMA((chunks,)), pltpu.SemaphoreType.DMA((2,))],
        mib=43, flops=20000000, moved=14000000)(pops, gx_hi, gx_lo, middle, pull)
    mom, ex_lo, ex_hi, ey_lo, ey_hi, yb_lo, yb_hi = call(
        edge_kernel, [sds(4, N, N, Z)] + [sds(19, N, Z)] * 4 + [msg, msg], "edge", "v" * 13, moved=3000000)(
        px_lo, px_hi, pr_lo, pr_hi, gx_lo, gx_hi, gy_lo, gy_hi, fx_lo, fx_hi, fy_lo, fy_hi, mom)
    yh_lo, yh_hi = swap("gy", yb_hi, yb_lo)
    xb_lo, xb_hi = call(corner_kernel, [msg, msg], "corner", "v" * 7)(ex_lo, ex_hi, yh_lo, yh_hi, yb_lo, yb_hi, mom)
    xh_lo, xh_hi = swap("gx", xb_hi, xb_lo)
    fy_late, _ = lax.optimization_barrier((fy_lo, yh_lo))
    pair = sds(2, N, N, Z)
    ring = sds(RING - 1, N, Z)
    base, wx, wy, wy_low, wz, wall, cond, drift, src, sy_lo, sy_hi = call(
        inner_kernel, [pair, sds(2, 4, N, Z), sds(2, 2, N, Z), sds(2, N, Z), sds(2, 2, N, Z), cube, cube, sds(3, N, N, Z), cube, ring, ring],
        "inner", "sh" + "v" * 14,
        scratch=[VM((2, N, Z), F32), VM((2, N, Z), F32), VM((N, N, Z), jnp.int32), pltpu.SemaphoreType.DMA],
        flops=10000000, moved=6000000)(
        charge, classes, mob, solid, conc, pot, fx_lo, fx_hi, fy_late, fy_hi, gy_lo, mom, yh_lo, yh_hi, yb_lo, yb_hi)
    conc_new, src, sy_lo, sy_hi = call(
        transport_kernel, [pair, cube, ring, ring], "transport", "v" * 24, flops=3000000, moved=4000000)(
        mom, cond, base, wx, wy, wy_low, wz, wall, drift, src, sy_lo, sy_hi,
        yh_lo, yh_hi, xh_lo, xh_hi, yb_lo, yb_hi, xb_lo, xb_hi, fx_lo, fx_hi, fy_lo, fy_hi)
    ys_lo, ys_hi = swap("gy", sy_hi, sy_lo)
    bs_hi, bs_lo = call(pack_src_kernel, [sds(SRC_LEN, Z)] * 2, "pack_src", "v" * 5)(src, ys_lo, ys_hi, fy_lo, fy_hi)
    xs_lo, xs_hi = swap("gx", bs_hi, bs_lo)
    packed = VM(((N + 2 * RING) // 2 + 2, N + 2 * OFF, Z), F32)
    prepared = call(
        prepare_kernel, [sds(N // 2, N + 2 * OFF, Z)] * 4, "prepare", "v" * 6,
        scratch=[VM((N, N + 2 * OFF, Z), F32)], flops=1000000, moved=4000000)(pot, src, fy_lo, fy_hi, ys_lo, ys_hi)
    potential_out = call(
        sweep_kernel, [cube], "sweep", "v" * 8,
        scratch=[VM((N + 2 * RING, N + 2 * OFF, Z), F32)] + [packed] * 4, flops=20000000, moved=4000000)(
        *prepared, fx_lo, fx_hi, xs_lo, xs_hi)[0]
    pop, conc_out = call(
        patch_kernel, [sds(19, N, N, Z), pair], "patch", "v" * 10, out_specs="hh",
        scratch=[VM((19, N, N, Z), F32), pltpu.SemaphoreType.DMA((20,))], mib=16, moved=10000000)(
        buf, ex_lo, ex_hi, ey_lo, ey_hi, yh_lo, yh_hi, xh_lo, xh_hi, conc_new)
    return (pop, conc_out, potential_out)


def solution(mesh):
    lattice = P(None, "gx", "gy", None)
    flat = P("gx", "gy", None)
    return jax.shard_map(
        body, mesh=mesh, in_specs=(lattice, lattice, flat, flat, flat, flat, P()),
        out_specs=(lattice, lattice, flat), check_vma=False)
```

```python
import jax
import jax.numpy as jnp
from jax import lax
from jax.experimental import pallas as pl
from jax.experimental.pallas import tpu as pltpu
from jax.sharding import PartitionSpec as P

C = [(0, 0, 0), (1, 0, 0), (-1, 0, 0), (0, 1, 0), (0, -1, 0), (0, 0, 1), (0, 0, -1),
     (1, 1, 0), (-1, -1, 0), (1, -1, 0), (-1, 1, 0), (1, 0, 1), (-1, 0, -1), (1, 0, -1), (-1, 0, 1),
     (0, 1, 1), (0, -1, -1), (0, 1, -1), (0, -1, 1)]
W = [1.0 / 3.0] + [1.0 / 18.0] * 6 + [1.0 / 36.0] * 12
XPOS = [i for i in range(19) if C[i][0] == 1]
XNEG = [i for i in range(19) if C[i][0] == -1]
YPOS = [i for i in range(19) if C[i][1] == 1]
YNEG = [i for i in range(19) if C[i][1] == -1]
RATES = (0.06, 0.08)
VAL = (1.0, -1.0)
N = 16
Z = 256
CHUNK = 4
RING = 6
OFF = 8
ROWS = 7 * N + 8
LINE = 7 * N
SOLID = 1.0
F32 = jnp.float32
VM = pltpu.VMEM


def sds(*shape):
    return jax.ShapeDtypeStruct(shape, F32)


def params(mib):
    return pltpu.CompilerParams(vmem_limit_bytes=mib * 1024 * 1024)


def rows():
    return lax.broadcasted_iota(jnp.int32, (N, Z), 0)


def roll_y(v, s):
    return pltpu.roll(v, s % v.shape[0], 0)


def roll_z(v, s):
    return pltpu.roll(v, s % v.shape[1], 1)


def row_of(v, y):
    return v[y:y + 1, :]


def spread(row):
    return jnp.broadcast_to(row, (N, Z))


def shift_up(v):
    return jnp.where(rows() == 0, 0.0, roll_y(v, 1))


def shift_down(v):
    return jnp.where(rows() == N - 1, 0.0, roll_y(v, -1))


def shift_by(v, c):
    return shift_up(v) if c == 1 else shift_down(v) if c == -1 else v


def call(kernel, outs, name, specs, scratch=(), mib=16, flops=0, out_specs=None, moved=0):
    return pl.pallas_call(
        kernel,
        in_specs=[pl.BlockSpec(memory_space={"v": VM, "h": pltpu.HBM, "s": pltpu.SMEM}[c]) for c in specs],
        out_specs=[pl.BlockSpec(memory_space={"v": VM, "h": pltpu.HBM}[c]) for c in out_specs or "v" * len(outs)],
        out_shape=outs,
        scratch_shapes=list(scratch),
        compiler_params=params(mib),
        cost_estimate=pl.CostEstimate(flops=flops, bytes_accessed=moved, transcendentals=0),
        name=name,
    )


def faces_kernel(pot_h, conc_h, mob_h, solid_h, gx_hi, gx_lo, gy_hi, gy_lo, pull, middle, pot, conc, mob, solid, sems):
    pairs = ((pot_h, pot), (conc_h, conc), (mob_h, mob), (solid_h, solid))
    copies = [pltpu.make_async_copy(a, b, sems.at[q]) for q, (a, b) in enumerate(pairs)]
    for c in copies:
        c.start()
    copies[0].wait()
    for x in range(N):
        for r in range(RING):
            gy_hi[r, x:x + 1, :] = pot[x, N - 1 - r:N - r, :]
            gy_lo[r, x:x + 1, :] = pot[x, r:r + 1, :]
    for r in range(RING):
        gx_hi[r] = pot[N - 1 - r]
        gx_lo[r] = pot[r]
    for x in range(RING, N - RING):
        middle[x - RING] = pot[x]
    copies[1].wait()
    for s in range(2):
        for x in range(N):
            gy_hi[RING + s, x:x + 1, :] = conc[s, x, N - 1:N, :]
            gy_lo[RING + s, x:x + 1, :] = conc[s, x, 0:1, :]
        gx_hi[RING + s] = conc[s, N - 1]
        gx_lo[RING + s] = conc[s, 0]
    copies[2].wait()
    copies[3].wait()
    for x in range(N):
        is_fluid = solid[x] == 0
        v = jnp.where(is_fluid, jnp.sqrt(mob[x]), 0.0)
        pull[x] = jnp.where(is_fluid, (conc[0, x] - conc[1, x]) * (-0.001), SOLID)
        gy_hi[RING + 2, x:x + 1, :] = row_of(v, N - 1)
        gy_lo[RING + 2, x:x + 1, :] = row_of(v, 0)
        if x == 0:
            gx_lo[RING + 2] = v
        if x == N - 1:
            gx_hi[RING + 2] = v


def post_of(p, fluid, q, slopes):
    pull = jnp.where(fluid, q, 0.0)
    force = [pull * d for d in slopes]
    density = p[0]
    for i in range(1, 19):
        density = density + p[i]
    inv = 1.0 / density
    u = []
    for a in range(3):
        total = 0.9 * force[a]
        for i in range(1, 19, 2):
            if C[i][a]:
                term = p[i] - p[i + 1]
                total = total + term if C[i][a] == 1 else total - term
        u.append(total * inv)
    base = 1.0 - 1.5 * (u[0] * u[0] + u[1] * u[1] + u[2] * u[2])
    scaled = density * (10.0 / 9.0)
    out = [jnp.where(fluid, (W[0] * scaled) * base - p[0] * (1.0 / 9.0), p[0])]
    for i in range(1, 19, 2):
        along = None
        for a in range(3):
            if C[i][a]:
                term = u[a] if C[i][a] == 1 else -u[a]
                along = term if along is None else along + term
        even = base + 4.5 * along * along
        odd = 3.0 * along
        ws = W[i] * scaled
        fwd = ws * (even + odd) - p[i] * (1.0 / 9.0)
        bwd = ws * (even - odd) - p[i + 1] * (1.0 / 9.0)
        out.append(jnp.where(fluid, fwd, p[i + 1]))
        out.append(jnp.where(fluid, bwd, p[i]))
    return out, force


def sums(values, keep):
    total = [None] * 4
    for cy in (0, 1, -1):
        part = [None] * 4
        for i, v in values:
            if C[i][1] != cy:
                continue
            for m, c in enumerate((1,) + C[i]):
                if c and m != 2:
                    w = v if c == 1 else -v
                    part[m] = w if part[m] is None else part[m] + w
        for m in (0, 1, 3):
            if part[m] is None:
                continue
            w = part[m] if keep[cy] is None else jnp.where(keep[cy], part[m], 0.0)
            total[m] = w if total[m] is None else total[m] + w
            if m == 0 and cy:
                w = w if cy == 1 else -w
                total[2] = w if total[2] is None else total[2] + w
    return total


def collide_kernel(pops, gx_hi, gx_lo, middle, pull, buf, mom, px_lo, px_hi, pr_lo, pr_hi, held, sems, psems):
    chunks = [pltpu.make_async_copy(pops.at[:, pl.ds(CHUNK * s, CHUNK)], held.at[:, pl.ds(CHUNK * s, CHUNK)], sems.at[s])
              for s in range(N // CHUNK)]
    ends = [pltpu.make_async_copy(pops.at[:, 0], px_lo, psems.at[0]),
            pltpu.make_async_copy(pops.at[:, N - 1], px_hi, psems.at[1])]
    for c in chunks + ends:
        c.start()
    row = rows()
    zero = jnp.zeros((N, Z), F32)
    keep = {0: (row >= 1) & (row <= N - 2), 1: row >= 2, -1: row <= N - 3}
    for m in range(4):
        mom[m, 0] = zero
        mom[m, 1] = zero

    def pot(x):
        return gx_lo[x] if x < RING else gx_hi[N - 1 - x] if x >= N - RING else middle[x - RING]

    def step(x):
        here = pl.ds(x, 1)
        p = [held[i, x] for i in range(19)]
        for i in range(19):
            pr_lo[i, here, :] = row_of(p[i], 0)
            pr_hi[i, here, :] = row_of(p[i], N - 1)
        centre = pot(x)
        slopes = (pot(x + 1) - pot(x - 1), roll_y(centre, -1) - roll_y(centre, 1), roll_z(centre, -1) - roll_z(centre, 1))
        post, force = post_of(p, pull[x] < 0.5 * SOLID, pull[x], slopes)
        moved = []
        for i in range(19):
            v = post[i]
            if C[i][2]:
                v = roll_z(v, C[i][2])
            if C[i][1]:
                v = roll_y(v, C[i][1])
            buf[i, x + C[i][0]] = v
            moved.append(v)
        g = sums([(i, moved[i]) for i in range(19) if C[i][0] == 0], keep)
        mom[0, x] += g[0]
        for m in (1, 2, 3):
            w = jnp.where(keep[0], 0.5 * force[m - 1], 0.0)
            mom[m, x] += w if g[m] is None else g[m] + w
        g = sums([(i, moved[i]) for i in XPOS], keep)
        for m in range(4):
            mom[m, x + 1] = g[m]
        g = sums([(i, moved[i]) for i in XNEG], keep)
        for m in range(4):
            mom[m, x - 1] += g[m]

    for s in range(N // CHUNK):
        chunks[s].wait()
        for x in range(max(CHUNK * s, 1), min(CHUNK * s + CHUNK, N - 1)):
            step(x)
    for c in ends:
        c.wait()


def edge_kernel(px_lo, px_hi, pr_lo, pr_hi, gx_lo, gx_hi, gy_lo, gy_hi, fx_lo, fx_hi, fy_lo, fy_hi, mom0,
                mom, ex_lo, ex_hi, ey_lo, ey_hi, yb_lo, yb_hi):
    row = rows()
    inner = (row >= 1) & (row <= N - 2)
    keep = {0: None, 1: row >= 1, -1: row <= N - 2}
    lines = {}
    for pr, gy, fy, ey, low in ((pr_lo, gy_lo, fy_lo, ey_lo, True), (pr_hi, gy_hi, fy_hi, ey_hi, False)):
        centre = gy[0]
        y_slope = gy[1] - fy[0] if low else fy[0] - gy[1]
        slopes = (roll_y(centre, -1) - roll_y(centre, 1), y_slope, roll_z(centre, -1) - roll_z(centre, 1))
        post, force = post_of([pr[i] for i in range(19)], gy[RING + 2] > 0.0, (gy[RING] - gy[RING + 1]) * (-0.001), slopes)
        for i in range(19):
            v = roll_z(post[i], C[i][2]) if C[i][2] else post[i]
            v = jnp.where(inner, v, 0.0)
            ey[i] = v
            if low and C[i][1] == -1:
                q = YNEG.index(i)
                yb_lo[q * N:(q + 1) * N, :] = v
            if not low and C[i][1] == 1:
                q = YPOS.index(i)
                yb_hi[q * N:(q + 1) * N, :] = v
            post[i] = shift_by(v, C[i][0])
        for cy in (0, 1 if low else -1):
            y = (0 if low else N - 1) + cy
            total = [None] * 4
            for i in range(19):
                if C[i][1] == cy:
                    for m, c in enumerate((1,) + C[i]):
                        if c:
                            w = post[i] if c == 1 else -post[i]
                            total[m] = w if total[m] is None else total[m] + w
            if cy == 0:
                for a in range(3):
                    w = jnp.where(inner, 0.5 * force[a], 0.0)
                    total[a + 1] = w if total[a + 1] is None else total[a + 1] + w
            lines[y] = total
    for x in range(N):
        for m in range(4):
            v = mom0[m, x]
            for y in (0, 1, N - 2, N - 1):
                v = v + jnp.where(row == y, spread(row_of(lines[y][m], x)), 0.0)
            mom[m, x] = v
    for px, gx, fx, ex, low in ((px_lo, gx_lo, fx_lo, ex_lo, True), (px_hi, gx_hi, fx_hi, ex_hi, False)):
        at = 0 if low else N - 1
        centre = gx[0]
        x_slope = gx[1] - fx[0] if low else fx[0] - gx[1]
        y_up = jnp.where(row == N - 1, spread(fy_hi[0, at:at + 1, :]), roll_y(centre, -1))
        y_dn = jnp.where(row == 0, spread(fy_lo[0, at:at + 1, :]), roll_y(centre, 1))
        slopes = (x_slope, y_up - y_dn, roll_z(centre, -1) - roll_z(centre, 1))
        post, force = post_of([px[i] for i in range(19)], gx[RING + 2] > 0.0, (gx[RING] - gx[RING + 1]) * (-0.001), slopes)
        for i in range(19):
            v = roll_z(post[i], C[i][2]) if C[i][2] else post[i]
            if C[i][1] == 1:
                v = roll_y(v, 1)
                at_row = YPOS.index(i) * N + at
                yb_hi[at_row:at_row + 1, :] = row_of(v, 0)
                v = jnp.where(row == 0, 0.0, v)
            elif C[i][1] == -1:
                v = roll_y(v, -1)
                at_row = YNEG.index(i) * N + at
                yb_lo[at_row:at_row + 1, :] = row_of(v, N - 1)
                v = jnp.where(row == N - 1, 0.0, v)
            ex[i] = v
            post[i] = v
        none = {0: None, 1: None, -1: None}
        g = sums([(i, post[i]) for i in range(19) if C[i][0] == 0], none)
        mom[0, at] += g[0]
        for m in (1, 2, 3):
            w = 0.5 * force[m - 1]
            mom[m, at] += w if g[m] is None else g[m] + w
        g = sums([(i, post[i]) for i in (XPOS if low else XNEG)], none)
        for m in range(4):
            mom[m, 1 if low else N - 2] += g[m]
        g = sums([(i, post[i]) for i in (XNEG if low else XPOS)], none)
        k = LINE + (2 if low else 0)
        yb_hi[k:k + 1, :] = row_of(g[0], N - 1)
        yb_hi[k + 1:k + 2, :] = row_of(g[2], N - 1)
        yb_lo[k:k + 1, :] = row_of(g[0], 0)
        yb_lo[k + 1:k + 2, :] = row_of(g[2], 0)
    for x in range(N):
        for q, m in ((5, 0), (6, 2)):
            yb_lo[q * N + x:q * N + x + 1, :] = mom[m, x, 0:1, :]
            yb_hi[q * N + x:q * N + x + 1, :] = mom[m, x, N - 1:N, :]
    yb_lo[LINE + 4:, :] = jnp.zeros((4, Z), F32)
    yb_hi[LINE + 4:, :] = jnp.zeros((4, Z), F32)


def plane(ref, q):
    return ref[q * N:(q + 1) * N, :]


def line(ref, q, x):
    return ref[q * N + x:q * N + x + 1, :]


def y_terms(lo, hi):
    s3, s7, s10, s15, s17 = (plane(lo, q) for q in range(5))
    s7, s10 = shift_up(s7), shift_down(s10)
    total = s3 + s7 + s10 + s15 + s17
    below = (total, s7 - s10, total, s15 - s17)
    s4, s8, s9, s16, s18 = (plane(hi, q) for q in range(5))
    s8, s9 = shift_down(s8), shift_up(s9)
    total = s4 + s8 + s9 + s16 + s18
    return below, (total, s9 - s8, -total, s18 - s16)


def corner_kernel(ex_lo, ex_hi, yh_lo, yh_hi, yb_lo, yb_hi, mom, xb_lo, xb_hi):
    row = rows()
    below, above = y_terms(yh_lo, yh_hi)
    for ex, xb, slots, at in ((ex_hi, xb_hi, XPOS, N - 1), (ex_lo, xb_lo, XNEG, 0)):
        for q, i in enumerate(slots):
            v = ex[i]
            if C[i][1] == 1:
                v = jnp.where(row == 0, spread(line(yh_lo, YPOS.index(i), at)), v)
            elif C[i][1] == -1:
                v = jnp.where(row == N - 1, spread(line(yh_hi, YNEG.index(i), at)), v)
            xb[q * N:(q + 1) * N, :] = v
        for q, m in ((5, 0), (6, 1)):
            v = mom[m, at] + jnp.where(row == 0, spread(row_of(below[m], at)), 0.0)
            xb[q * N:(q + 1) * N, :] = v + jnp.where(row == N - 1, spread(row_of(above[m], at)), 0.0)
        c = 1 if at else -1
        k = LINE if at else LINE + 2
        down = line(yb_lo, YNEG.index(9 if c == 1 else 8), at)
        up = line(yb_hi, YPOS.index(7 if c == 1 else 10), at)
        xb[LINE:LINE + 1, :] = yh_lo[k:k + 1, :] + down
        xb[LINE + 1:LINE + 2, :] = yh_lo[k + 1:k + 2, :] - down
        xb[LINE + 2:LINE + 3, :] = yh_hi[k:k + 1, :] + up
        xb[LINE + 3:LINE + 4, :] = yh_hi[k + 1:k + 2, :] + up
        xb[LINE + 4:, :] = jnp.zeros((4, Z), F32)


def velocity(conductance, density, momentum):
    return jnp.where(conductance > 0.0, momentum / density, 0.0)


def full_moment(mom, m, x, below, above):
    v = mom[m, x] + jnp.where(rows() == 0, spread(row_of(below[m], x)), 0.0)
    return v + jnp.where(rows() == N - 1, spread(row_of(above[m], x)), 0.0)


def inner_kernel(charge, classes_h, mob, solid, conc, pot, fx_lo, fx_hi, fy_lo, fy_hi, gy_lo, mom, yh_lo, yh_hi, yb_lo, yb_hi,
                 base, wx, wy, wy_low, wz, wall, cond, drift, src, sy_lo, sy_hi, low, adv, classes, sem):
    fetch = pltpu.make_async_copy(classes_h, classes, sem)
    fetch.start()
    row = rows()

    def faces(ref):
        return tuple(ref[RING + q] for q in range(3)) + (ref[0],)

    rest, weight = flux(faces(fy_lo), faces(gy_lo))
    for s in range(2):
        low[s] = rest[s]
        wy_low[s] = weight[s]
    upper = faces(fy_hi)
    for x in range(N):
        cond[x] = jnp.where(solid[x] == 0, jnp.sqrt(mob[x]), 0.0)
    below, above = y_terms(yh_lo, yh_hi)
    for x in range(1, N - 1):
        scale = jnp.where(cond[x] > 0.0, 1.0 / full_moment(mom, 0, x, below, above), 0.0)
        for a in range(3):
            drift[a, x] = full_moment(mom, a + 1, x, below, above) * scale
    from_hi, from_lo = y_terms(yb_hi, yb_lo)
    dy_lo = velocity(fy_lo[RING + 2], plane(yh_lo, 5) + from_lo[0], plane(yh_lo, 6) + from_lo[2])
    dy_hi = velocity(fy_hi[RING + 2], plane(yh_hi, 5) + from_hi[0], plane(yh_hi, 6) + from_hi[2])
    for x in range(1, N - 1):
        carried = row_of(dy_lo, x) + drift[1, x, 0:1, :]
        for s in range(2):
            adv[s, x:x + 1, :] = wy_low[s, x:x + 1, :] * carried

    def fields(x):
        return (conc[0, x], conc[1, x], cond[x], pot[x])

    behind, weight = flux(faces(fx_lo), fields(0))
    for s in range(2):
        wx[s, 0] = weight[s]
    fetch.wait()
    for x in range(N):
        known = 1 <= x <= N - 2
        me = fields(x)
        ahead, weight = flux(me, fields(x + 1) if x < N - 1 else faces(fx_hi))
        if 1 <= x <= N - 3:
            carried = drift[0, x] + drift[0, x + 1]
            ahead = [ahead[s] + weight[s] * carried for s in range(2)]
        elif x in (0, N - 2):
            for s in range(2):
                wx[s, 1 if x == 0 else 2] = weight[s]
        else:
            for s in range(2):
                wx[s, 3] = weight[s]
        tot = [ahead[s] - behind[s] for s in range(2)]
        behind = ahead
        nxt = tuple(jnp.where(row == N - 1, spread(row_of(upper[q], x)), roll_y(me[q], -1)) for q in range(4))
        rest, weight = flux(me, nxt)
        first = [low[s, x:x + 1, :] for s in range(2)]
        if known:
            v = drift[1, x]
            carried = v + jnp.where(row == N - 1, spread(row_of(dy_hi, x)), roll_y(v, -1))
            rest = [rest[s] + weight[s] * carried for s in range(2)]
            first = [first[s] + adv[s, x:x + 1, :] for s in range(2)]
        else:
            for s in range(2):
                wy[s, x // (N - 1)] = weight[s]
        for s in range(2):
            tot[s] = tot[s] + (rest[s] - jnp.where(row == 0, spread(first[s]), roll_y(rest[s], 1)))
        rest, weight = flux(me, tuple(roll_z(v, -1) for v in me))
        if known:
            v = drift[2, x]
            carried = v + roll_z(v, -1)
            rest = [rest[s] + weight[s] * carried for s in range(2)]
        else:
            for s in range(2):
                wz[s, x // (N - 1)] = weight[s]
        for s in range(2):
            tot[s] = tot[s] + (rest[s] - roll_z(rest[s], 1))
            base[s, x] = me[s] - tot[s]
        cls = classes[x]
        total = jnp.zeros((N, Z), F32)
        for q in range(4):
            total = total + jnp.where(cls == q, charge[q], 0.0)
        if 2 <= x <= N - 3:
            source_plane(x, jnp.where(cond[x] > 0.0, me[0] - tot[0] - (me[1] - tot[1]), total), src, sy_lo, sy_hi)
        else:
            wall[x] = total


def source_plane(x, v, src, sy_lo, sy_hi):
    src[x] = v
    for r in range(RING - 1):
        sy_lo[r, x:x + 1, :] = row_of(v, r)
        sy_hi[r, x:x + 1, :] = row_of(v, N - 1 - r)


def transport_kernel(mom, cond, base, wx, wy, wy_low, wz, wall, drift, src0, sy_lo0, sy_hi0,
                     yh_lo, yh_hi, xh_lo, xh_hi, yb_lo, yb_hi, xb_lo, xb_hi,
                     fx_lo, fx_hi, fy_lo, fy_hi, conc_out, src, sy_lo, sy_hi):
    row = rows()
    below, above = y_terms(yh_lo, yh_hi)
    sy_lo[...] = sy_lo0[...]
    sy_hi[...] = sy_hi0[...]
    for x in range(2, N - 2):
        src[x] = src0[x]
        for s in range(2):
            conc_out[s, x] = base[s, x]
    from_hi, from_lo = y_terms(yb_hi, yb_lo)

    def y_line(fy, yh, terms, k, xh, x):
        density = line(yh, 5, x) + row_of(terms[0], x) + xh[k:k + 1, :]
        momentum = line(yh, 6, x) + row_of(terms[2], x) + xh[k + 1:k + 2, :]
        return velocity(fy[RING + 2, x:x + 1, :], density, momentum)

    for x, near, xh, xb, fx, sign in ((0, 1, xh_lo, xb_lo, fx_lo, 1.0), (N - 1, N - 2, xh_hi, xb_hi, fx_hi, -1.0)):
        a = [plane(xh, q) for q in range(5)]
        total = a[0] + a[1] + a[2] + a[3] + a[4]
        extra = (total, sign * total, sign * (a[1] - a[2]), sign * (a[3] - a[4]))
        full = [full_moment(mom, m, x, below, above) + extra[m] for m in range(4)]
        scale = jnp.where(cond[x] > 0.0, 1.0 / full[0], 0.0)
        d = [full[m] * scale for m in (1, 2, 3)]
        out = plane(xb, 0) + plane(xb, 1) + plane(xb, 2) + plane(xb, 3) + plane(xb, 4)
        beyond = velocity(fx[RING + 2], plane(xh, 5) + out, plane(xh, 6) - sign * out)
        e = x // (N - 1)
        outer = 3 * e
        dy_lo = y_line(fy_lo, yh_lo, from_lo, LINE, xh, x)
        dy_hi = y_line(fy_hi, yh_hi, from_hi, LINE + 2, xh, x)
        c, c_near = [], []
        up = d[1] + jnp.where(row == N - 1, spread(dy_hi), roll_y(d[1], -1))
        turn = d[2] + roll_z(d[2], -1)
        for s in range(2):
            far = wx[s, outer] * (beyond + d[0])
            close = wx[s, 1 + e] * (d[0] + drift[0, near])
            f = wy[s, e] * up
            first = wy_low[s, x:x + 1, :] * (dy_lo + row_of(d[1], 0))
            g = wz[s, e] * turn
            tot = sign * (close - far) + (f - jnp.where(row == 0, spread(first), roll_y(f, 1))) + (g - roll_z(g, 1))
            c.append(base[s, x] - tot)
            c_near.append(base[s, near] + sign * close)
            conc_out[s, x] = c[s]
            conc_out[s, near] = c_near[s]
        source_plane(x, jnp.where(cond[x] > 0.0, c[0] - c[1], wall[x]), src, sy_lo, sy_hi)
        source_plane(near, jnp.where(cond[near] > 0.0, c_near[0] - c_near[1], wall[near]), src, sy_lo, sy_hi)


def split(ext, a, b, pairs, shift):
    shape = (N + 2 * OFF, Z)
    mask = (lax.broadcasted_iota(jnp.int32, shape, 0) + lax.broadcasted_iota(jnp.int32, shape, 1)) % 2 == 0
    for k in pairs:
        p, q = ext[2 * k], ext[2 * k + 1]
        a[k + shift] = jnp.where(mask, p, q)
        b[k + shift] = jnp.where(mask, q, p)


def prepare_kernel(pot, src, fy_lo, fy_hi, ys_lo, ys_hi, even, odd, s_even, s_odd, ext):
    for centre, y_lo, y_hi, depth, a, b in ((pot, fy_lo, fy_hi, RING, even, odd), (src, ys_lo, ys_hi, RING - 1, s_even, s_odd)):
        for x in range(N):
            ext[x, OFF:OFF + N] = centre[x]
            for r in range(depth):
                ext[x, OFF - 1 - r:OFF - r, :] = y_lo[r, x:x + 1, :]
                ext[x, OFF + N + r:OFF + N + r + 1, :] = y_hi[r, x:x + 1, :]
        split(ext, a, b, range(N // 2), 0)


def sweep_kernel(even_in, odd_in, s_even_in, s_odd_in, fx_lo, fx_hi, xs_lo, xs_hi, out, ext, even, odd, s_even, s_odd, done, sems):
    mid = slice(OFF, OFF + N)
    top = RING + N
    half = (N + 2 * RING) // 2
    shape = (N + 2 * OFF, Z)
    mask = (lax.broadcasted_iota(jnp.int32, shape, 0) + lax.broadcasted_iota(jnp.int32, shape, 1)) % 2 == 0
    zero = jnp.zeros(shape, F32)
    for ref in (even, odd):
        ref[0] = zero
        ref[half + 1] = zero
    for ref, given in ((even, even_in), (odd, odd_in), (s_even, s_even_in), (s_odd, s_odd_in)):
        for k in range(N // 2):
            ref[k + 1 + RING // 2] = given[k]
    ends = list(range(RING // 2)) + list(range(RING // 2 + N // 2, half))
    def far(ref):
        v = ref[FAR:FAR + N // 2, :]
        return jnp.concatenate([v, roll_z(v, -1)], axis=0)

    for x_lo, x_hi, depth, single, shared, a, b in (
            (lambda r: fx_lo[r], lambda r: fx_hi[r], RING, POT_ROWS, POT_SHARED, even, odd),
            (lambda r: plane(xs_lo, r) if r < RING - 2 else far(xs_lo), lambda r: plane(xs_hi, r) if r < RING - 2 else far(xs_hi),
             RING - 1, SRC_ROWS, SRC_SHARED, s_even, s_odd)):
        for r in range(depth):
            ext[RING - 1 - r, mid] = x_lo(r)
            ext[top + r, mid] = x_hi(r)
        for at, a_ring, side, b_ring in single + [(at, p, side, q) for at, p, q in shared for side in (0, 1)]:
            y = OFF + N + b_ring - 1 if side else OFF - b_ring
            ext[RING - a_ring, y:y + 1, :] = xs_lo[at:at + 1, :]
            ext[top + a_ring - 1, y:y + 1, :] = xs_hi[at:at + 1, :]
        split(ext, a, b, ends, 1)

    copies = []
    for h in range(6):
        this, other, s = (even, odd, s_even) if h % 2 == 0 else (odd, even, s_odd)

        def update(k, carry, h=h, this=this, other=other, s=s):
            c = other[k]
            before, after = other[k - 1], other[k + 1]
            far = jnp.where(mask, before, after) if h % 2 == 0 else jnp.where(mask, after, before)
            nb = (c + far) + (roll_y(c, 1) + roll_y(c, -1)) + (roll_z(c, 1) + roll_z(c, -1))
            this[k] = -0.6 * this[k] + (1.6 / 6.0) * (nb + s[k])
            return carry

        lo = (h + 1) // 2
        for k in range(lo + 1, half - lo + 1):
            update(k, 0)
            if h == 5:
                p, q = even[k], odd[k]
                x = 2 * (k - 1) - RING
                done[x] = jnp.where(mask, p, q)[OFF:OFF + N]
                done[x + 1] = jnp.where(mask, q, p)[OFF:OFF + N]
                copies.append(pltpu.make_async_copy(done.at[x:x + 2], out.at[x:x + 2], sems.at[x // 2]))
                copies[-1].start()
    for c in copies:
        c.wait()


def patch_kernel(buf, ex_lo, ex_hi, ey_lo, ey_hi, yh_lo, yh_hi, xh_lo, xh_hi, conc, out, conc_out, done, sems):
    row = rows()
    copies = [pltpu.make_async_copy(conc, conc_out, sems.at[19])]
    copies[0].start()
    for i in range(19):
        cx, cy, _ = C[i]

        def halo(v, src, i=i, cy=cy):
            if cy == 1:
                return jnp.where(row == 0, spread(yh_lo[pl.ds(YPOS.index(i) * N + src, 1), :]), v)
            if cy == -1:
                return jnp.where(row == N - 1, spread(yh_hi[pl.ds(YNEG.index(i) * N + src, 1), :]), v)
            return v

        def inner(src, carry, i=i, cx=cx, cy=cy, halo=halo):
            here = pl.ds(src, 1)
            v = buf[i, src + cx]
            if cy != -1:
                v = jnp.where(row == cy, spread(ey_lo[i, here, :]), v)
            if cy != 1:
                v = jnp.where(row == N - 1 + cy, spread(ey_hi[i, here, :]), v)
            done[i, src + cx] = halo(v, src)
            return carry

        lax.fori_loop(1, N - 1, inner, 0, unroll=True)
        if cx != -1:
            done[i, cx] = halo(ex_lo[i], 0)
        if cx != 1:
            done[i, N - 1 + cx] = halo(ex_hi[i], N - 1)
        if cx == 1:
            done[i, 0] = plane(xh_lo, XPOS.index(i))
        if cx == -1:
            done[i, N - 1] = plane(xh_hi, XNEG.index(i))
        copy = pltpu.make_async_copy(done.at[i], out.at[i], sems.at[i])
        copy.start()
        copies.append(copy)
    for copy in copies:
        copy.wait()


def flux(a, b):
    link = a[2] * b[2]
    drop = a[3] - b[3]
    rest, weight = [], []
    for s in range(2):
        both = a[s] + b[s]
        rest.append(link * (RATES[s] * ((a[s] - b[s]) + ((0.5 * VAL[s]) * both) * drop)))
        weight.append((0.25 * link) * both)
    return rest, weight


def ring_rows(at, total):
    single, shared = [], []
    for a in range(1, total):
        for b in range(1, total - a):
            for side in (0, 1):
                single.append((at, a, side, b))
                at += 1
    for a in range(1, total):
        shared.append((at, a, total - a))
        at += 1
    return single, shared, at


FAR = (RING - 2) * N
SRC_ROWS, SRC_SHARED, POT_START = ring_rows(FAR + N // 2, RING - 1)
POT_ROWS, POT_SHARED, SRC_END = ring_rows(POT_START, RING)
SRC_LEN = -(-SRC_END // 8) * 8


def pack_src_kernel(src, ys_lo, ys_hi, fy_lo, fy_hi, o_hi, o_lo):
    lane = lax.broadcasted_iota(jnp.int32, (1, Z), 1) % 2
    half = (N // 2, Z)
    shade = (lax.broadcasted_iota(jnp.int32, half, 0) + lax.broadcasted_iota(jnp.int32, half, 1)) % 2
    for o, high in ((o_hi, True), (o_lo, False)):
        def at_x(a, high=high):
            return N - a if high else a - 1

        for k in range(RING - 2):
            o[k * N:(k + 1) * N, :] = src[at_x(k + 1)]
        x = at_x(RING - 1)
        v = src[x]
        o[FAR:FAR + N // 2, :] = jnp.where(shade == x % 2, v[:N // 2], roll_z(v[N // 2:], 1))
        for single, shared, lo, hi, odd in ((SRC_ROWS, SRC_SHARED, ys_lo, ys_hi, 0), (POT_ROWS, POT_SHARED, fy_lo, fy_hi, 1)):
            for at, a, side, b in single:
                halo = hi if side else lo
                o[at:at + 1, :] = halo[b - 1, at_x(a):at_x(a) + 1, :]
            for at, a, b in shared:
                x = at_x(a)
                o[at:at + 1, :] = jnp.where(lane == (x + b + odd) % 2, lo[b - 1, x:x + 1, :], hi[b - 1, x:x + 1, :])
        o[SRC_END:, :] = jnp.zeros((SRC_LEN - SRC_END, Z), F32)


def swap(axis, hi, lo):
    n = lax.axis_size(axis)
    even = lax.axis_index(axis) % 2 == 0
    first = lax.ppermute(jnp.where(even, hi, lo), axis, [(i, i + 1 - 2 * (i % 2)) for i in range(n)])
    second = lax.ppermute(jnp.where(even, lo, hi), axis, [(i, (i - 1 + 2 * (i % 2)) % n) for i in range(n)])
    return jnp.where(even, second, first), jnp.where(even, first, second)


def body(pops, conc, pot, mob, solid, classes, charge):
    cube = sds(N, N, Z)
    msg = sds(ROWS, Z)
    gx_hi, gx_lo, gy_hi, gy_lo, pull, middle = call(
        faces_kernel, [sds(RING + 3, N, Z)] * 4 + [cube, sds(N - 2 * RING, N, Z)], "faces", "hhhh",
        scratch=[VM((N, N, Z), F32), VM((2, N, N, Z), F32), VM((N, N, Z), F32),
                 VM((N, N, Z), jnp.int32),
                 pltpu.SemaphoreType.DMA((4,))], mib=53, moved=2600000)(
        pot, conc, mob, solid)
    fx_lo, fx_hi = swap("gx", gx_hi, gx_lo)
    fy_lo, fy_hi = swap("gy", gy_hi, gy_lo)
    chunks = N // CHUNK
    buf, mom, px_lo, px_hi, pr_lo, pr_hi = call(
        collide_kernel, [sds(19, N, N, Z), sds(4, N, N, Z)] + [sds(19, N, Z)] * 4, "collide", "hvvvv",
        scratch=[VM((19, N, N, Z), F32), pltpu.SemaphoreType.DMA((chunks,)), pltpu.SemaphoreType.DMA((2,))],
        mib=43, flops=20000000, moved=14000000)(pops, gx_hi, gx_lo, middle, pull)
    mom, ex_lo, ex_hi, ey_lo, ey_hi, yb_lo, yb_hi = call(
        edge_kernel, [sds(4, N, N, Z)] + [sds(19, N, Z)] * 4 + [msg, msg], "edge", "v" * 13, moved=3000000)(
        px_lo, px_hi, pr_lo, pr_hi, gx_lo, gx_hi, gy_lo, gy_hi, fx_lo, fx_hi, fy_lo, fy_hi, mom)
    yh_lo, yh_hi = swap("gy", yb_hi, yb_lo)
    xb_lo, xb_hi = call(corner_kernel, [msg, msg], "corner", "v" * 7)(ex_lo, ex_hi, yh_lo, yh_hi, yb_lo, yb_hi, mom)
    xh_lo, xh_hi = swap("gx", xb_hi, xb_lo)
    fy_late, _ = lax.optimization_barrier((fy_lo, yh_lo))
    pair = sds(2, N, N, Z)
    ring = sds(RING - 1, N, Z)
    base, wx, wy, wy_low, wz, wall, cond, drift, src, sy_lo, sy_hi = call(
        inner_kernel, [pair, sds(2, 4, N, Z), sds(2, 2, N, Z), sds(2, N, Z), sds(2, 2, N, Z), cube, cube, sds(3, N, N, Z), cube, ring, ring],
        "inner", "sh" + "v" * 14,
        scratch=[VM((2, N, Z), F32), VM((2, N, Z), F32), VM((N, N, Z), jnp.int32), pltpu.SemaphoreType.DMA],
        flops=10000000, moved=6000000)(
        charge, classes, mob, solid, conc, pot, fx_lo, fx_hi, fy_late, fy_hi, gy_lo, mom, yh_lo, yh_hi, yb_lo, yb_hi)
    conc_new, src, sy_lo, sy_hi = call(
        transport_kernel, [pair, cube, ring, ring], "transport", "v" * 24, flops=3000000, moved=4000000)(
        mom, cond, base, wx, wy, wy_low, wz, wall, drift, src, sy_lo, sy_hi,
        yh_lo, yh_hi, xh_lo, xh_hi, yb_lo, yb_hi, xb_lo, xb_hi, fx_lo, fx_hi, fy_lo, fy_hi)
    ys_lo, ys_hi = swap("gy", sy_hi, sy_lo)
    bs_hi, bs_lo = call(pack_src_kernel, [sds(SRC_LEN, Z)] * 2, "pack_src", "v" * 5)(src, ys_lo, ys_hi, fy_lo, fy_hi)
    xs_lo, xs_hi = swap("gx", bs_hi, bs_lo)
    packed = VM(((N + 2 * RING) // 2 + 2, N + 2 * OFF, Z), F32)
    prepared = call(
        prepare_kernel, [sds(N // 2, N + 2 * OFF, Z)] * 4, "prepare", "v" * 6,
        scratch=[VM((N, N + 2 * OFF, Z), F32)], flops=1000000, moved=4000000)(pot, src, fy_lo, fy_hi, ys_lo, ys_hi)
    potential_out = call(
        sweep_kernel, [cube], "sweep", "v" * 8,
        scratch=[VM((N + 2 * RING, N + 2 * OFF, Z), F32)] + [packed] * 4 + [VM((N, N, Z), F32), pltpu.SemaphoreType.DMA((N // 2,))], out_specs="h", flops=20000000, moved=4000000)(
        *prepared, fx_lo, fx_hi, xs_lo, xs_hi)[0]
    pop, conc_out = call(
        patch_kernel, [sds(19, N, N, Z), pair], "patch", "v" * 10, out_specs="hh",
        scratch=[VM((19, N, N, Z), F32), pltpu.SemaphoreType.DMA((20,))], mib=16, moved=10000000)(
        buf, ex_lo, ex_hi, ey_lo, ey_hi, yh_lo, yh_hi, xh_lo, xh_hi, conc_new)
    return (pop, conc_out, potential_out)


def solution(mesh):
    lattice = P(None, "gx", "gy", None)
    flat = P("gx", "gy", None)
    return jax.shard_map(
        body, mesh=mesh, in_specs=(lattice, lattice, flat, flat, flat, flat, P()),
        out_specs=(lattice, lattice, flat), check_vma=False)
```
